32 devices in a mesh: frames: 8 (over z, y), heads: 4 (over x, core).
Axes of the slice: x: 2, y: 2, z: 4, core: 2. Of those that a mesh axis runs over, the one named last changes fastest.
Arguments:
- bank_query: bfloat16 [64, 64, 5120], P(None, 'frames', 'heads'), may hold values from -2048 to 2048
- char_bank: bfloat16 [2, 8, 768, 5120], P(None, None, 'frames', 'heads'), may hold values from -8 to 8
- char_slots: int32 [8, 2], replicated, may hold values from 0 to 7, as said below
- slot_live: int32 [8, 2], replicated, may hold values from 0 to 1, as said below
- frame_tokens: bfloat16 [3, 64, 64, 5120], P(None, None, 'frames', 'heads'), may hold values from -2048 to 2048
- out_weight: bfloat16 [5120, 5120], P('heads'), may hold values from -0.078125 to 0.078125
Outputs:
- blended: bfloat16 [64, 64, 5120], P('heads', 'frames')
The draws below stay inside these ranges and needn't reach their ends.
Inputs may be any that keep to these rules, and one draw needn't show every extreme that they name: `char_slots`: the two ids of a shard differ. `slot_live`: slot 0 of every shard is 1.
All inputs are finite; a program needn't handle non-finite values.
Results may differ from the reference program's by a relative error of at most 0.014.
Values may be sent and summed in bfloat16 or wider, within the bound.
No kernel may reach another device: no remote copies, remote signals or barrier semaphores. Data moves between devices by JAX's collectives and lax.ppermute only.
A program may use at most 128 MiB of HBM per device.

```python
import jax
import jax.numpy as jnp
from jax import lax

D = 5120
HEADS = 40
HEAD_DIM = 128
CHARACTERS = 8
REF_TOKENS = 768
FRAMES_DEV = 8
SPATIAL = 64
FRAMES = 64
SHARDS = 8
GROUP_WIDTH = 1280
N_HEADS = 4


def pick_chars(key):
    base_key = jax.random.fold_in(key, 101)
    key_first, key_offset = jax.random.split(base_key)
    first_char = jax.random.randint(key_first, (SHARDS,), 0, CHARACTERS)
    offset = jax.random.randint(key_offset, (SHARDS,), 1, CHARACTERS)
    second = (first_char + offset) % CHARACTERS
    return jnp.stack([first_char, second], axis=1).astype(jnp.int32)


def make_bank(key):
    base_key = jax.random.fold_in(key, 103)
    key_keys, key_values = jax.random.split(base_key)
    key_rows = jnp.clip(jax.random.normal(key_keys, (CHARACTERS, REF_TOKENS, D), jnp.float32), -5.0, 5.0) * 1.6
    value_rows = jnp.clip(jax.random.normal(key_values, (CHARACTERS, REF_TOKENS, D), jnp.float32), -5.0, 5.0)
    return jnp.stack([key_rows, value_rows])


def draw_char_slots(key, part):
    return pick_chars(key)


def draw_slot_live(key, part):
    second = jax.random.randint(jax.random.fold_in(key, 102), (SHARDS,), 0, 2)
    return jnp.stack([jnp.ones_like(second), second], axis=1).astype(jnp.int32)


def draw_char_bank(key, part):
    return make_bank(key).astype(jnp.bfloat16)


def draw_bank_query(key, part):
    queries = jnp.clip(jax.random.normal(jax.random.fold_in(key, 104), (SPATIAL, FRAMES, D), jnp.float32), -5.0, 5.0) * 1.6
    return queries.astype(jnp.bfloat16)


def draw_frame_tokens(key, part):
    raw = jnp.clip(jax.random.normal(jax.random.fold_in(key, 105), (3, SPATIAL, FRAMES, D), jnp.float32), -5.0, 5.0)
    raw = raw * jnp.array([1.4, 1.4, 1.0], jnp.float32)[:, None, None, None]
    return raw.astype(jnp.bfloat16)


def block_scale(stream_key, shape, cuts, smallest, high):
    def one(position, parts):
        draws = jax.random.uniform(jax.random.fold_in(jax.random.fold_in(stream_key, 6), position), (parts,), jnp.float32, smallest / len(cuts), high / len(cuts))
        return jnp.repeat(jnp.exp(draws), shape[position] // parts).reshape((-1,) + (1,) * (len(shape) - position - 1))

    loudness = one(*cuts[0])
    for cut in cuts[1:]:
        loudness = loudness * one(*cut)
    return loudness


def bell_draw(key, dims, deviation, bound, cuts=(), held_as=jnp.bfloat16):
    values = deviation * jax.random.normal(key, dims, jnp.float32)
    if cuts:
        values = values * block_scale(key, dims, cuts, -0.22, 0.18)
    return jnp.clip(values, -bound, bound).astype(held_as)


def setup_inputs(seed: int = 0) -> dict:
    key_of = jax.random.split(jax.random.key(seed), 7)
    return {
        "bank_query": draw_bank_query(jax.random.fold_in(key_of[6], 71), 0),
        "char_bank": draw_char_bank(jax.random.fold_in(key_of[6], 71), 0),
        "char_slots": draw_char_slots(jax.random.fold_in(key_of[6], 71), 0),
        "slot_live": draw_slot_live(jax.random.fold_in(key_of[6], 71), 0),
        "frame_tokens": draw_frame_tokens(jax.random.fold_in(key_of[6], 71), 0),
        "out_weight": bell_draw(key_of[5], (D, D), D ** -0.5, 0.078125, ((0, 4),)),
    }


def bank_attend(operands, char_bank):
    queries, listed, opened = operands
    key_rows = char_bank[0][listed].reshape(2 * REF_TOKENS, HEADS, HEAD_DIM)
    value_rows = char_bank[1][listed].reshape(2 * REF_TOKENS, HEADS, HEAD_DIM)
    live_rows = jnp.repeat(opened > 0, REF_TOKENS)
    scores = jnp.einsum("sfhd,khd->sfhk", queries.astype(jnp.float32), key_rows.astype(jnp.float32)) * (HEAD_DIM ** -0.5)
    masked = jnp.where(live_rows, scores, -jnp.inf)
    peak = jnp.max(masked, axis=-1, keepdims=True)
    weights = jnp.exp(masked - peak)
    totals = jnp.sum(weights, axis=-1, keepdims=True)
    rounded = lax.optimization_barrier(weights.astype(jnp.bfloat16)).astype(jnp.float32)
    attended = jnp.einsum("sfhk,khd->sfhd", rounded, value_rows.astype(jnp.float32))
    return attended / totals


def frame_attend(tokens):
    queries = tokens[0].astype(jnp.float32)
    key_rows = tokens[1].astype(jnp.float32)
    value_rows = tokens[2].astype(jnp.float32)
    scores = jnp.einsum("fhd,ghd->fhg", queries, key_rows) * (HEAD_DIM ** -0.5)
    peak = jnp.max(scores, axis=-1, keepdims=True)
    weights = jnp.exp(scores - peak)
    totals = jnp.sum(weights, axis=-1, keepdims=True)
    rounded = lax.optimization_barrier(weights.astype(jnp.bfloat16)).astype(jnp.float32)
    attended = jnp.einsum("fhg,ghd->fhd", rounded, value_rows) / totals
    return attended.astype(jnp.bfloat16)


def reference(bank_query, char_bank, char_slots, slot_live, frame_tokens, out_weight):
    grouped = bank_query.reshape(SPATIAL, SHARDS, FRAMES_DEV, HEADS, HEAD_DIM)
    grouped = jnp.moveaxis(grouped, 1, 0)
    ref_out = lax.map(lambda operands: bank_attend(operands, char_bank), (grouped, char_slots, slot_live))
    ref_out = jnp.moveaxis(ref_out, 0, 1).reshape(SPATIAL, FRAMES, D)
    tokens = jnp.moveaxis(frame_tokens.reshape(3, SPATIAL, FRAMES, HEADS, HEAD_DIM), 1, 0)
    frame_out = lax.map(frame_attend, tokens).reshape(SPATIAL, FRAMES, D)
    combined = (ref_out + frame_out.astype(jnp.float32)).astype(jnp.bfloat16).reshape(SPATIAL * FRAMES, D)
    summed = jnp.zeros((SPATIAL * FRAMES, D), jnp.float32)
    for group in range(N_HEADS):
        low = group * GROUP_WIDTH
        partial_sum = jnp.dot(combined[:, low:low + GROUP_WIDTH], out_weight[low:low + GROUP_WIDTH], preferred_element_type=jnp.float32)
        summed = summed + lax.optimization_barrier(partial_sum.astype(jnp.bfloat16)).astype(jnp.float32)
    return summed.astype(jnp.bfloat16).reshape(SPATIAL, FRAMES, D)
```

```python
import functools

import jax
import jax.numpy as jnp
from jax import lax
from jax.experimental import pallas as pl
from jax.experimental.pallas import tpu as pltpu
from jax.sharding import PartitionSpec as P

HEAD_DIM = 128
PARTS = 4


def softmax_over_rows(score_blocks):
    scale = HEAD_DIM ** (-0.5)
    peak = functools.reduce(
        jnp.maximum, [jnp.max(block, axis=0, keepdims=True) for block in score_blocks]
    )
    weights = [jnp.exp((block - peak) * scale) for block in score_blocks]
    totals = functools.reduce(
        jnp.add, [jnp.sum(block, axis=0, keepdims=True) for block in weights]
    )
    return weights, totals, peak * scale + jnp.log(totals)


def weighted(value_blocks, weights, totals):
    gathered = functools.reduce(
        jnp.add,
        [
            lax.dot_general(
                rows, block.astype(jnp.bfloat16), (((0,), (0,)), ((), ())),
                preferred_element_type=jnp.float32,
            )
            for rows, block in zip(value_blocks, weights)
        ],
    )
    return gathered * (1.0 / totals)


def attend_kernel(frames_here, slots_ref, live_ref, query_ref, bank_ref, frame_ref, ref_out, frame_out, stats_ref):
    head = pl.program_id(0)
    shards = query_ref.shape[0]
    rows = query_ref.shape[2]
    frame_keys = frame_ref.shape[1]
    key_spot = lax.broadcasted_iota(jnp.int32, (frame_keys, rows), 0) % rows // frames_here
    query_spot = lax.broadcasted_iota(jnp.int32, (frame_keys, rows), 1) // frames_here
    same_spot = key_spot == query_spot
    for shard in range(shards):
        queries = query_ref[shard, 0]
        blocks = []
        for slot in range(2):
            keys = bank_ref[0, slots_ref[shard, slot]]
            scores = lax.dot_general(
                keys, queries, (((1,), (1,)), ((), ())), preferred_element_type=jnp.float32
            )
            blocks.append(jnp.where(live_ref[shard, slot] > 0, scores, -jnp.inf))
        weights, totals, level = softmax_over_rows(blocks)
        values = [bank_ref[1, slots_ref[shard, slot]] for slot in range(2)]
        ref_out[shard] = weighted(values, weights, totals).astype(ref_out.dtype)
        stats_ref[shard, 0, pl.ds(head, 1), :] = level
        scores = lax.dot_general(
            frame_ref[0], query_ref[shard, 1], (((1,), (1,)), ((), ())),
            preferred_element_type=jnp.float32,
        )
        weights, totals, level = softmax_over_rows([jnp.where(same_spot, scores, -jnp.inf)])
        frame_out[shard] = weighted([frame_ref[1]], weights, totals).astype(frame_out.dtype)
        stats_ref[shard, 1, pl.ds(head, 1), :] = level


def attend(frames_here, slots, live, queries, bank, frame_kv):
    shards, _, rows, width = queries.shape
    heads = width // HEAD_DIM
    _, characters, tokens, _ = bank.shape
    frame_keys = frame_kv.shape[1]
    flops = 4 * shards * rows * width * (2 * tokens + frame_keys)
    return pl.pallas_call(
        functools.partial(attend_kernel, frames_here),
        grid=(heads,),
        in_specs=[
            pl.BlockSpec(memory_space=pltpu.SMEM),
            pl.BlockSpec(memory_space=pltpu.SMEM),
            pl.BlockSpec((shards, 2, rows, HEAD_DIM), lambda h: (0, 0, 0, h)),
            pl.BlockSpec((2, characters, tokens, HEAD_DIM), lambda h: (0, 0, 0, h)),
            pl.BlockSpec((2, frame_keys, HEAD_DIM), lambda h: (0, 0, h)),
        ],
        out_specs=[
            pl.BlockSpec((shards, HEAD_DIM, rows), lambda h: (0, h, 0)),
            pl.BlockSpec((shards, HEAD_DIM, rows), lambda h: (0, h, 0)),
            pl.BlockSpec((shards, 2, heads, rows), lambda h: (0, 0, 0, 0)),
        ],
        out_shape=[
            jax.ShapeDtypeStruct((shards, width, rows), jnp.bfloat16),
            jax.ShapeDtypeStruct((shards, width, rows), jnp.bfloat16),
            jax.ShapeDtypeStruct((shards, 2, heads, rows), jnp.float32),
        ],
        compiler_params=pltpu.CompilerParams(vmem_limit_bytes=32 * 1024 * 1024),
        cost_estimate=pl.CostEstimate(
            flops=4 * flops,
            bytes_accessed=2 * (queries.size + bank.size + frame_kv.size + queries.size),
            transcendentals=shards * rows * heads * (2 * tokens + frame_keys),
        ),
    )(slots, live, queries, bank, frame_kv)


def local(bank_query, char_bank, char_slots, slot_live, frame_tokens, out_weight):
    spatial, frames_here, width = bank_query.shape
    heads_here = width // HEAD_DIM
    head_groups = lax.axis_size("heads")
    shard_count = lax.axis_size("frames")
    across = 1 << ((shard_count.bit_length() - 1) // 2)
    along = shard_count // across
    lines = [[z * across + y for z in range(along)] for y in range(across)]
    column = lax.axis_index("frames") % across

    def mine(table):
        return lax.dynamic_index_in_dim(table.reshape(along, across, 2), column, 1, keepdims=False)

    slots, live = mine(char_slots), mine(slot_live)

    def from_plane(block):
        copies = [block]
        for step in range(1, across):
            pairs = [
                (z * across + y, z * across + (y + step) % across)
                for z in range(along)
                for y in range(across)
            ]
            copies.append(lax.ppermute(block, "frames", pairs))
        return copies

    parts = PARTS
    rows = spatial // parts * frames_here

    def part_of(block, part):
        lead = block.shape[:-3]
        cut = block.reshape(*lead, head_groups, parts, spatial // head_groups // parts, frames_here, width)
        return cut[..., part, :, :, :].reshape(*lead, rows, width)

    bank = jnp.concatenate(from_plane(char_bank), axis=2)
    pieces = []
    for part in range(parts):
        queries = jnp.stack([part_of(bank_query, part), part_of(frame_tokens[0], part)])
        queries = lax.all_gather(queries, "frames", axis_index_groups=lines)
        frame_kv = jnp.concatenate(from_plane(part_of(frame_tokens[1:], part)), axis=1)
        ref_part, frame_part, stats = attend(frames_here, slots, live, queries, bank, frame_kv)
        levels = lax.all_gather(stats, "frames", axis_index_groups=lines)
        peak = jnp.max(levels, axis=0)
        share = jnp.exp(stats - peak) / jnp.sum(jnp.exp(levels - peak), axis=0)
        share = share[:, :, :, None, :]
        split = (along, heads_here, HEAD_DIM, rows)
        summed = (
            ref_part.reshape(split).astype(jnp.float32) * share[:, 0]
            + frame_part.reshape(split).astype(jnp.float32) * share[:, 1]
        ).astype(jnp.bfloat16).reshape(along, width, rows)
        combined = lax.psum_scatter(
            summed, "frames", scatter_dimension=0, axis_index_groups=lines, tiled=False
        )
        projected = lax.dot_general(
            combined, out_weight, (((0,), (0,)), ((), ())), preferred_element_type=jnp.float32
        ).astype(jnp.bfloat16)
        pieces.append(lax.psum_scatter(projected, "heads", scatter_dimension=0, tiled=True))
    return jnp.concatenate(pieces, axis=0).reshape(spatial // head_groups, frames_here, -1)


def solution(mesh):
    in_specs = (
        P(None, "frames", "heads"),
        P(None, None, "frames", "heads"),
        P(),
        P(),
        P(None, None, "frames", "heads"),
        P("heads", None),
    )
    out_specs = P("heads", "frames", None)
    return jax.shard_map(local, mesh=mesh, in_specs=in_specs, out_specs=out_specs, check_vma=False)
```

```python
import functools

import jax
import jax.numpy as jnp
from jax import lax
from jax.experimental import pallas as pl
from jax.experimental.pallas import tpu as pltpu
from jax.sharding import PartitionSpec as P

HEAD_DIM = 128
PARTS = 4
SPOTS = 8
VMEM_BYTES = 48 * 1024 * 1024


def attend_columns(keys, values, queries, allowed):
    scale = HEAD_DIM ** (-0.5)
    scores = lax.dot_general(
        keys, queries, (((1,), (1,)), ((), ())), preferred_element_type=jnp.float32
    )
    scores = jnp.where(allowed, scores, -jnp.inf)
    peak = jnp.max(scores, axis=0, keepdims=True)
    weights = jnp.exp((scores - peak) * scale)
    totals = jnp.sum(weights, axis=0, keepdims=True)
    gathered = lax.dot_general(
        values, weights.astype(jnp.bfloat16), (((0,), (0,)), ((), ())),
        preferred_element_type=jnp.float32,
    )
    return gathered * (1.0 / totals), peak * scale + jnp.log(totals)


def attend_kernel(frames_here, banks, slots_ref, live_ref, query_ref, *refs):
    bank_refs, frame_refs = refs[:banks], refs[banks:-3]
    ref_out, frame_out, stats_ref = refs[-3:]
    head = pl.program_id(0)
    shards, _, rows, _ = query_ref.shape
    tokens = sum(bank.shape[2] for bank in bank_refs)
    second = lax.broadcasted_iota(jnp.int32, (2 * tokens, rows), 0) >= tokens
    for shard in range(shards):
        keys, values = (
            jnp.concatenate(
                [bank[which, slots_ref[shard, slot]] for slot in range(2) for bank in bank_refs], axis=0
            )
            for which in range(2)
        )
        open_second = live_ref[shard, 1] > 0
        gathered, level = attend_columns(
            keys, values, query_ref[shard, 0], jnp.logical_or(jnp.logical_not(second), open_second)
        )
        ref_out[shard] = gathered.astype(ref_out.dtype)
        stats_ref[shard, 0, pl.ds(head, 1), :] = level
    block = SPOTS * frames_here
    copies = len(frame_refs)
    key_spot = lax.broadcasted_iota(jnp.int32, (copies * block, shards * block), 0) % block // frames_here
    query_spot = lax.broadcasted_iota(jnp.int32, (copies * block, shards * block), 1) % block // frames_here
    same_spot = key_spot == query_spot
    results = []
    for low in range(0, rows, block):
        here = slice(low, low + block)
        keys, values = (
            jnp.concatenate([frame[which, here] for frame in frame_refs], axis=0) for which in range(2)
        )
        queries = jnp.concatenate([query_ref[shard, 1, here] for shard in range(shards)], axis=0)
        results.append(attend_columns(keys, values, queries, same_spot))
    for shard in range(shards):
        here = slice(shard * block, (shard + 1) * block)
        frame_out[shard] = jnp.concatenate(
            [gathered[:, here] for gathered, _ in results], axis=1
        ).astype(frame_out.dtype)
        stats_ref[shard, 1, pl.ds(head, 1), :] = jnp.concatenate(
            [level[:, here] for _, level in results], axis=1
        )


def attend(frames_here, slots, live, queries, banks, frame_kv):
    shards, _, rows, width = queries.shape
    heads = width // HEAD_DIM
    _, characters, tokens, _ = banks[0].shape
    keys_each = 2 * tokens * len(banks) + SPOTS * frames_here * len(frame_kv)
    kernel_flops = 4 * shards * rows * width * keys_each
    bytes_read = 2 * (2 * queries.size + len(banks) * banks[0].size + len(frame_kv) * frame_kv[0].size)
    return pl.pallas_call(
        functools.partial(attend_kernel, frames_here, len(banks)),
        grid=(heads,),
        in_specs=[
            pl.BlockSpec(memory_space=pltpu.SMEM),
            pl.BlockSpec(memory_space=pltpu.SMEM),
            pl.BlockSpec((shards, 2, rows, HEAD_DIM), lambda h: (0, 0, 0, h)),
        ]
        + [pl.BlockSpec((2, characters, tokens, HEAD_DIM), lambda h: (0, 0, 0, h)) for _ in banks]
        + [pl.BlockSpec((2, rows, HEAD_DIM), lambda h: (0, 0, h)) for _ in frame_kv],
        out_specs=[
            pl.BlockSpec((shards, HEAD_DIM, rows), lambda h: (0, h, 0)),
            pl.BlockSpec((shards, HEAD_DIM, rows), lambda h: (0, h, 0)),
            pl.BlockSpec((shards, 2, heads, rows), lambda h: (0, 0, 0, 0)),
        ],
        out_shape=[
            jax.ShapeDtypeStruct((shards, width, rows), jnp.bfloat16),
            jax.ShapeDtypeStruct((shards, width, rows), jnp.bfloat16),
            jax.ShapeDtypeStruct((shards, 2, heads, rows), jnp.float32),
        ],
        compiler_params=pltpu.CompilerParams(vmem_limit_bytes=VMEM_BYTES),
        cost_estimate=pl.CostEstimate(
            flops=8 * kernel_flops,
            bytes_accessed=bytes_read,
            transcendentals=shards * rows * heads * keys_each,
        ),
    )(slots, live, queries, *banks, *frame_kv)


def local(bank_query, char_bank, char_slots, slot_live, frame_tokens, out_weight):
    spatial, frames_here, width = bank_query.shape
    heads_here = width // HEAD_DIM
    head_groups = lax.axis_size("heads")
    shard_count = lax.axis_size("frames")
    across = 1 << ((shard_count.bit_length() - 1) // 2)
    along = shard_count // across
    place = lax.axis_index("frames")
    z, column = place // across, place % across
    parts = PARTS
    rows = spatial // parts * frames_here

    def along_z(block, moves):
        pairs = [(a * across + y, b * across + y) for a, b in moves for y in range(across)]
        return lax.ppermute(block, "frames", pairs)

    def from_plane(block):
        copies = [block]
        for step in range(1, across):
            pairs = [
                (a * across + y, a * across + (y + step) % across)
                for a in range(along)
                for y in range(across)
            ]
            copies.append(lax.ppermute(block, "frames", pairs))
        return copies

    def mine(table):
        table = lax.dynamic_index_in_dim(table.reshape(along, across, 2), column, 1, keepdims=False)
        return jnp.roll(table, -z, axis=0)

    def gather_line(block):
        from_low, from_high = [block], [block]
        for step in range(1, along):
            from_low.append(along_z(from_low[-1], [(a, a + 1) for a in range(step - 1, along - 1)]))
            from_high.append(along_z(from_high[-1], [(a, a - 1) for a in range(1, along + 1 - step)]))
        return jnp.stack(
            [block] + [jnp.where(z + r < along, from_high[r], from_low[along - r]) for r in range(1, along)]
        )

    def scatter_line(blocks):
        def wide(block):
            return block.astype(jnp.float32)

        upward, downward = blocks[along - 1], blocks[1]
        for far in range(along - 1, 0, -1):
            upward = along_z(upward, [(a, a + 1) for a in range(along - far)])
            downward = along_z(downward, [(a, a - 1) for a in range(far, along)])
            if far > 1:
                upward = (wide(blocks[far - 1]) + wide(upward)).astype(jnp.bfloat16)
                downward = (wide(blocks[along + 1 - far]) + wide(downward)).astype(jnp.bfloat16)
        return (wide(blocks[0]) + wide(upward) + wide(downward)).astype(jnp.bfloat16)

    def weigh(stats):
        levels = [stats]
        for step in range(1, along):
            arrived = along_z(stats, [((a + step) % along, a) for a in range(along)])
            levels.append(jnp.roll(arrived, step, axis=0))
        peak = functools.reduce(jnp.maximum, levels)
        total = functools.reduce(jnp.add, [jnp.exp(level - peak) for level in levels])
        return jnp.exp(stats - peak) / total

    place_heads = lax.axis_index("heads")
    chips, core = head_groups // 2, place_heads % 2
    chip = place_heads // 2

    def scatter_heads(block):
        block = block.reshape(chips, 2, -1, block.shape[-1])
        give = lax.dynamic_index_in_dim(block, 1 - core, 1, keepdims=False)
        keep = lax.dynamic_index_in_dim(block, core, 1, keepdims=False)
        got = lax.ppermute(give, "heads", [(h, h ^ 1) for h in range(head_groups)])
        summed = (keep.astype(jnp.float32) + got.astype(jnp.float32)).astype(jnp.bfloat16)
        result = lax.dynamic_index_in_dim(summed, chip, 0, keepdims=False).astype(jnp.float32)
        for step in range(1, chips):
            give = lax.dynamic_index_in_dim(summed, (chip + step) % chips, 0, keepdims=False)
            got = lax.ppermute(give, "heads", [(h, (h + 2 * step) % head_groups) for h in range(head_groups)])
            result = result + got.astype(jnp.float32)
        return result.astype(jnp.bfloat16)

    def part_of(block, part):
        lead = block.shape[:-3]
        cut = block.reshape(*lead, head_groups, parts, spatial // head_groups // parts, frames_here, width)
        return cut[..., part, :, :, :].reshape(*lead, rows, width)

    slots, live = mine(char_slots), mine(slot_live)
    banks = from_plane(char_bank)
    if char_bank.shape[2] % 16:
        banks = [jnp.concatenate(banks, axis=2)]
    pieces = []
    for part in range(parts):
        queries = gather_line(jnp.stack([part_of(bank_query, part), part_of(frame_tokens[0], part)]))
        frame_kv = from_plane(part_of(frame_tokens[1:], part))
        ref_part, frame_part, stats = attend(frames_here, slots, live, queries, banks, frame_kv)
        share = weigh(stats)[:, :, :, None, :]
        split = (along, heads_here, HEAD_DIM, rows)
        blocks = (
            ref_part.reshape(split).astype(jnp.float32) * share[:, 0]
            + frame_part.reshape(split).astype(jnp.float32) * share[:, 1]
        ).astype(jnp.bfloat16).reshape(along, width, rows)
        combined = scatter_line([blocks[r] for r in range(along)])
        projected = lax.dot_general(
            combined, out_weight, (((0,), (0,)), ((), ())), preferred_element_type=jnp.float32
        ).astype(jnp.bfloat16)
        pieces.append(scatter_heads(projected))
    return jnp.concatenate(pieces, axis=0).reshape(spatial // head_groups, frames_here, -1)


def solution(mesh):
    in_specs = (
        P(None, "frames", "heads"),
        P(None, None, "frames", "heads"),
        P(),
        P(),
        P(None, None, "frames", "heads"),
        P("heads", None),
    )
    out_specs = P("heads", "frames", None)
    return jax.shard_map(local, mesh=mesh, in_specs=in_specs, out_specs=out_specs, check_vma=False)
```

```python
import functools

import jax
import jax.numpy as jnp
from jax import lax
from jax.experimental import pallas as pl
from jax.experimental.pallas import tpu as pltpu
from jax.sharding import PartitionSpec as P

HEAD_DIM = 128
PARTS = 4
SPOTS = 8
VMEM_BYTES = 48 * 1024 * 1024
KERNEL_FROM = 7


def after(block, *before):
    return lax.optimization_barrier((block, *before))[0] if before else block


def attend_columns(keys, values, queries, allowed):
    scale = HEAD_DIM ** (-0.5)
    scores = lax.dot_general(
        keys, queries, (((1,), (1,)), ((), ())), preferred_element_type=jnp.float32
    )
    scores = jnp.where(allowed, scores, -jnp.inf)
    peak = jnp.max(scores, axis=0, keepdims=True)
    weights = jnp.exp((scores - peak) * scale)
    totals = jnp.sum(weights, axis=0, keepdims=True)
    gathered = lax.dot_general(
        values, weights.astype(jnp.bfloat16), (((0,), (0,)), ((), ())),
        preferred_element_type=jnp.float32,
    )
    return gathered * (1.0 / totals), peak * scale + jnp.log(totals)


def attend_kernel(frames_here, banks, slots_ref, live_ref, query_ref, *refs):
    bank_refs, frame_refs = refs[:banks], refs[banks:-3]
    ref_out, frame_out, stats_ref = refs[-3:]
    head = pl.program_id(0)
    shards, _, rows, _ = query_ref.shape
    tokens = sum(bank.shape[2] for bank in bank_refs)
    second = lax.broadcasted_iota(jnp.int32, (2 * tokens, rows), 0) >= tokens
    for shard in range(shards):
        keys, values = (
            jnp.concatenate(
                [bank[which, slots_ref[shard, slot]] for slot in range(2) for bank in bank_refs], axis=0
            )
            for which in range(2)
        )
        open_second = live_ref[shard, 1] > 0
        gathered, level = attend_columns(
            keys, values, query_ref[shard, 0], jnp.logical_or(jnp.logical_not(second), open_second)
        )
        ref_out[shard] = gathered.astype(ref_out.dtype)
        stats_ref[shard, 0, pl.ds(head, 1), :] = level
    block = SPOTS * frames_here
    copies = len(frame_refs)
    key_spot = lax.broadcasted_iota(jnp.int32, (copies * block, shards * block), 0) % block // frames_here
    query_spot = lax.broadcasted_iota(jnp.int32, (copies * block, shards * block), 1) % block // frames_here
    same_spot = key_spot == query_spot
    results = []
    for low in range(0, rows, block):
        here = slice(low, low + block)
        keys, values = (
            jnp.concatenate([frame[which, here] for frame in frame_refs], axis=0) for which in range(2)
        )
        queries = jnp.concatenate([query_ref[shard, 1, here] for shard in range(shards)], axis=0)
        results.append(attend_columns(keys, values, queries, same_spot))
    for shard in range(shards):
        here = slice(shard * block, (shard + 1) * block)
        frame_out[shard] = jnp.concatenate(
            [gathered[:, here] for gathered, _ in results], axis=1
        ).astype(frame_out.dtype)
        stats_ref[shard, 1, pl.ds(head, 1), :] = jnp.concatenate(
            [level[:, here] for _, level in results], axis=1
        )


def attend(frames_here, slots, live, queries, banks, frame_kv):
    shards, _, rows, width = queries.shape
    heads = width // HEAD_DIM
    _, characters, tokens, _ = banks[0].shape
    keys_each = 2 * tokens * len(banks) + SPOTS * frames_here * len(frame_kv)
    kernel_flops = 4 * shards * rows * width * keys_each
    bytes_read = 2 * (2 * queries.size + len(banks) * banks[0].size + len(frame_kv) * frame_kv[0].size)
    return pl.pallas_call(
        functools.partial(attend_kernel, frames_here, len(banks)),
        grid=(heads,),
        in_specs=[
            pl.BlockSpec(memory_space=pltpu.SMEM),
            pl.BlockSpec(memory_space=pltpu.SMEM),
            pl.BlockSpec((shards, 2, rows, HEAD_DIM), lambda h: (0, 0, 0, h)),
        ]
        + [pl.BlockSpec((2, characters, tokens, HEAD_DIM), lambda h: (0, 0, 0, h)) for _ in banks]
        + [pl.BlockSpec((2, rows, HEAD_DIM), lambda h: (0, 0, h)) for _ in frame_kv],
        out_specs=[
            pl.BlockSpec((shards, HEAD_DIM, rows), lambda h: (0, h, 0)),
            pl.BlockSpec((shards, HEAD_DIM, rows), lambda h: (0, h, 0)),
            pl.BlockSpec((shards, 2, heads, rows), lambda h: (0, 0, 0, 0)),
        ],
        out_shape=[
            jax.ShapeDtypeStruct((shards, width, rows), jnp.bfloat16),
            jax.ShapeDtypeStruct((shards, width, rows), jnp.bfloat16),
            jax.ShapeDtypeStruct((shards, 2, heads, rows), jnp.float32),
        ],
        compiler_params=pltpu.CompilerParams(vmem_limit_bytes=VMEM_BYTES),
        cost_estimate=pl.CostEstimate(
            flops=8 * kernel_flops,
            bytes_accessed=bytes_read,
            transcendentals=shards * rows * heads * keys_each,
        ),
    )(slots, live, queries, *banks, *frame_kv)


def local(bank_query, char_bank, char_slots, slot_live, frame_tokens, out_weight):
    spatial, frames_here, width = bank_query.shape
    heads_here = width // HEAD_DIM
    head_groups = lax.axis_size("heads")
    shard_count = lax.axis_size("frames")
    across = 1 << ((shard_count.bit_length() - 1) // 2)
    along = shard_count // across
    place = lax.axis_index("frames")
    z, column = place // across, place % across
    parts = PARTS
    rows = spatial // parts * frames_here

    def along_z(block, moves):
        pairs = [(a * across + y, b * across + y) for a, b in moves for y in range(across)]
        return lax.ppermute(block, "frames", pairs)

    def from_plane(block):
        copies = [block]
        for step in range(1, across):
            pairs = [
                (a * across + y, a * across + (y + step) % across)
                for a in range(along)
                for y in range(across)
            ]
            copies.append(lax.ppermute(block, "frames", pairs))
        return copies

    def mine(table):
        table = lax.dynamic_index_in_dim(table.reshape(along, across, 2), column, 1, keepdims=False)
        return jnp.roll(table, -z, axis=0)

    def gather_step(low, high, step):
        return (
            along_z(low, [(a, a + 1) for a in range(step - 1, along - 1)]),
            along_z(high, [(a, a - 1) for a in range(1, along + 1 - step)]),
        )

    def place_line(from_low, from_high):
        return jnp.stack(
            [from_low[0]]
            + [jnp.where(z + r < along, from_high[r], from_low[along - r]) for r in range(1, along)]
        )

    def scatter_line(blocks):
        def wide(block):
            return block.astype(jnp.float32)

        upward, downward = blocks[along - 1], blocks[1]
        for far in range(along - 1, 0, -1):
            upward = along_z(upward, [(a, a + 1) for a in range(along - far)])
            downward = along_z(downward, [(a, a - 1) for a in range(far, along)])
            if far > 1:
                upward = (wide(blocks[far - 1]) + wide(upward)).astype(jnp.bfloat16)
                downward = (wide(blocks[along + 1 - far]) + wide(downward)).astype(jnp.bfloat16)
        return (wide(blocks[0]) + wide(upward) + wide(downward)).astype(jnp.bfloat16)

    def weigh(stats):
        levels = [stats]
        for step in range(1, along):
            arrived = along_z(stats, [((a + step) % along, a) for a in range(along)])
            levels.append(jnp.roll(arrived, step, axis=0))
        peak = functools.reduce(jnp.maximum, levels)
        total = functools.reduce(jnp.add, [jnp.exp(level - peak) for level in levels])
        return jnp.exp(stats - peak) / total

    place_heads = lax.axis_index("heads")
    chips, core = head_groups // 2, place_heads % 2
    chip = place_heads // 2

    def scatter_heads(block):
        block = block.reshape(chips, 2, -1, block.shape[-1])
        give = lax.dynamic_index_in_dim(block, 1 - core, 1, keepdims=False)
        keep = lax.dynamic_index_in_dim(block, core, 1, keepdims=False)
        got = lax.ppermute(give, "heads", [(h, h ^ 1) for h in range(head_groups)])
        summed = (keep.astype(jnp.float32) + got.astype(jnp.float32)).astype(jnp.bfloat16)
        result = lax.dynamic_index_in_dim(summed, chip, 0, keepdims=False).astype(jnp.float32)
        for step in range(1, chips):
            give = lax.dynamic_index_in_dim(summed, (chip + step) % chips, 0, keepdims=False)
            got = lax.ppermute(give, "heads", [(h, (h + 2 * step) % head_groups) for h in range(head_groups)])
            result = result + got.astype(jnp.float32)
        return result.astype(jnp.bfloat16)

    def part_of(block, part):
        lead = block.shape[:-3]
        cut = block.reshape(*lead, head_groups, parts, spatial // head_groups // parts, frames_here, width)
        return cut[..., part, :, :, :].reshape(*lead, rows, width)

    slots, live = mine(char_slots), mine(slot_live)
    banks = from_plane(char_bank)
    if char_bank.shape[2] % 16:
        banks = [jnp.concatenate(banks, axis=2)]

    gathered, frame_kv, attended = {}, {}, {}

    def begin(part, *before):
        queries = jnp.stack([part_of(bank_query, part), part_of(frame_tokens[0], part)])
        queries = after(queries, *before)
        gathered[part] = ([queries], [queries])

    def extend(part, *before):
        low, high = gathered[part]
        moved = gather_step(after(low[-1], *before), after(high[-1], *before), len(low))
        low.append(moved[0])
        high.append(moved[1])

    def last(part, step=-1):
        return [line[step] for line in gathered[part]]

    def compute(part):
        queries = place_line(*gathered[part])
        attended[part] = attend(frames_here, slots, live, queries, banks, frame_kv[part])
        return attended[part][2]

    kv_before = []
    for part in range(parts):
        frame_kv[part] = from_plane(after(part_of(frame_tokens[1:], part), *kv_before))
        kv_before = [banks[-1]] if part == 0 else frame_kv[part][1:]

    for part in range(parts):
        begin(part)
    events = sorted(
        ((2 * part + step * 2 - (1 if part else 0), part, step) for part in range(parts) for step in range(1, along)),
    )
    in_flight = []
    done_parts = []
    for _, part, step in events:
        before = []
        if len(in_flight) >= 2:
            before += last(*in_flight[-2])
        ready = [p for p in range(parts) if p not in done_parts and len(gathered[p][0]) == along]
        if ready and len(in_flight) >= KERNEL_FROM:
            done_parts.append(ready[0])
            before.append(compute(ready[0]))
        extend(part, *before)
        in_flight.append((part, step))
    for part in range(parts):
        if part not in done_parts:
            compute(part)

    pieces = []
    for part in range(parts):
        ref_part, frame_part, stats = attended[part]
        share = weigh(stats)[:, :, :, None, :]
        split = (along, heads_here, HEAD_DIM, rows)
        blocks = (
            ref_part.reshape(split).astype(jnp.float32) * share[:, 0]
            + frame_part.reshape(split).astype(jnp.float32) * share[:, 1]
        ).astype(jnp.bfloat16).reshape(along, width, rows)
        combined = scatter_line([blocks[r] for r in range(along)])
        projected = lax.dot_general(
            combined, out_weight, (((0,), (0,)), ((), ())), preferred_element_type=jnp.float32
        ).astype(jnp.bfloat16)
        pieces.append(scatter_heads(projected))
    return jnp.concatenate(pieces, axis=0).reshape(spatial // head_groups, frames_here, -1)


def solution(mesh):
    in_specs = (
        P(None, "frames", "heads"),
        P(None, None, "frames", "heads"),
        P(),
        P(),
        P(None, None, "frames", "heads"),
        P("heads", None),
    )
    out_specs = P("heads", "frames", None)
    return jax.shard_map(local, mesh=mesh, in_specs=in_specs, out_specs=out_specs, check_vma=False)
```

```python
import functools

import jax
import jax.numpy as jnp
from jax import lax
from jax.experimental import pallas as pl
from jax.experimental.pallas import tpu as pltpu
from jax.sharding import PartitionSpec as P

HEAD_DIM = 128
PARTS = 4
SPOTS = 8
VMEM_BYTES = 48 * 1024 * 1024


def after(block, *before):
    return lax.optimization_barrier((block, *before))[0] if before else block


def attend_columns(keys, values, queries, allowed):
    scale = HEAD_DIM ** (-0.5)
    scores = lax.dot_general(
        keys, queries, (((1,), (1,)), ((), ())), preferred_element_type=jnp.float32
    )
    scores = jnp.where(allowed, scores, -jnp.inf)
    peak = jnp.max(scores, axis=0, keepdims=True)
    weights = jnp.exp((scores - peak) * scale)
    totals = jnp.sum(weights, axis=0, keepdims=True)
    gathered = lax.dot_general(
        values, weights.astype(jnp.bfloat16), (((0,), (0,)), ((), ())),
        preferred_element_type=jnp.float32,
    )
    return gathered * (1.0 / totals), peak * scale + jnp.log(totals)


def pick(choices, refs, inner_plane, which, here=slice(None)):
    pieces, low = [], 0
    for count in choices:
        options = [ref[which, here] for ref in refs[low : low + count]]
        pieces.append(options[0] if count == 1 else jnp.where(inner_plane, options[0], options[1]))
        low += count
    return pieces


def bank_kernel(choices, banks, slots_ref, live_ref, plane_ref, *refs):
    pieces = sum(choices)
    query_refs, bank_refs = refs[:pieces], refs[pieces : pieces + banks]
    out_ref, stats_ref = refs[-2:]
    head = pl.program_id(0)
    queries = pick(choices, query_refs, plane_ref[0] > 0, 0)
    tokens = sum(bank.shape[2] for bank in bank_refs)
    second = lax.broadcasted_iota(jnp.int32, (2 * tokens, queries[0].shape[0]), 0) >= tokens
    for shard, rows in enumerate(queries):
        keys, values = (
            jnp.concatenate(
                [bank[which, slots_ref[shard, slot]] for slot in range(2) for bank in bank_refs], axis=0
            )
            for which in range(2)
        )
        open_second = live_ref[shard, 1] > 0
        gathered, level = attend_columns(
            keys, values, rows, jnp.logical_or(jnp.logical_not(second), open_second)
        )
        out_ref[shard] = gathered.astype(out_ref.dtype)
        stats_ref[shard, pl.ds(head, 1), :] = level


def frame_kernel(choices, frames_here, plane_ref, *refs):
    pieces = sum(choices)
    query_refs, frame_refs = refs[:pieces], refs[pieces:-2]
    out_ref, stats_ref = refs[-2:]
    head = pl.program_id(0)
    shards = len(choices)
    rows = out_ref.shape[2]
    block = SPOTS * frames_here
    copies = len(frame_refs)
    key_spot = lax.broadcasted_iota(jnp.int32, (copies * block, shards * block), 0) % block // frames_here
    query_spot = lax.broadcasted_iota(jnp.int32, (copies * block, shards * block), 1) % block // frames_here
    same_spot = key_spot == query_spot
    results = []
    for low in range(0, rows, block):
        here = slice(low, low + block)
        keys, values = (
            jnp.concatenate([frame[which, here] for frame in frame_refs], axis=0) for which in range(2)
        )
        queries = jnp.concatenate(pick(choices, query_refs, plane_ref[0] > 0, 1, here), axis=0)
        results.append(attend_columns(keys, values, queries, same_spot))
    for shard in range(shards):
        here = slice(shard * block, (shard + 1) * block)
        out_ref[shard] = jnp.concatenate(
            [gathered[:, here] for gathered, _ in results], axis=1
        ).astype(out_ref.dtype)
        stats_ref[shard, pl.ds(head, 1), :] = jnp.concatenate(
            [level[:, here] for _, level in results], axis=1
        )


def attend(body, choices, keys_each, tables, pieces, sources):
    shards = len(choices)
    _, rows, width = pieces[0].shape
    heads = width // HEAD_DIM
    read = sum(block.size for block in pieces) // 2 + sum(block.size for block in sources)

    def column(block):
        lead = block.ndim - 1
        return pl.BlockSpec((*block.shape[:-1], HEAD_DIM), lambda h: (0,) * lead + (h,))

    return pl.pallas_call(
        body,
        grid=(heads,),
        in_specs=[pl.BlockSpec(memory_space=pltpu.SMEM) for _ in tables]
        + [column(block) for block in (*pieces, *sources)],
        out_specs=[
            pl.BlockSpec((shards, HEAD_DIM, rows), lambda h: (0, h, 0)),
            pl.BlockSpec((shards, heads, rows), lambda h: (0, 0, 0)),
        ],
        out_shape=[
            jax.ShapeDtypeStruct((shards, width, rows), jnp.bfloat16),
            jax.ShapeDtypeStruct((shards, heads, rows), jnp.float32),
        ],
        compiler_params=pltpu.CompilerParams(vmem_limit_bytes=VMEM_BYTES),
        cost_estimate=pl.CostEstimate(
            flops=32 * shards * rows * width * keys_each,
            bytes_accessed=2 * (read + shards * rows * width),
            transcendentals=shards * rows * heads * keys_each,
        ),
    )(*tables, *pieces, *sources)


def wide(block):
    return block.astype(jnp.float32)


def added(*blocks):
    return functools.reduce(jnp.add, [wide(block) for block in blocks]).astype(jnp.bfloat16)


def local(bank_query, char_bank, char_slots, slot_live, frame_tokens, out_weight):
    spatial, frames_here, width = bank_query.shape
    heads_here = width // HEAD_DIM
    head_groups = lax.axis_size("heads")
    shard_count = lax.axis_size("frames")
    across = 1 << ((shard_count.bit_length() - 1) // 2)
    along = shard_count // across
    place = lax.axis_index("frames")
    z, column = place // across, place % across
    parts = PARTS
    rows = spatial // parts * frames_here
    relayed = along == 4
    inner_plane = jnp.logical_and(z > 0, z < along - 1).astype(jnp.int32).reshape(1)
    to_inner, to_ends, between = [(0, 1), (3, 2)], [(1, 0), (2, 3)], [(1, 2), (2, 1)]

    def along_z(block, moves):
        pairs = [(a * across + y, b * across + y) for a, b in moves for y in range(across)]
        return lax.ppermute(block, "frames", pairs)

    def swap(block, step):
        return along_z(block, [(a, a ^ step) for a in range(along)])

    def from_plane(block):
        copies = [block]
        for step in range(1, across):
            pairs = [(a * across + y, a * across + (y ^ step)) for a in range(along) for y in range(across)]
            copies.append(lax.ppermute(block, "frames", pairs))
        return copies

    def mine(table):
        table = lax.dynamic_index_in_dim(table.reshape(along, across, 2), column, 1, keepdims=False)
        return table[jnp.arange(along) ^ z]

    def scatter_line(blocks):
        if not relayed:
            return added(blocks[0], *[swap(blocks[r], r) for r in range(1, along)])
        far = along_z(blocks[3], to_inner)
        near = along_z(blocks[2], to_inner)
        far = along_z(added(blocks[2], far), between)
        near = along_z(added(blocks[3], near), between)
        return added(blocks[0], near, swap(added(blocks[1], far), 1))

    def weigh(stats):
        levels = [stats]
        for step in range(1, along):
            arrived = swap(stats, step)
            levels.append(jnp.stack([arrived[r ^ step] for r in range(along)]))
        peak = functools.reduce(jnp.maximum, levels)
        total = functools.reduce(jnp.add, [jnp.exp(level - peak) for level in levels])
        return jnp.exp(stats - peak) / total

    place_heads = lax.axis_index("heads")
    chips, core = head_groups // 2, place_heads % 2
    chip = place_heads // 2

    def scatter_heads(block):
        block = block.reshape(chips, 2, -1, block.shape[-1])
        give = lax.dynamic_index_in_dim(block, 1 - core, 1, keepdims=False)
        keep = lax.dynamic_index_in_dim(block, core, 1, keepdims=False)
        got = lax.ppermute(give, "heads", [(h, h ^ 1) for h in range(head_groups)])
        summed = added(keep, got)
        parcels = [lax.dynamic_index_in_dim(summed, chip, 0, keepdims=False)]
        for step in range(1, chips):
            give = lax.dynamic_index_in_dim(summed, (chip + step) % chips, 0, keepdims=False)
            parcels.append(
                lax.ppermute(give, "heads", [(h, (h + 2 * step) % head_groups) for h in range(head_groups)])
            )
        return added(*parcels)

    def part_of(block, part):
        lead = block.shape[:-3]
        cut = block.reshape(*lead, head_groups, parts, spatial // head_groups // parts, frames_here, width)
        return cut[..., part, :, :, :].reshape(*lead, rows, width)

    slots, live = mine(char_slots), mine(slot_live)
    banks = from_plane(char_bank)
    if char_bank.shape[2] % 16:
        banks = [jnp.concatenate(banks, axis=2)]
    tokens = sum(bank.shape[2] for bank in banks)

    frame_kv, kv_before = {}, []
    for part in range(parts):
        frame_kv[part] = from_plane(after(part_of(frame_tokens[1:], part), *kv_before))
        kv_before = banks[-1:] if part == 0 else frame_kv[part][-1:]

    own = {p: jnp.stack([part_of(bank_query, p), part_of(frame_tokens[0], p)]) for p in range(parts)}
    near, mids, relay, ends, far, results = {}, {}, {}, {}, {}, {}

    def compute(part, *before):
        if relayed:
            choices = (1, 1, 2, 2)
            pieces = [own[part], near[part], relay[part], ends[part], mids[part], far[part]]
        else:
            choices = (1,) * along
            pieces = [own[part]] + [swap(own[part], r) for r in range(1, along)]
        frame_part, frame_level = attend(
            functools.partial(frame_kernel, choices, frames_here), choices,
            SPOTS * frames_here * across, [inner_plane], pieces, frame_kv[part],
        )
        ref_part, ref_level = attend(
            functools.partial(bank_kernel, choices, len(banks)), choices,
            2 * tokens, [after(slots, *before), live, inner_plane], pieces, banks,
        )
        results[part] = ref_part, frame_part, jnp.stack([ref_level, frame_level], axis=1)
        return ref_level

    if not relayed:
        for part in range(parts):
            compute(part)
    else:
        ready = ()
        for first in range(0, parts, 2):
            pair = range(first, min(first + 2, parts))
            for part in pair:
                mids[part] = along_z(after(own[part], *([mids[part - 1]] if first else [])), between)
                before = [] if not first else [near[first - 1] if part == first else far[first - 2]]
                near[part] = swap(after(own[part], *before), 1)
            for part in pair:
                before = ready if first else (frame_kv[0][-1:] if part == 0 else ())
                relay[part] = along_z(after(near[part], *before), between)
                ends[part] = along_z(after(mids[part], *before), to_ends)
            for part in pair:
                far[part] = along_z(relay[part], to_ends)
            waits = [relay[pair[-1]], ends[pair[-1]]] if first == 0 else []
            ready = [compute(part, *waits) for part in pair][-1:]

    pieces = []
    for part in range(parts):
        ref_part, frame_part, stats = results[part]
        share = weigh(stats)[:, :, :, None, :]
        split = (along, heads_here, HEAD_DIM, rows)
        blocks = (wide(ref_part.reshape(split)) * share[:, 0] + wide(frame_part.reshape(split)) * share[:, 1])
        blocks = blocks.astype(jnp.bfloat16).reshape(along, width, rows)
        combined = scatter_line([blocks[r] for r in range(along)])
        projected = lax.dot_general(
            combined, out_weight, (((0,), (0,)), ((), ())), preferred_element_type=jnp.float32
        ).astype(jnp.bfloat16)
        pieces.append(scatter_heads(projected))
    return jnp.concatenate(pieces, axis=0).reshape(spatial // head_groups, frames_here, -1)


def solution(mesh):
    in_specs = (
        P(None, "frames", "heads"),
        P(None, None, "frames", "heads"),
        P(),
        P(),
        P(None, None, "frames", "heads"),
        P("heads", None),
    )
    out_specs = P("heads", "frames", None)
    return jax.shard_map(local, mesh=mesh, in_specs=in_specs, out_specs=out_specs, check_vma=False)
```

```python
import functools

import jax
import jax.numpy as jnp
from jax import lax
from jax.experimental import pallas as pl
from jax.experimental.pallas import tpu as pltpu
from jax.sharding import PartitionSpec as P

HEAD_DIM = 128
PARTS = 4
SPOTS = 8
VMEM_BYTES = 48 * 1024 * 1024
RELAYED_PARTS = 2


def after(block, *before):
    return lax.optimization_barrier((block, *before))[0] if before else block


def attend_columns(keys, values, queries, allowed):
    scale = HEAD_DIM ** (-0.5)
    scores = lax.dot_general(
        keys, queries, (((1,), (1,)), ((), ())), preferred_element_type=jnp.float32
    )
    scores = jnp.where(allowed, scores, -jnp.inf)
    peak = jnp.max(scores, axis=0, keepdims=True)
    weights = jnp.exp((scores - peak) * scale)
    totals = jnp.sum(weights, axis=0, keepdims=True)
    gathered = lax.dot_general(
        values, weights.astype(jnp.bfloat16), (((0,), (0,)), ((), ())),
        preferred_element_type=jnp.float32,
    )
    return gathered * (1.0 / totals), peak * scale + jnp.log(totals)


def pick(choices, refs, plane_ref, which, here=slice(None)):
    if len(refs) == 1:
        return [refs[0][plane_ref[1] ^ slot, which, here] for slot in range(len(choices))]
    pieces, low = [], 0
    for count in choices:
        options = [ref[which, here] for ref in refs[low : low + count]]
        pieces.append(options[0] if count == 1 else jnp.where(plane_ref[0] > 0, options[0], options[1]))
        low += count
    return pieces


def attend_kernel(choices, banks, frame_sets, frames_here, slots_ref, live_ref, plane_ref, *refs):
    query_refs = refs[: -3 - banks - frame_sets]
    bank_refs, frame_refs = refs[-3 - banks - frame_sets : -3 - frame_sets], refs[-3 - frame_sets : -3]
    ref_out, frame_out, stats_ref = refs[-3:]
    head = pl.program_id(0)
    queries = pick(choices, query_refs, plane_ref, 0)
    shards, rows = len(choices), ref_out.shape[2]
    tokens = sum(bank.shape[2] for bank in bank_refs)
    second = lax.broadcasted_iota(jnp.int32, (2 * tokens, rows), 0) >= tokens
    for shard in range(shards):
        keys, values = (
            jnp.concatenate(
                [bank[which, slots_ref[shard, slot]] for slot in range(2) for bank in bank_refs], axis=0
            )
            for which in range(2)
        )
        open_second = live_ref[shard, 1] > 0
        gathered, level = attend_columns(
            keys, values, queries[shard], jnp.logical_or(jnp.logical_not(second), open_second)
        )
        ref_out[shard] = gathered.astype(ref_out.dtype)
        stats_ref[shard, 0, pl.ds(head, 1), :] = level
    block = SPOTS * frames_here
    key_spot = lax.broadcasted_iota(jnp.int32, (frame_sets * block, shards * block), 0) % block // frames_here
    query_spot = lax.broadcasted_iota(jnp.int32, (frame_sets * block, shards * block), 1) % block // frames_here
    same_spot = key_spot == query_spot
    results = []
    for low in range(0, rows, block):
        here = slice(low, low + block)
        keys, values = (
            jnp.concatenate([frame[which, here] for frame in frame_refs], axis=0) for which in range(2)
        )
        packed = jnp.concatenate(pick(choices, query_refs, plane_ref, 1, here), axis=0)
        results.append(attend_columns(keys, values, packed, same_spot))
    for shard in range(shards):
        here = slice(shard * block, (shard + 1) * block)
        frame_out[shard] = jnp.concatenate(
            [gathered[:, here] for gathered, _ in results], axis=1
        ).astype(frame_out.dtype)
        stats_ref[shard, 1, pl.ds(head, 1), :] = jnp.concatenate(
            [level[:, here] for _, level in results], axis=1
        )


def attend(choices, frames_here, tables, pieces, banks, frame_kv):
    shards = len(choices)
    rows, width = pieces[0].shape[-2:]
    heads = width // HEAD_DIM
    keys_each = 2 * sum(bank.shape[2] for bank in banks) + SPOTS * frames_here * len(frame_kv)
    read = sum(block.size for block in (*pieces, *banks, *frame_kv))

    def column(block):
        lead = block.ndim - 1
        return pl.BlockSpec((*block.shape[:-1], HEAD_DIM), lambda h: (0,) * lead + (h,))

    return pl.pallas_call(
        functools.partial(attend_kernel, choices, len(banks), len(frame_kv), frames_here),
        grid=(heads,),
        in_specs=[pl.BlockSpec(memory_space=pltpu.SMEM) for _ in tables]
        + [column(block) for block in (*pieces, *banks, *frame_kv)],
        out_specs=[
            pl.BlockSpec((shards, HEAD_DIM, rows), lambda h: (0, h, 0)),
            pl.BlockSpec((shards, HEAD_DIM, rows), lambda h: (0, h, 0)),
            pl.BlockSpec((shards, 2, heads, rows), lambda h: (0, 0, 0, 0)),
        ],
        out_shape=[
            jax.ShapeDtypeStruct((shards, width, rows), jnp.bfloat16),
            jax.ShapeDtypeStruct((shards, width, rows), jnp.bfloat16),
            jax.ShapeDtypeStruct((shards, 2, heads, rows), jnp.float32),
        ],
        compiler_params=pltpu.CompilerParams(vmem_limit_bytes=VMEM_BYTES),
        cost_estimate=pl.CostEstimate(
            flops=32 * shards * rows * width * keys_each,
            bytes_accessed=2 * (read + 2 * shards * rows * width),
            transcendentals=shards * rows * heads * keys_each,
        ),
    )(*tables, *pieces, *banks, *frame_kv)


def wide(block):
    return block.astype(jnp.float32)


def added(*blocks):
    return functools.reduce(jnp.add, [wide(block) for block in blocks]).astype(jnp.bfloat16)


def local(bank_query, char_bank, char_slots, slot_live, frame_tokens, out_weight):
    spatial, frames_here, width = bank_query.shape
    heads_here = width // HEAD_DIM
    head_groups = lax.axis_size("heads")
    shard_count = lax.axis_size("frames")
    across = 1 << ((shard_count.bit_length() - 1) // 2)
    along = shard_count // across
    place = lax.axis_index("frames")
    z, column = place // across, place % across
    parts = PARTS
    rows = spatial // parts * frames_here
    relayed = along == 4
    plane = jnp.stack([jnp.logical_and(z > 0, z < along - 1).astype(jnp.int32), z])
    to_inner, to_ends, between = [(0, 1), (3, 2)], [(1, 0), (2, 3)], [(1, 2), (2, 1)]

    def along_z(block, moves):
        pairs = [(a * across + y, b * across + y) for a, b in moves for y in range(across)]
        return lax.ppermute(block, "frames", pairs)

    def swap(block, step):
        return along_z(block, [(a, a ^ step) for a in range(along)])

    def from_plane(block):
        copies = [block]
        for step in range(1, across):
            pairs = [(a * across + y, a * across + (y ^ step)) for a in range(along) for y in range(across)]
            copies.append(lax.ppermute(block, "frames", pairs))
        return copies

    def mine(table):
        table = lax.dynamic_index_in_dim(table.reshape(along, across, 2), column, 1, keepdims=False)
        return table[jnp.arange(along) ^ z]

    def scatter_line(blocks):
        if not relayed:
            return added(blocks[0], *[swap(blocks[r], r) for r in range(1, along)])
        far = along_z(blocks[3], to_inner)
        near = along_z(blocks[2], to_inner)
        far = along_z(added(blocks[2], far), between)
        near = along_z(added(blocks[3], near), between)
        return added(blocks[0], near, swap(added(blocks[1], far), 1))

    def weigh(stats):
        levels = [stats]
        for step in range(1, along):
            arrived = swap(stats, step)
            levels.append(jnp.stack([arrived[r ^ step] for r in range(along)]))
        peak = functools.reduce(jnp.maximum, levels)
        total = functools.reduce(jnp.add, [jnp.exp(level - peak) for level in levels])
        return jnp.exp(stats - peak) / total

    place_heads = lax.axis_index("heads")
    chips, core = head_groups // 2, place_heads % 2
    chip = place_heads // 2

    def scatter_heads(block):
        block = block.reshape(chips, 2, -1, block.shape[-1])
        give = lax.dynamic_index_in_dim(block, 1 - core, 1, keepdims=False)
        keep = lax.dynamic_index_in_dim(block, core, 1, keepdims=False)
        got = lax.ppermute(give, "heads", [(h, h ^ 1) for h in range(head_groups)])
        summed = added(keep, got)
        parcels = [lax.dynamic_index_in_dim(summed, chip, 0, keepdims=False)]
        for step in range(1, chips):
            give = lax.dynamic_index_in_dim(summed, (chip + step) % chips, 0, keepdims=False)
            parcels.append(
                lax.ppermute(give, "heads", [(h, (h + 2 * step) % head_groups) for h in range(head_groups)])
            )
        return added(*parcels)

    def part_of(block, part):
        lead = block.shape[:-3]
        cut = block.reshape(*lead, head_groups, parts, spatial // head_groups // parts, frames_here, width)
        return cut[..., part, :, :, :].reshape(*lead, rows, width)

    slots, live = mine(char_slots), mine(slot_live)
    banks = from_plane(char_bank)
    if char_bank.shape[2] % 16:
        banks = [jnp.concatenate(banks, axis=2)]

    frame_kv = {part: from_plane(part_of(frame_tokens[1:], part)) for part in range(parts)}
    own = {p: jnp.stack([part_of(bank_query, p), part_of(frame_tokens[0], p)]) for p in range(parts)}
    lines = [[a * across + y for a in range(along)] for y in range(across)]

    def gather_relayed(block):
        near, mids = swap(block, 1), along_z(block, between)
        relay, ends = along_z(near, between), along_z(mids, to_ends)
        far = along_z(relay, to_ends)
        return (1, 1, 2, 2), [block, near, relay, ends, mids, far]

    def merge(ref_part, frame_part, stats):
        share = weigh(stats)[:, :, :, None, :]
        split = (along, heads_here, HEAD_DIM, rows)
        blocks = wide(ref_part.reshape(split)) * share[:, 0] + wide(frame_part.reshape(split)) * share[:, 1]
        blocks = blocks.astype(jnp.bfloat16).reshape(along, width, rows)
        return scatter_line([blocks[r] for r in range(along)])

    combined, order = [], ()
    for part in range(parts):
        if relayed and part < RELAYED_PARTS:
            choices, pieces = gather_relayed(own[part])
        else:
            choices = (1,) * along
            pieces = [lax.all_gather(own[part], "frames", axis_index_groups=lines)]
        tables = [after(slots, *order, *combined[max(part - 2, 0) : max(part - 1, 0)]), live, plane]
        result = attend(choices, frames_here, tables, pieces, banks, frame_kv[part])
        order = result[-1:]
        combined.append(merge(*result))
    pieces = []
    for block in combined:
        projected = lax.dot_general(
            block, out_weight, (((0,), (0,)), ((), ())), preferred_element_type=jnp.float32
        ).astype(jnp.bfloat16)
        pieces.append(scatter_heads(projected))
    return jnp.concatenate(pieces, axis=0).reshape(spatial // head_groups, frames_here, -1)


def solution(mesh):
    in_specs = (
        P(None, "frames", "heads"),
        P(None, None, "frames", "heads"),
        P(),
        P(),
        P(None, None, "frames", "heads"),
        P("heads", None),
    )
    out_specs = P("heads", "frames", None)
    return jax.shard_map(local, mesh=mesh, in_specs=in_specs, out_specs=out_specs, check_vma=False)
```

```python
import functools

import jax
import jax.numpy as jnp
from jax import lax
from jax.experimental import pallas as pl
from jax.experimental.pallas import tpu as pltpu
from jax.sharding import PartitionSpec as P

HEAD_DIM = 128
TILE_ROWS = 16
HEAD_GROUPS = 2
VMEM_BYTES = 48 * 1024 * 1024


def after(block, *before):
    return lax.optimization_barrier((block, *before))[0] if before else block


def wide(block):
    return block.astype(jnp.float32)


def added(*blocks):
    return functools.reduce(jnp.add, [wide(block) for block in blocks]).astype(jnp.bfloat16)


def attend_columns(keys, values, queries, allowed):
    scale = HEAD_DIM ** (-0.5)
    scores = lax.dot_general(
        keys, queries, (((1,), (1,)), ((), ())), preferred_element_type=jnp.float32
    )
    scores = jnp.where(allowed, scores, -jnp.inf)
    peak = jnp.max(scores, axis=0, keepdims=True)
    weights = jnp.exp((scores - peak) * scale)
    totals = jnp.sum(weights, axis=0, keepdims=True)
    gathered = lax.dot_general(
        values, weights.astype(jnp.bfloat16), (((0,), (0,)), ((), ())),
        preferred_element_type=jnp.float32,
    )
    return gathered * (1.0 / totals), peak * scale + jnp.log(totals)


def bank_kernel(banks, live_ref, own_ref, far_ref, *refs):
    bank_refs = refs[:banks]
    head = pl.program_id(0)
    tokens = sum(bank.shape[2] for bank in bank_refs)
    second = lax.broadcasted_iota(jnp.int32, (2 * tokens, own_ref.shape[0]), 0) >= tokens
    for side, query_ref in enumerate((own_ref, far_ref)):
        out_ref, level_ref = refs[banks + 2 * side : banks + 2 * side + 2]
        keys, values = (
            jnp.concatenate([bank[which, 2 * side + slot] for slot in range(2) for bank in bank_refs], axis=0)
            for which in range(2)
        )
        allowed = jnp.logical_or(jnp.logical_not(second), live_ref[side, 1] > 0)
        gathered, level = attend_columns(keys, values, query_ref[...], allowed)
        rows = out_ref.shape[2]
        for part in range(out_ref.shape[0]):
            here = slice(part * rows, (part + 1) * rows)
            out_ref[part] = gathered[:, here].astype(out_ref.dtype)
            level_ref[part, pl.ds(head, 1), :] = level[:, here]


def attend_bank(group, parts, rows, live, own, far, banks):
    width = banks[0].shape[3]
    heads = width // HEAD_DIM
    keys_each = 2 * sum(bank.shape[2] for bank in banks)
    query_spec = pl.BlockSpec((parts * rows, HEAD_DIM), lambda h: (0, group * heads + h))
    out = jax.ShapeDtypeStruct((parts, width, rows), jnp.bfloat16)
    level = jax.ShapeDtypeStruct((parts, heads, rows), jnp.float32)
    out_spec = pl.BlockSpec((parts, HEAD_DIM, rows), lambda h: (0, h, 0))
    level_spec = pl.BlockSpec((parts, heads, rows), lambda h: (0, 0, 0))
    return pl.pallas_call(
        functools.partial(bank_kernel, len(banks)),
        grid=(heads,),
        in_specs=[pl.BlockSpec(memory_space=pltpu.SMEM), query_spec, query_spec]
        + [pl.BlockSpec((*bank.shape[:3], HEAD_DIM), lambda h: (0, 0, 0, h)) for bank in banks],
        out_specs=[out_spec, level_spec] * 2,
        out_shape=[out, level] * 2,
        compiler_params=pltpu.CompilerParams(vmem_limit_bytes=VMEM_BYTES),
        cost_estimate=pl.CostEstimate(
            flops=32 * parts * rows * width * keys_each,
            bytes_accessed=2 * (4 * parts * rows * width + sum(bank.size for bank in banks)),
            transcendentals=2 * parts * rows * heads * keys_each,
        ),
    )(live, own, far, *banks)


def frame_kernel(frames_here, *refs):
    piece_refs, out_ref = refs[:-1], refs[-1]
    scale = HEAD_DIM ** (-0.5)
    _, parts, rows, _ = piece_refs[0].shape
    size = len(piece_refs) * rows
    query_spot = lax.broadcasted_iota(jnp.int32, (size, size), 0) % rows // frames_here
    key_spot = lax.broadcasted_iota(jnp.int32, (size, size), 1) % rows // frames_here
    same_spot = query_spot == key_spot
    for part in range(parts):
        queries, keys, values = (
            jnp.concatenate([piece[which, part] for piece in piece_refs], axis=0) for which in range(3)
        )
        scores = lax.dot_general(
            queries, keys, (((1,), (1,)), ((), ())), preferred_element_type=jnp.float32
        )
        scores = jnp.where(same_spot, scores, -jnp.inf)
        weights = jnp.exp((scores - jnp.max(scores, axis=1, keepdims=True)) * scale)
        totals = jnp.sum(weights, axis=1, keepdims=True)
        gathered = jnp.dot(weights.astype(jnp.bfloat16), values, preferred_element_type=jnp.float32)
        gathered = (gathered / totals).astype(out_ref.dtype)
        for piece in range(len(piece_refs)):
            out_ref[piece, part] = gathered[piece * rows : (piece + 1) * rows]


def attend_frames(frames_here, pieces):
    _, parts, rows, width = pieces[0].shape
    count = len(pieces)
    return pl.pallas_call(
        functools.partial(frame_kernel, frames_here),
        grid=(width // HEAD_DIM,),
        in_specs=[pl.BlockSpec((3, parts, rows, HEAD_DIM), lambda h: (0, 0, 0, h)) for _ in pieces],
        out_specs=pl.BlockSpec((count, parts, rows, HEAD_DIM), lambda h: (0, 0, 0, h)),
        out_shape=jax.ShapeDtypeStruct((count, parts, rows, width), jnp.bfloat16),
        compiler_params=pltpu.CompilerParams(vmem_limit_bytes=VMEM_BYTES),
        cost_estimate=pl.CostEstimate(
            flops=16 * parts * (count * rows) ** 2 * width,
            bytes_accessed=8 * count * parts * rows * width,
            transcendentals=parts * (count * rows) ** 2 * width // HEAD_DIM,
        ),
    )(*pieces)


def local(bank_query, char_bank, char_slots, slot_live, frame_tokens, out_weight):
    spatial, frames_here, width = bank_query.shape
    heads_here = width // HEAD_DIM
    head_groups = lax.axis_size("heads")
    shards = lax.axis_size("frames")
    half = shards // 2
    place = lax.axis_index("frames")
    parts = max(1, spatial * frames_here // (TILE_ROWS * shards))
    across = shards // head_groups
    spots = spatial // (shards * parts)
    tile = spots * frames_here
    rows = shards * tile

    def swap(block, step):
        return lax.ppermute(block, "frames", [(a, a ^ step) for a in range(shards)])

    def by_part(block):
        cut = block.reshape(head_groups, parts, across, spots, frames_here, width)
        return jnp.moveaxis(cut, 1, 0).reshape(parts * rows, width)

    own = by_part(bank_query)
    far = swap(own, half)

    def positions_of(shard):
        cut = frame_tokens.reshape(3, head_groups, parts, across, spots, frames_here, width)
        cut = lax.dynamic_slice_in_dim(cut, shard // across, 1, 1)
        cut = lax.dynamic_slice_in_dim(cut, shard % across, 1, 3)
        return cut.reshape(3, parts, tile, width)

    groups = HEAD_GROUPS if heads_here % HEAD_GROUPS == 0 else 1
    group_width = width // groups

    def listed(shard, group):
        ids = [char_slots[shard ^ flip, slot] for flip in (0, half) for slot in range(2)]
        size = (2, 1, char_bank.shape[2], group_width)
        return jnp.concatenate(
            [lax.dynamic_slice(char_bank, (0, i, 0, group * group_width), size) for i in ids], axis=1
        )

    def banks_of(group, before):
        banks = [listed(place, group)] + [
            swap(after(listed(place ^ step, group), *before), step) for step in range(1, half)
        ]
        return banks if char_bank.shape[2] % TILE_ROWS == 0 else [jnp.concatenate(banks, axis=2)]

    def send_tokens(step, *before):
        token_blocks[step] = swap(after(positions_of(place ^ step), *before), step)

    banks = [banks_of(0, ())]
    token_blocks = {0: positions_of(place)}
    for number, step in enumerate(range(half, shards)):
        send_tokens(step, *(banks[0][min(number, len(banks[0]) - 1) :][:1] if number else ()))
    for step in range(1, half):
        send_tokens(step, token_blocks[half + step - 1])
    for group in range(1, groups):
        banks.append(banks_of(group, [token_blocks[shards - 1]]))
    frame_parts = attend_frames(frames_here, [token_blocks[step] for step in range(shards)])
    live = jnp.stack([slot_live[place], slot_live[place ^ half]])

    back = jnp.stack([frame_parts[0]] + [swap(frame_parts[step], step) for step in range(1, shards)])
    back = back[jnp.arange(shards) ^ place]

    def scatter_heads(block):
        place_heads = lax.axis_index("heads")
        chips, core, chip = head_groups // 2, place_heads % 2, place_heads // 2
        block = block.reshape(chips, 2, -1, block.shape[-1])
        give = lax.dynamic_index_in_dim(block, 1 - core, 1, keepdims=False)
        keep = lax.dynamic_index_in_dim(block, core, 1, keepdims=False)
        got = lax.ppermute(give, "heads", [(h, h ^ 1) for h in range(head_groups)])
        summed = added(keep, got)
        parcels = [lax.dynamic_index_in_dim(summed, chip, 0, keepdims=False)]
        for step in range(1, chips):
            give = lax.dynamic_index_in_dim(summed, (chip + step) % chips, 0, keepdims=False)
            parcels.append(
                lax.ppermute(give, "heads", [(h, (h + 2 * step) % head_groups) for h in range(head_groups)])
            )
        return added(*parcels)

    live = after(live, token_blocks[half])
    split = (heads_here // groups, HEAD_DIM, rows)
    shared = [[] for _ in range(parts)]
    for group in range(groups):
        near_out, near_level, far_out, far_level = attend_bank(group, parts, rows, live, own, far, banks[group])
        got_level = swap(far_level, half)
        if group < groups - 1:
            got_out = swap(far_out, half)
        else:
            got_out = [swap(far_out[part], half) for part in range(parts)]
        peak = jnp.maximum(near_level, got_level)
        near_share, got_share = jnp.exp(near_level - peak), jnp.exp(got_level - peak)
        total = near_share + got_share
        near_share, got_share = near_share / total, got_share / total
        for part in range(parts):
            shared[part].append(
                wide(near_out[part].reshape(split)) * near_share[part][:, None, :]
                + wide(got_out[part].reshape(split)) * got_share[part][:, None, :]
            )
    pieces = []
    for part in range(parts):
        ref_out = jnp.concatenate(shared[part], axis=0).reshape(width, rows)
        frame_out = back[:, part].reshape(rows, width)
        combined = (ref_out + wide(frame_out.T)).astype(jnp.bfloat16)
        projected = lax.dot_general(
            combined, out_weight, (((0,), (0,)), ((), ())), preferred_element_type=jnp.float32
        ).astype(jnp.bfloat16)
        pieces.append(scatter_heads(projected))
    return jnp.concatenate(pieces, axis=0).reshape(spatial // head_groups, frames_here, -1)


def solution(mesh):
    in_specs = (
        P(None, "frames", "heads"),
        P(None, None, "frames", "heads"),
        P(),
        P(),
        P(None, None, "frames", "heads"),
        P("heads", None),
    )
    out_specs = P("heads", "frames", None)
    return jax.shard_map(local, mesh=mesh, in_specs=in_specs, out_specs=out_specs, check_vma=False)
```

```python
import functools

import jax
import jax.numpy as jnp
from jax import lax
from jax.experimental import pallas as pl
from jax.experimental.pallas import tpu as pltpu
from jax.sharding import PartitionSpec as P

HEAD_DIM = 128
TILE_ROWS = 16
HEAD_GROUPS = 2
VMEM_BYTES = 48 * 1024 * 1024


def after(block, *before):
    return lax.optimization_barrier((block, *before))[0] if before else block


def wide(block):
    return block.astype(jnp.float32)


def added(*blocks):
    return functools.reduce(jnp.add, [wide(block) for block in blocks]).astype(jnp.bfloat16)


def attend_columns(keys, values, queries, allowed):
    scale = HEAD_DIM ** (-0.5)
    scores = lax.dot_general(
        keys, queries, (((1,), (1,)), ((), ())), preferred_element_type=jnp.float32
    )
    scores = jnp.where(allowed, scores, -jnp.inf)
    peak = jnp.max(scores, axis=0, keepdims=True)
    weights = jnp.exp((scores - peak) * scale)
    totals = jnp.sum(weights, axis=0, keepdims=True)
    gathered = lax.dot_general(
        values, weights.astype(jnp.bfloat16), (((0,), (0,)), ((), ())),
        preferred_element_type=jnp.float32,
    )
    return gathered * (1.0 / totals), peak * scale + jnp.log(totals)


def bank_kernel(banks, live_ref, own_ref, far_ref, *refs):
    bank_refs = refs[:banks]
    head = pl.program_id(0)
    tokens = sum(bank.shape[2] for bank in bank_refs)
    second = lax.broadcasted_iota(jnp.int32, (2 * tokens, own_ref.shape[0]), 0) >= tokens
    for side, query_ref in enumerate((own_ref, far_ref)):
        out_ref, level_ref = refs[banks + 2 * side : banks + 2 * side + 2]
        keys, values = (
            jnp.concatenate([bank[which, 2 * side + slot] for slot in range(2) for bank in bank_refs], axis=0)
            for which in range(2)
        )
        allowed = jnp.logical_or(jnp.logical_not(second), live_ref[side, 1] > 0)
        gathered, level = attend_columns(keys, values, query_ref[...], allowed)
        rows = out_ref.shape[2]
        for part in range(out_ref.shape[0]):
            here = slice(part * rows, (part + 1) * rows)
            out_ref[part] = gathered[:, here].astype(out_ref.dtype)
            level_ref[part, pl.ds(head, 1), :] = level[:, here]


def attend_bank(group, parts, rows, live, own, far, banks):
    width = banks[0].shape[3]
    heads = width // HEAD_DIM
    keys_each = 2 * sum(bank.shape[2] for bank in banks)
    query_spec = pl.BlockSpec((parts * rows, HEAD_DIM), lambda h: (0, group * heads + h))
    out = jax.ShapeDtypeStruct((parts, width, rows), jnp.bfloat16)
    level = jax.ShapeDtypeStruct((parts, heads, rows), jnp.float32)
    out_spec = pl.BlockSpec((parts, HEAD_DIM, rows), lambda h: (0, h, 0))
    level_spec = pl.BlockSpec((parts, heads, rows), lambda h: (0, 0, 0))
    return pl.pallas_call(
        functools.partial(bank_kernel, len(banks)),
        grid=(heads,),
        in_specs=[pl.BlockSpec(memory_space=pltpu.SMEM), query_spec, query_spec]
        + [pl.BlockSpec((*bank.shape[:3], HEAD_DIM), lambda h: (0, 0, 0, h)) for bank in banks],
        out_specs=[out_spec, level_spec] * 2,
        out_shape=[out, level] * 2,
        compiler_params=pltpu.CompilerParams(vmem_limit_bytes=VMEM_BYTES),
        cost_estimate=pl.CostEstimate(
            flops=32 * parts * rows * width * keys_each,
            bytes_accessed=2 * (4 * parts * rows * width + sum(bank.size for bank in banks)),
            transcendentals=2 * parts * rows * heads * keys_each,
        ),
    )(live, own, far, *banks)


def frame_kernel(frames_here, token_ref, out_ref):
    scale = HEAD_DIM ** (-0.5)
    pieces, _, parts, rows, _ = token_ref.shape
    size = pieces * rows
    query_spot = lax.broadcasted_iota(jnp.int32, (size, size), 0) % rows // frames_here
    key_spot = lax.broadcasted_iota(jnp.int32, (size, size), 1) % rows // frames_here
    same_spot = query_spot == key_spot
    for part in range(parts):
        queries, keys, values = (
            jnp.concatenate([token_ref[piece, which, part] for piece in range(pieces)], axis=0)
            for which in range(3)
        )
        scores = lax.dot_general(
            queries, keys, (((1,), (1,)), ((), ())), preferred_element_type=jnp.float32
        )
        scores = jnp.where(same_spot, scores, -jnp.inf)
        weights = jnp.exp((scores - jnp.max(scores, axis=1, keepdims=True)) * scale)
        totals = jnp.sum(weights, axis=1, keepdims=True)
        gathered = jnp.dot(weights.astype(jnp.bfloat16), values, preferred_element_type=jnp.float32)
        gathered = (gathered / totals).astype(out_ref.dtype)
        for piece in range(pieces):
            out_ref[piece, part] = gathered[piece * rows : (piece + 1) * rows]


def attend_frames(frames_here, tokens):
    pieces, _, parts, rows, width = tokens.shape
    return pl.pallas_call(
        functools.partial(frame_kernel, frames_here),
        grid=(width // HEAD_DIM,),
        in_specs=[pl.BlockSpec((pieces, 3, parts, rows, HEAD_DIM), lambda h: (0, 0, 0, 0, h))],
        out_specs=pl.BlockSpec((pieces, parts, rows, HEAD_DIM), lambda h: (0, 0, 0, h)),
        out_shape=jax.ShapeDtypeStruct((pieces, parts, rows, width), jnp.bfloat16),
        compiler_params=pltpu.CompilerParams(vmem_limit_bytes=VMEM_BYTES),
        cost_estimate=pl.CostEstimate(
            flops=16 * parts * (pieces * rows) ** 2 * width,
            bytes_accessed=8 * pieces * parts * rows * width,
            transcendentals=parts * (pieces * rows) ** 2 * width // HEAD_DIM,
        ),
    )(tokens)


def listed_kernel(place_ref, slots_ref, *refs):
    count = len(refs) // 2
    for source, target in zip(refs[:count], refs[count:]):
        target[...] = source[...]


def listed_banks(place, char_slots, char_bank, half, group, group_width):
    _, _, tokens, _ = char_bank.shape
    block = (2, 1, tokens, group_width)

    def source(step):
        def index(entry, place_ref, slots_ref):
            shard = place_ref[0] ^ step ^ (entry // 2 * half)
            return 0, slots_ref[shard * 2 + entry % 2], 0, group

        return pl.BlockSpec(block, index)

    return pl.pallas_call(
        listed_kernel,
        grid_spec=pltpu.PrefetchScalarGridSpec(
            num_scalar_prefetch=2,
            grid=(4,),
            in_specs=[source(step) for step in range(half)],
            out_specs=[pl.BlockSpec(block, lambda entry, *_: (0, entry, 0, 0)) for _ in range(half)],
        ),
        out_shape=[jax.ShapeDtypeStruct((2, 4, tokens, group_width), char_bank.dtype) for _ in range(half)],
        compiler_params=pltpu.CompilerParams(vmem_limit_bytes=VMEM_BYTES),
        cost_estimate=pl.CostEstimate(
            flops=0, bytes_accessed=32 * half * tokens * group_width, transcendentals=0
        ),
    )(place.reshape(1), char_slots.reshape(-1), *[char_bank] * half)


def local(bank_query, char_bank, char_slots, slot_live, frame_tokens, out_weight):
    spatial, frames_here, width = bank_query.shape
    heads_here = width // HEAD_DIM
    head_groups = lax.axis_size("heads")
    shards = lax.axis_size("frames")
    half = shards // 2
    place = lax.axis_index("frames")
    parts = max(1, spatial * frames_here // (TILE_ROWS * shards))
    across = shards // head_groups
    spots = spatial // (shards * parts)
    tile = spots * frames_here
    rows = shards * tile

    def swap(block, step):
        return lax.ppermute(block, "frames", [(a, a ^ step) for a in range(shards)])

    def by_part(block):
        cut = block.reshape(head_groups, parts, across, spots, frames_here, width)
        return jnp.moveaxis(cut, 1, 0).reshape(parts * rows, width)

    own = by_part(bank_query)
    far = swap(own, half)

    groups = HEAD_GROUPS if heads_here % HEAD_GROUPS == 0 else 1

    def banks_of(group, *before):
        blocks = listed_banks(
            place, after(char_slots, *before), char_bank, half, group, width // groups
        )
        blocks = [blocks[0]] + [swap(blocks[step], step) for step in range(1, half)]
        return blocks if char_bank.shape[2] % TILE_ROWS == 0 else [jnp.concatenate(blocks, axis=2)]

    banks = [banks_of(0)]
    tokens = frame_tokens.reshape(3, head_groups, parts, across, spots, frames_here, width)
    tokens = tokens.transpose(1, 3, 0, 2, 4, 5, 6).reshape(shards, 3, parts, tile, width)
    tokens = lax.all_to_all(tokens, "frames", split_axis=0, concat_axis=0, tiled=True)
    live = jnp.stack([slot_live[place], slot_live[place ^ half]])

    def scatter_heads(block):
        place_heads = lax.axis_index("heads")
        chips, core, chip = head_groups // 2, place_heads % 2, place_heads // 2
        block = block.reshape(chips, 2, -1, block.shape[-1])
        give = lax.dynamic_index_in_dim(block, 1 - core, 1, keepdims=False)
        keep = lax.dynamic_index_in_dim(block, core, 1, keepdims=False)
        got = lax.ppermute(give, "heads", [(h, h ^ 1) for h in range(head_groups)])
        summed = added(keep, got)
        parcels = [lax.dynamic_index_in_dim(summed, chip, 0, keepdims=False)]
        for step in range(1, chips):
            give = lax.dynamic_index_in_dim(summed, (chip + step) % chips, 0, keepdims=False)
            parcels.append(
                lax.ppermute(give, "heads", [(h, (h + 2 * step) % head_groups) for h in range(head_groups)])
            )
        return added(*parcels)

    split = (heads_here // groups, HEAD_DIM, rows)
    shared = [[] for _ in range(parts)]
    for group in range(groups):
        near_out, near_level, far_out, far_level = attend_bank(group, parts, rows, live, own, far, banks[group])
        if group < groups - 1:
            banks.append(banks_of(group + 1, far_level))
        if group == 0:
            frame_parts = attend_frames(frames_here, after(tokens, far_level))
            back = lax.all_to_all(frame_parts, "frames", split_axis=0, concat_axis=0, tiled=True)
        got_level = swap(far_level, half)
        if group < groups - 1:
            got_out = swap(far_out, half)
        else:
            got_out = [swap(far_out[part], half) for part in range(parts)]
        peak = jnp.maximum(near_level, got_level)
        near_share, got_share = jnp.exp(near_level - peak), jnp.exp(got_level - peak)
        total = near_share + got_share
        near_share, got_share = near_share / total, got_share / total
        for part in range(parts):
            shared[part].append(
                wide(near_out[part].reshape(split)) * near_share[part][:, None, :]
                + wide(got_out[part].reshape(split)) * got_share[part][:, None, :]
            )
    pieces = []
    for part in range(parts):
        ref_out = jnp.concatenate(shared[part], axis=0).reshape(width, rows)
        frame_out = back[:, part].reshape(rows, width)
        combined = (ref_out + wide(frame_out.T)).astype(jnp.bfloat16)
        projected = lax.dot_general(
            combined, out_weight, (((0,), (0,)), ((), ())), preferred_element_type=jnp.float32
        ).astype(jnp.bfloat16)
        pieces.append(scatter_heads(projected))
    return jnp.concatenate(pieces, axis=0).reshape(spatial // head_groups, frames_here, -1)


def solution(mesh):
    in_specs = (
        P(None, "frames", "heads"),
        P(None, None, "frames", "heads"),
        P(),
        P(),
        P(None, None, "frames", "heads"),
        P("heads", None),
    )
    out_specs = P("heads", "frames", None)
    return jax.shard_map(local, mesh=mesh, in_specs=in_specs, out_specs=out_specs, check_vma=False)
```

```python
import functools

import jax
import jax.numpy as jnp
from jax import lax
from jax.experimental import pallas as pl
from jax.experimental.pallas import tpu as pltpu
from jax.sharding import PartitionSpec as P

HEAD_DIM = 128
TILE_ROWS = 16
HEAD_GROUPS = 2
VMEM_BYTES = 48 * 1024 * 1024


def after(block, *before):
    return lax.optimization_barrier((block, *before))[0] if before else block


def wide(block):
    return block.astype(jnp.float32)


def added(*blocks):
    return functools.reduce(jnp.add, [wide(block) for block in blocks]).astype(jnp.bfloat16)


def attend_columns(keys, values, queries, allowed):
    scale = HEAD_DIM ** (-0.5)
    scores = lax.dot_general(
        keys, queries, (((1,), (1,)), ((), ())), preferred_element_type=jnp.float32
    )
    scores = jnp.where(allowed, scores, -jnp.inf)
    peak = jnp.max(scores, axis=0, keepdims=True)
    weights = jnp.exp((scores - peak) * scale)
    totals = jnp.sum(weights, axis=0, keepdims=True)
    gathered = lax.dot_general(
        values, weights.astype(jnp.bfloat16), (((0,), (0,)), ((), ())),
        preferred_element_type=jnp.float32,
    )
    return gathered * (1.0 / totals), peak * scale + jnp.log(totals)


def bank_kernel(banks, live_ref, own_ref, far_ref, *refs):
    bank_refs = refs[:banks]
    head = pl.program_id(0)
    tokens = sum(bank.shape[2] for bank in bank_refs)
    second = lax.broadcasted_iota(jnp.int32, (2 * tokens, own_ref.shape[0]), 0) >= tokens
    for side, query_ref in enumerate((own_ref, far_ref)):
        out_ref, level_ref = refs[banks + 2 * side : banks + 2 * side + 2]
        keys, values = (
            jnp.concatenate([bank[which, 2 * side + slot] for slot in range(2) for bank in bank_refs], axis=0)
            for which in range(2)
        )
        allowed = jnp.logical_or(jnp.logical_not(second), live_ref[side, 1] > 0)
        gathered, level = attend_columns(keys, values, query_ref[...], allowed)
        rows = out_ref.shape[2]
        for part in range(out_ref.shape[0]):
            here = slice(part * rows, (part + 1) * rows)
            out_ref[part] = gathered[:, here].astype(out_ref.dtype)
            level_ref[part, pl.ds(head, 1), :] = level[:, here]


def attend_bank(group, parts, rows, live, own, far, banks):
    width = banks[0].shape[3]
    heads = width // HEAD_DIM
    keys_each = 2 * sum(bank.shape[2] for bank in banks)
    query_spec = pl.BlockSpec((parts * rows, HEAD_DIM), lambda h: (0, group * heads + h))
    out = jax.ShapeDtypeStruct((parts, width, rows), jnp.bfloat16)
    level = jax.ShapeDtypeStruct((parts, heads, rows), jnp.float32)
    out_spec = pl.BlockSpec((parts, HEAD_DIM, rows), lambda h: (0, h, 0))
    level_spec = pl.BlockSpec((parts, heads, rows), lambda h: (0, 0, 0))
    return pl.pallas_call(
        functools.partial(bank_kernel, len(banks)),
        grid=(heads,),
        in_specs=[pl.BlockSpec(memory_space=pltpu.SMEM), query_spec, query_spec]
        + [pl.BlockSpec((*bank.shape[:3], HEAD_DIM), lambda h: (0, 0, 0, h)) for bank in banks],
        out_specs=[out_spec, level_spec] * 2,
        out_shape=[out, level] * 2,
        compiler_params=pltpu.CompilerParams(vmem_limit_bytes=VMEM_BYTES),
        cost_estimate=pl.CostEstimate(
            flops=32 * parts * rows * width * keys_each,
            bytes_accessed=2 * (4 * parts * rows * width + sum(bank.size for bank in banks)),
            transcendentals=2 * parts * rows * heads * keys_each,
        ),
    )(live, own, far, *banks)


def frame_kernel(frames_here, token_ref, out_ref):
    scale = HEAD_DIM ** (-0.5)
    pieces, _, parts, rows, _ = token_ref.shape
    size = pieces * rows
    query_spot = lax.broadcasted_iota(jnp.int32, (size, size), 0) % rows // frames_here
    key_spot = lax.broadcasted_iota(jnp.int32, (size, size), 1) % rows // frames_here
    same_spot = query_spot == key_spot
    for part in range(parts):
        queries, keys, values = (
            jnp.concatenate([token_ref[piece, which, part] for piece in range(pieces)], axis=0)
            for which in range(3)
        )
        scores = lax.dot_general(
            queries, keys, (((1,), (1,)), ((), ())), preferred_element_type=jnp.float32
        )
        scores = jnp.where(same_spot, scores, -jnp.inf)
        weights = jnp.exp((scores - jnp.max(scores, axis=1, keepdims=True)) * scale)
        totals = jnp.sum(weights, axis=1, keepdims=True)
        gathered = jnp.dot(weights.astype(jnp.bfloat16), values, preferred_element_type=jnp.float32)
        gathered = (gathered / totals).astype(out_ref.dtype)
        for piece in range(pieces):
            out_ref[piece, part] = gathered[piece * rows : (piece + 1) * rows]


def attend_frames(frames_here, tokens):
    pieces, _, parts, rows, width = tokens.shape
    return pl.pallas_call(
        functools.partial(frame_kernel, frames_here),
        grid=(width // HEAD_DIM,),
        in_specs=[pl.BlockSpec((pieces, 3, parts, rows, HEAD_DIM), lambda h: (0, 0, 0, 0, h))],
        out_specs=pl.BlockSpec((pieces, parts, rows, HEAD_DIM), lambda h: (0, 0, 0, h)),
        out_shape=jax.ShapeDtypeStruct((pieces, parts, rows, width), jnp.bfloat16),
        compiler_params=pltpu.CompilerParams(vmem_limit_bytes=VMEM_BYTES),
        cost_estimate=pl.CostEstimate(
            flops=16 * parts * (pieces * rows) ** 2 * width,
            bytes_accessed=8 * pieces * parts * rows * width,
            transcendentals=parts * (pieces * rows) ** 2 * width // HEAD_DIM,
        ),
    )(tokens)


def listed_kernel(place_ref, slots_ref, *refs):
    count = len(refs) // 2
    for source, target in zip(refs[:count], refs[count:]):
        target[...] = source[...]


def listed_banks(place, char_slots, char_bank, half, group, group_width):
    _, _, tokens, _ = char_bank.shape
    block = (2, 1, tokens, group_width)

    def source(step):
        def index(entry, place_ref, slots_ref):
            shard = place_ref[0] ^ step ^ (entry // 2 * half)
            return 0, slots_ref[shard * 2 + entry % 2], 0, group

        return pl.BlockSpec(block, index)

    return pl.pallas_call(
        listed_kernel,
        grid_spec=pltpu.PrefetchScalarGridSpec(
            num_scalar_prefetch=2,
            grid=(4,),
            in_specs=[source(step) for step in range(half)],
            out_specs=[pl.BlockSpec(block, lambda entry, *_: (0, entry, 0, 0)) for _ in range(half)],
        ),
        out_shape=[jax.ShapeDtypeStruct((2, 4, tokens, group_width), char_bank.dtype) for _ in range(half)],
        compiler_params=pltpu.CompilerParams(vmem_limit_bytes=VMEM_BYTES),
        cost_estimate=pl.CostEstimate(
            flops=0, bytes_accessed=32 * half * tokens * group_width, transcendentals=0
        ),
    )(place.reshape(1), char_slots.reshape(-1), *[char_bank] * half)


def local(bank_query, char_bank, char_slots, slot_live, frame_tokens, out_weight):
    spatial, frames_here, width = bank_query.shape
    heads_here = width // HEAD_DIM
    head_groups = lax.axis_size("heads")
    shards = lax.axis_size("frames")
    half = shards // 2
    place = lax.axis_index("frames")
    parts = max(1, spatial * frames_here // (TILE_ROWS * shards))
    across = shards // head_groups
    spots = spatial // (shards * parts)
    tile = spots * frames_here
    rows = shards * tile

    def swap(block, step):
        return lax.ppermute(block, "frames", [(a, a ^ step) for a in range(shards)])

    def by_part(block):
        cut = block.reshape(head_groups, parts, across, spots, frames_here, width)
        return jnp.moveaxis(cut, 1, 0).reshape(parts * rows, width)

    own = by_part(bank_query)
    far = swap(own, half)

    groups = HEAD_GROUPS if heads_here % HEAD_GROUPS == 0 else 1

    def banks_of(group, *before):
        blocks = listed_banks(
            place, after(char_slots, *before), char_bank, half, group, width // groups
        )
        blocks = [blocks[0]] + [swap(blocks[step], step) for step in range(1, half)]
        return blocks if char_bank.shape[2] % TILE_ROWS == 0 else [jnp.concatenate(blocks, axis=2)]

    banks = [banks_of(0)]
    tokens = frame_tokens.reshape(3, head_groups, parts, across, spots, frames_here, width)
    tokens = tokens.transpose(1, 3, 0, 2, 4, 5, 6).reshape(shards, 3, parts, tile, width)
    tokens = lax.all_to_all(after(tokens, banks[0][-1 if len(banks[0]) == 1 else 1]), "frames", 0, 0, tiled=True)
    live = jnp.stack([slot_live[place], slot_live[place ^ half]])

    place_heads = lax.axis_index("heads")
    chips, core, chip = head_groups // 2, place_heads % 2, place_heads // 2

    def scatter_cores(block):
        block = block.reshape(chips, 2, -1, block.shape[-1])
        give = lax.dynamic_index_in_dim(block, 1 - core, 1, keepdims=False)
        keep = lax.dynamic_index_in_dim(block, core, 1, keepdims=False)
        return added(keep, lax.ppermute(give, "heads", [(h, h ^ 1) for h in range(head_groups)]))

    def scatter_chips(summed):
        parcels = [lax.dynamic_index_in_dim(summed, chip, 0, keepdims=False)]
        for step in range(1, chips):
            give = lax.dynamic_index_in_dim(summed, (chip + step) % chips, 0, keepdims=False)
            parcels.append(
                lax.ppermute(give, "heads", [(h, (h + 2 * step) % head_groups) for h in range(head_groups)])
            )
        return added(*parcels)

    split = (heads_here // groups, HEAD_DIM, rows)
    shared = [[] for _ in range(parts)]
    for group in range(groups):
        near_out, near_level, far_out, far_level = attend_bank(group, parts, rows, live, own, far, banks[group])
        if group < groups - 1:
            banks.append(banks_of(group + 1, far_level))
        if group == 0:
            frame_parts = attend_frames(frames_here, after(tokens, far_level))
            live = after(live, frame_parts)
            back = lax.all_to_all(frame_parts, "frames", 0, 0, tiled=True)
        got_level = swap(far_level, half)
        if group < groups - 1:
            got_out = swap(far_out, half)
        else:
            got_out = [swap(far_out[part], half) for part in range(parts)]
        peak = jnp.maximum(near_level, got_level)
        near_share, got_share = jnp.exp(near_level - peak), jnp.exp(got_level - peak)
        total = near_share + got_share
        near_share, got_share = near_share / total, got_share / total
        for part in range(parts):
            shared[part].append(
                wide(near_out[part].reshape(split)) * near_share[part][:, None, :]
                + wide(got_out[part].reshape(split)) * got_share[part][:, None, :]
            )
    summed = []
    for part in range(parts):
        ref_out = jnp.concatenate(shared[part], axis=0).reshape(width, rows)
        frame_out = back[:, part].reshape(rows, width)
        combined = (ref_out + wide(frame_out.T)).astype(jnp.bfloat16)
        combined = after(combined, *summed[max(part - 2, 0) : max(part - 1, 0)])
        projected = lax.dot_general(
            combined, out_weight, (((0,), (0,)), ((), ())), preferred_element_type=jnp.float32
        ).astype(jnp.bfloat16)
        summed.append(scatter_cores(projected))
    pieces = [scatter_chips(block) for block in summed]
    return jnp.concatenate(pieces, axis=0).reshape(spatial // head_groups, frames_here, -1)


def solution(mesh):
    in_specs = (
        P(None, "frames", "heads"),
        P(None, None, "frames", "heads"),
        P(),
        P(),
        P(None, None, "frames", "heads"),
        P("heads", None),
    )
    out_specs = P("heads", "frames", None)
    return jax.shard_map(local, mesh=mesh, in_specs=in_specs, out_specs=out_specs, check_vma=False)
```

```python
import functools

import jax
import jax.numpy as jnp
from jax import lax
from jax.experimental import pallas as pl
from jax.experimental.pallas import tpu as pltpu
from jax.sharding import PartitionSpec as P

HEAD_DIM = 128
TILE_ROWS = 16
HEAD_GROUPS = 2
VMEM_BYTES = 24 * 1024 * 1024


def after(block, *before):
    return lax.optimization_barrier((block, *before))[0] if before else block


def wide(block):
    return block.astype(jnp.float32)


def added(*blocks):
    return functools.reduce(jnp.add, [wide(block) for block in blocks]).astype(jnp.bfloat16)


def in_three(block):
    terms = []
    for _ in range(3):
        term = lax.reduce_precision(block, 8, 7)
        terms.append(term.astype(jnp.bfloat16))
        block = block - term
    return terms


def attend_columns(keys, values, queries, allowed):
    scale = HEAD_DIM ** (-0.5)
    scores = lax.dot_general(
        keys, queries, (((1,), (1,)), ((), ())), preferred_element_type=jnp.float32
    )
    scores = jnp.where(allowed, scores, -jnp.inf)
    peak = jnp.max(scores, axis=0, keepdims=True)
    weights = jnp.exp((scores - peak) * scale)
    totals = jnp.sum(weights, axis=0, keepdims=True)
    gathered = lax.dot_general(
        values, weights.astype(jnp.bfloat16), (((0,), (0,)), ((), ())),
        preferred_element_type=jnp.float32,
    )
    return gathered * (1.0 / totals), peak * scale + jnp.log(totals)


def bank_kernel(banks, live_ref, own_ref, far_ref, *refs):
    bank_refs = refs[:banks]
    head = pl.program_id(0)
    tokens = sum(bank.shape[2] for bank in bank_refs)
    second = lax.broadcasted_iota(jnp.int32, (2 * tokens, own_ref.shape[0]), 0) >= tokens
    for side, query_ref in enumerate((own_ref, far_ref)):
        out_ref, level_ref = refs[banks + 2 * side : banks + 2 * side + 2]
        keys, values = (
            jnp.concatenate([bank[which, 2 * side + slot] for slot in range(2) for bank in bank_refs], axis=0)
            for which in range(2)
        )
        allowed = jnp.logical_or(jnp.logical_not(second), live_ref[side, 1] > 0)
        gathered, level = attend_columns(keys, values, query_ref[...], allowed)
        rows = out_ref.shape[2]
        for part in range(out_ref.shape[0]):
            here = slice(part * rows, (part + 1) * rows)
            out_ref[part] = gathered[:, here].astype(out_ref.dtype)
            level_ref[part, pl.ds(head, 1), :] = level[:, here]


def attend_bank(group, parts, rows, live, own, far, banks):
    width = banks[0].shape[3]
    heads = width // HEAD_DIM
    keys_each = 2 * sum(bank.shape[2] for bank in banks)
    query_spec = pl.BlockSpec((parts * rows, HEAD_DIM), lambda h: (0, group * heads + h))
    out = jax.ShapeDtypeStruct((parts, width, rows), jnp.bfloat16)
    level = jax.ShapeDtypeStruct((parts, heads, rows), jnp.float32)
    out_spec = pl.BlockSpec((parts, HEAD_DIM, rows), lambda h: (0, h, 0))
    level_spec = pl.BlockSpec((parts, heads, rows), lambda h: (0, 0, 0))
    return pl.pallas_call(
        functools.partial(bank_kernel, len(banks)),
        grid=(heads,),
        in_specs=[pl.BlockSpec(memory_space=pltpu.SMEM), query_spec, query_spec]
        + [pl.BlockSpec((*bank.shape[:3], HEAD_DIM), lambda h: (0, 0, 0, h)) for bank in banks],
        out_specs=[out_spec, level_spec] * 2,
        out_shape=[out, level] * 2,
        compiler_params=pltpu.CompilerParams(vmem_limit_bytes=VMEM_BYTES),
        cost_estimate=pl.CostEstimate(
            flops=32 * parts * rows * width * keys_each,
            bytes_accessed=2 * (4 * parts * rows * width + sum(bank.size for bank in banks)),
            transcendentals=2 * parts * rows * heads * keys_each,
        ),
    )(live, own, far, *banks)


def frame_kernel(frames_here, token_ref, out_ref):
    scale = HEAD_DIM ** (-0.5)
    pieces, _, parts, rows, _ = token_ref.shape
    size = pieces * rows
    query_spot = lax.broadcasted_iota(jnp.int32, (size, size), 0) % rows // frames_here
    key_spot = lax.broadcasted_iota(jnp.int32, (size, size), 1) % rows // frames_here
    same_spot = query_spot == key_spot
    for part in range(parts):
        queries, keys, values = (
            jnp.concatenate([token_ref[piece, which, part] for piece in range(pieces)], axis=0)
            for which in range(3)
        )
        scores = lax.dot_general(
            queries, keys, (((1,), (1,)), ((), ())), preferred_element_type=jnp.float32
        )
        scores = jnp.where(same_spot, scores, -jnp.inf)
        weights = jnp.exp((scores - jnp.max(scores, axis=1, keepdims=True)) * scale)
        totals = jnp.sum(weights, axis=1, keepdims=True)
        gathered = jnp.dot(weights.astype(jnp.bfloat16), values, preferred_element_type=jnp.float32)
        gathered = (gathered / totals).astype(out_ref.dtype)
        for piece in range(pieces):
            out_ref[piece, part] = gathered[piece * rows : (piece + 1) * rows]


def attend_frames(frames_here, tokens):
    pieces, _, parts, rows, width = tokens.shape
    return pl.pallas_call(
        functools.partial(frame_kernel, frames_here),
        grid=(width // HEAD_DIM,),
        in_specs=[pl.BlockSpec((pieces, 3, parts, rows, HEAD_DIM), lambda h: (0, 0, 0, 0, h))],
        out_specs=pl.BlockSpec((pieces, parts, rows, HEAD_DIM), lambda h: (0, 0, 0, h)),
        out_shape=jax.ShapeDtypeStruct((pieces, parts, rows, width), jnp.bfloat16),
        compiler_params=pltpu.CompilerParams(vmem_limit_bytes=VMEM_BYTES),
        cost_estimate=pl.CostEstimate(
            flops=16 * parts * (pieces * rows) ** 2 * width,
            bytes_accessed=8 * pieces * parts * rows * width,
            transcendentals=parts * (pieces * rows) ** 2 * width // HEAD_DIM,
        ),
    )(tokens)


def listed_kernel(place_ref, slots_ref, *refs):
    count = len(refs) // 2
    for source, target in zip(refs[:count], refs[count:]):
        target[...] = source[...]


def listed_banks(place, char_slots, char_bank, half, group, group_width):
    _, _, tokens, _ = char_bank.shape
    block = (2, 1, tokens, group_width)

    def source(step):
        def index(entry, place_ref, slots_ref):
            shard = place_ref[0] ^ step ^ (entry // 2 * half)
            return 0, slots_ref[shard * 2 + entry % 2], 0, group

        return pl.BlockSpec(block, index)

    return pl.pallas_call(
        listed_kernel,
        grid_spec=pltpu.PrefetchScalarGridSpec(
            num_scalar_prefetch=2,
            grid=(4,),
            in_specs=[source(step) for step in range(half)],
            out_specs=[pl.BlockSpec(block, lambda entry, *_: (0, entry, 0, 0)) for _ in range(half)],
        ),
        out_shape=[jax.ShapeDtypeStruct((2, 4, tokens, group_width), char_bank.dtype) for _ in range(half)],
        compiler_params=pltpu.CompilerParams(vmem_limit_bytes=VMEM_BYTES),
        cost_estimate=pl.CostEstimate(
            flops=0, bytes_accessed=32 * half * tokens * group_width, transcendentals=0
        ),
    )(place.reshape(1), char_slots.reshape(-1), *[char_bank] * half)


def local(bank_query, char_bank, char_slots, slot_live, frame_tokens, out_weight):
    spatial, frames_here, width = bank_query.shape
    heads_here = width // HEAD_DIM
    head_groups = lax.axis_size("heads")
    shards = lax.axis_size("frames")
    half = shards // 2
    place = lax.axis_index("frames")
    parts = max(1, spatial * frames_here // (TILE_ROWS * shards))
    across = shards // head_groups
    spots = spatial // (shards * parts)
    tile = spots * frames_here
    rows = shards * tile

    def swap(block, step):
        return lax.ppermute(block, "frames", [(a, a ^ step) for a in range(shards)])

    def by_part(block):
        cut = block.reshape(head_groups, parts, across, spots, frames_here, width)
        return jnp.moveaxis(cut, 1, 0).reshape(parts * rows, width)

    own = by_part(bank_query)
    far = swap(own, half)

    groups = HEAD_GROUPS if heads_here % HEAD_GROUPS == 0 else 1

    def banks_of(group, *before):
        blocks = listed_banks(
            place, after(char_slots, *before), char_bank, half, group, width // groups
        )
        blocks = [blocks[0]] + [swap(blocks[step], step) for step in range(1, half)]
        return blocks if char_bank.shape[2] % TILE_ROWS == 0 else [jnp.concatenate(blocks, axis=2)]

    banks = [banks_of(0)]
    tokens = frame_tokens.reshape(3, head_groups, parts, across, spots, frames_here, width)
    tokens = tokens.transpose(1, 3, 0, 2, 4, 5, 6).reshape(shards, 3, parts, tile, width)
    tokens = lax.all_to_all(after(tokens, far), "frames", 0, 0, tiled=True)
    live = jnp.stack([slot_live[place], slot_live[place ^ half]])

    place_heads = lax.axis_index("heads")
    chips, core, chip = head_groups // 2, place_heads % 2, place_heads // 2

    def scatter_cores(block):
        block = block.reshape(chips, 2, -1, block.shape[-1])
        give = lax.dynamic_index_in_dim(block, 1 - core, 1, keepdims=False)
        keep = lax.dynamic_index_in_dim(block, core, 1, keepdims=False)
        return added(keep, lax.ppermute(give, "heads", [(h, h ^ 1) for h in range(head_groups)]))

    def scatter_chips(summed):
        parcels = [lax.dynamic_index_in_dim(summed, chip, 0, keepdims=False)]
        for step in range(1, chips):
            give = lax.dynamic_index_in_dim(summed, (chip + step) % chips, 0, keepdims=False)
            parcels.append(
                lax.ppermute(give, "heads", [(h, (h + 2 * step) % head_groups) for h in range(head_groups)])
            )
        return added(*parcels)

    split = (heads_here // groups, HEAD_DIM, rows)
    results = []
    for group in range(groups):
        near_out, near_level, far_out, far_level = attend_bank(group, parts, rows, live, own, far, banks[group])
        if group < groups - 1:
            banks.append(banks_of(group + 1, far_level))
        if group == 0:
            frame_parts = attend_frames(frames_here, after(tokens, far_level))
            back = lax.all_to_all(frame_parts, "frames", 0, 0, tiled=True)
            live = after(live, frame_parts)
        message = jnp.concatenate([far_out, *in_three(far_level)], axis=1)
        message = jnp.pad(message, ((0, 0), (0, -message.shape[1] % TILE_ROWS), (0, 0)))
        if group < groups - 1:
            got = swap(message, half)
        else:
            got = [swap(message[part], half) for part in range(parts)]
        results.append((near_out, near_level, got))

    def share_of(group, part):
        near_out, near_level, got = results[group]
        got = after(got[part], *([results[-1][1]] if group < groups - 1 else []))
        size = heads_here // groups
        got_level = sum(wide(got[low : low + size]) for low in range(width // groups, width // groups + 3 * size, size))
        peak = jnp.maximum(near_level[part], got_level)
        near_share, got_share = jnp.exp(near_level[part] - peak), jnp.exp(got_level - peak)
        total = near_share + got_share
        return (
            wide(near_out[part].reshape(split)) * (near_share / total)[:, None, :]
            + wide(got[: width // groups].reshape(split)) * (got_share / total)[:, None, :]
        )

    summed = []
    for part in range(parts):
        ref_out = jnp.concatenate([share_of(group, part) for group in range(groups)], axis=0).reshape(width, rows)
        frame_out = back[:, part].reshape(rows, width)
        combined = (ref_out + wide(frame_out.T)).astype(jnp.bfloat16)
        combined = after(combined, *summed[max(part - 2, 0) : max(part - 1, 0)])
        projected = lax.dot_general(
            combined, out_weight, (((0,), (0,)), ((), ())), preferred_element_type=jnp.float32
        ).astype(jnp.bfloat16)
        summed.append(scatter_cores(projected))
    pieces = [scatter_chips(block) for block in summed]
    return jnp.concatenate(pieces, axis=0).reshape(spatial // head_groups, frames_here, -1)


def solution(mesh):
    in_specs = (
        P(None, "frames", "heads"),
        P(None, None, "frames", "heads"),
        P(),
        P(),
        P(None, None, "frames", "heads"),
        P("heads", None),
    )
    out_specs = P("heads", "frames", None)
    return jax.shard_map(local, mesh=mesh, in_specs=in_specs, out_specs=out_specs, check_vma=False)
```

```python
import functools

import jax
import jax.numpy as jnp
from jax import lax
from jax.experimental import pallas as pl
from jax.experimental.pallas import tpu as pltpu
from jax.sharding import PartitionSpec as P

HEAD_DIM = 128
TILE_ROWS = 16
HEAD_GROUPS = 2
VMEM_BYTES = 24 * 1024 * 1024


def after(block, *before):
    return lax.optimization_barrier((block, *before))[0] if before else block


def wide(block):
    return block.astype(jnp.float32)


def added(*blocks):
    return functools.reduce(jnp.add, [wide(block) for block in blocks]).astype(jnp.bfloat16)


def in_three(block):
    terms = []
    for _ in range(3):
        term = lax.reduce_precision(block, 8, 7)
        terms.append(term.astype(jnp.bfloat16))
        block = block - term
    return terms


def attend_columns(keys, values, queries, allowed):
    scale = HEAD_DIM ** (-0.5)
    scores = lax.dot_general(
        keys, queries, (((1,), (1,)), ((), ())), preferred_element_type=jnp.float32
    )
    scores = jnp.where(allowed, scores, -jnp.inf)
    peak = jnp.max(scores, axis=0, keepdims=True)
    weights = jnp.exp((scores - peak) * scale)
    totals = jnp.sum(weights, axis=0, keepdims=True)
    gathered = lax.dot_general(
        values, weights.astype(jnp.bfloat16), (((0,), (0,)), ((), ())),
        preferred_element_type=jnp.float32,
    )
    return gathered * (1.0 / totals), peak * scale + jnp.log(totals)


def bank_kernel(banks, live_ref, own_ref, far_ref, *refs):
    bank_refs = refs[:banks]
    head = pl.program_id(0)
    tokens = sum(bank.shape[2] for bank in bank_refs)
    second = lax.broadcasted_iota(jnp.int32, (2 * tokens, own_ref.shape[0]), 0) >= tokens
    for side, query_ref in enumerate((own_ref, far_ref)):
        out_ref, level_ref = refs[banks + 2 * side : banks + 2 * side + 2]
        keys, values = (
            jnp.concatenate([bank[which, 2 * side + slot] for slot in range(2) for bank in bank_refs], axis=0)
            for which in range(2)
        )
        allowed = jnp.logical_or(jnp.logical_not(second), live_ref[side, 1] > 0)
        gathered, level = attend_columns(keys, values, query_ref[...], allowed)
        rows = out_ref.shape[2]
        for part in range(out_ref.shape[0]):
            here = slice(part * rows, (part + 1) * rows)
            out_ref[part] = gathered[:, here].astype(out_ref.dtype)
            level_ref[part, pl.ds(head, 1), :] = level[:, here]


def attend_bank(group, parts, rows, live, own, far, banks):
    width = banks[0].shape[3]
    heads = width // HEAD_DIM
    keys_each = 2 * sum(bank.shape[2] for bank in banks)
    query_spec = pl.BlockSpec((parts * rows, HEAD_DIM), lambda h: (0, group * heads + h))
    out = jax.ShapeDtypeStruct((parts, width, rows), jnp.bfloat16)
    level = jax.ShapeDtypeStruct((parts, heads, rows), jnp.float32)
    out_spec = pl.BlockSpec((parts, HEAD_DIM, rows), lambda h: (0, h, 0))
    level_spec = pl.BlockSpec((parts, heads, rows), lambda h: (0, 0, 0))
    return pl.pallas_call(
        functools.partial(bank_kernel, len(banks)),
        grid=(heads,),
        in_specs=[pl.BlockSpec(memory_space=pltpu.SMEM), query_spec, query_spec]
        + [pl.BlockSpec((*bank.shape[:3], HEAD_DIM), lambda h: (0, 0, 0, h)) for bank in banks],
        out_specs=[out_spec, level_spec] * 2,
        out_shape=[out, level] * 2,
        compiler_params=pltpu.CompilerParams(vmem_limit_bytes=VMEM_BYTES),
        cost_estimate=pl.CostEstimate(
            flops=32 * parts * rows * width * keys_each,
            bytes_accessed=2 * (4 * parts * rows * width + sum(bank.size for bank in banks)),
            transcendentals=2 * parts * rows * heads * keys_each,
        ),
    )(live, own, far, *banks)


def frame_kernel(frames_here, token_ref, out_ref):
    scale = HEAD_DIM ** (-0.5)
    pieces, _, parts, rows, _ = token_ref.shape
    size = pieces * rows
    query_spot = lax.broadcasted_iota(jnp.int32, (size, size), 0) % rows // frames_here
    key_spot = lax.broadcasted_iota(jnp.int32, (size, size), 1) % rows // frames_here
    same_spot = query_spot == key_spot
    for part in range(parts):
        queries, keys, values = (
            jnp.concatenate([token_ref[piece, which, part] for piece in range(pieces)], axis=0)
            for which in range(3)
        )
        scores = lax.dot_general(
            queries, keys, (((1,), (1,)), ((), ())), preferred_element_type=jnp.float32
        )
        scores = jnp.where(same_spot, scores, -jnp.inf)
        weights = jnp.exp((scores - jnp.max(scores, axis=1, keepdims=True)) * scale)
        totals = jnp.sum(weights, axis=1, keepdims=True)
        gathered = jnp.dot(weights.astype(jnp.bfloat16), values, preferred_element_type=jnp.float32)
        gathered = (gathered / totals).astype(out_ref.dtype)
        for piece in range(pieces):
            out_ref[piece, part] = gathered[piece * rows : (piece + 1) * rows]


def attend_frames(frames_here, tokens):
    pieces, _, parts, rows, width = tokens.shape
    return pl.pallas_call(
        functools.partial(frame_kernel, frames_here),
        grid=(width // HEAD_DIM,),
        in_specs=[pl.BlockSpec((pieces, 3, parts, rows, HEAD_DIM), lambda h: (0, 0, 0, 0, h))],
        out_specs=pl.BlockSpec((pieces, parts, rows, HEAD_DIM), lambda h: (0, 0, 0, h)),
        out_shape=jax.ShapeDtypeStruct((pieces, parts, rows, width), jnp.bfloat16),
        compiler_params=pltpu.CompilerParams(vmem_limit_bytes=VMEM_BYTES),
        cost_estimate=pl.CostEstimate(
            flops=16 * parts * (pieces * rows) ** 2 * width,
            bytes_accessed=8 * pieces * parts * rows * width,
            transcendentals=parts * (pieces * rows) ** 2 * width // HEAD_DIM,
        ),
    )(tokens)


def listed_kernel(place_ref, slots_ref, *refs):
    count = len(refs) // 2
    for source, target in zip(refs[:count], refs[count:]):
        target[...] = source[...]


def listed_banks(place, char_slots, char_bank, half, group, group_width):
    _, _, tokens, _ = char_bank.shape
    block = (2, 1, tokens, group_width)

    def source(step):
        def index(entry, place_ref, slots_ref):
            shard = place_ref[0] ^ step ^ (entry // 2 * half)
            return 0, slots_ref[shard * 2 + entry % 2], 0, group

        return pl.BlockSpec(block, index)

    return pl.pallas_call(
        listed_kernel,
        grid_spec=pltpu.PrefetchScalarGridSpec(
            num_scalar_prefetch=2,
            grid=(4,),
            in_specs=[source(step) for step in range(half)],
            out_specs=[pl.BlockSpec(block, lambda entry, *_: (0, entry, 0, 0)) for _ in range(half)],
        ),
        out_shape=[jax.ShapeDtypeStruct((2, 4, tokens, group_width), char_bank.dtype) for _ in range(half)],
        compiler_params=pltpu.CompilerParams(vmem_limit_bytes=VMEM_BYTES),
        cost_estimate=pl.CostEstimate(
            flops=0, bytes_accessed=32 * half * tokens * group_width, transcendentals=0
        ),
    )(place.reshape(1), char_slots.reshape(-1), *[char_bank] * half)


def local(bank_query, char_bank, char_slots, slot_live, frame_tokens, out_weight):
    spatial, frames_here, width = bank_query.shape
    heads_here = width // HEAD_DIM
    head_groups = lax.axis_size("heads")
    shards = lax.axis_size("frames")
    half = shards // 2
    place = lax.axis_index("frames")
    parts = max(1, spatial * frames_here // (TILE_ROWS * shards))
    across = shards // head_groups
    spots = spatial // (shards * parts)
    tile = spots * frames_here
    rows = shards * tile

    def swap(block, step):
        return lax.ppermute(block, "frames", [(a, a ^ step) for a in range(shards)])

    def by_part(block):
        cut = block.reshape(head_groups, parts, across, spots, frames_here, width)
        return jnp.moveaxis(cut, 1, 0).reshape(parts * rows, width)

    own = by_part(bank_query)
    far = swap(own, half)

    groups = HEAD_GROUPS if heads_here % HEAD_GROUPS == 0 else 1

    def banks_of(group, *before):
        blocks = listed_banks(
            place, after(char_slots, *before), char_bank, half, group, width // groups
        )
        blocks = [blocks[0]] + [swap(blocks[step], step) for step in range(1, half)]
        return blocks if char_bank.shape[2] % TILE_ROWS == 0 else [jnp.concatenate(blocks, axis=2)]

    banks = [banks_of(0)]
    tokens = frame_tokens.reshape(3, head_groups, parts, across, spots, frames_here, width)
    tokens = tokens.transpose(1, 3, 0, 2, 4, 5, 6).reshape(shards, 3, parts, tile, width)
    tokens = lax.all_to_all(after(tokens, far, *banks[0]), "frames", 0, 0, tiled=True)
    live = jnp.stack([slot_live[place], slot_live[place ^ half]])

    place_heads = lax.axis_index("heads")
    chips, core, chip = head_groups // 2, place_heads % 2, place_heads // 2

    def scatter_cores(block):
        block = block.reshape(chips, 2, -1, block.shape[-1])
        give = lax.dynamic_index_in_dim(block, 1 - core, 1, keepdims=False)
        keep = lax.dynamic_index_in_dim(block, core, 1, keepdims=False)
        return added(keep, lax.ppermute(give, "heads", [(h, h ^ 1) for h in range(head_groups)]))

    def scatter_chips(summed):
        parcels = [lax.dynamic_index_in_dim(summed, chip, 0, keepdims=False)]
        for step in range(1, chips):
            give = lax.dynamic_index_in_dim(summed, (chip + step) % chips, 0, keepdims=False)
            parcels.append(
                lax.ppermute(give, "heads", [(h, (h + 2 * step) % head_groups) for h in range(head_groups)])
            )
        return added(*parcels)

    split = (heads_here // groups, HEAD_DIM, rows)
    results = []
    for group in range(groups):
        near_out, near_level, far_out, far_level = attend_bank(group, parts, rows, live, own, far, banks[group])
        if group < groups - 1:
            banks.append(banks_of(group + 1, far_level))
        if group == 0:
            frame_parts = attend_frames(frames_here, after(tokens, far_level))
            back = lax.all_to_all(frame_parts, "frames", 0, 0, tiled=True)
            live = after(live, frame_parts)
        message = jnp.concatenate([far_out, *in_three(far_level)], axis=1)
        message = jnp.pad(message, ((0, 0), (0, -message.shape[1] % TILE_ROWS), (0, 0)))
        if group < groups - 1:
            got = swap(message, half)
        else:
            got = [swap(message[part], half) for part in range(parts)]
        results.append((near_out, near_level, got))
    results = [
        (near_out, near_level, after(got, results[-1][1]) if group < groups - 1 else got)
        for group, (near_out, near_level, got) in enumerate(results)
    ]

    def share_of(group, part, *before):
        near_out, near_level, got = results[group]
        got = after(got[part], *(before if group == groups - 1 else ()))
        size = heads_here // groups
        got_level = sum(wide(got[low : low + size]) for low in range(width // groups, width // groups + 3 * size, size))
        peak = jnp.maximum(near_level[part], got_level)
        near_share, got_share = jnp.exp(near_level[part] - peak), jnp.exp(got_level - peak)
        total = near_share + got_share
        return (
            wide(near_out[part].reshape(split)) * (near_share / total)[:, None, :]
            + wide(got[: width // groups].reshape(split)) * (got_share / total)[:, None, :]
        )

    projected, summed = [], []
    for part in range(parts):
        shares = [share_of(group, part, *projected[-1:]) for group in range(groups)]
        ref_out = jnp.concatenate(shares, axis=0).reshape(width, rows)
        frame_out = back[:, part].reshape(rows, width)
        combined = (ref_out + wide(frame_out.T)).astype(jnp.bfloat16)
        projected.append(
            lax.dot_general(
                after(combined, *summed[-1:]), out_weight, (((0,), (0,)), ((), ())),
                preferred_element_type=jnp.float32,
            ).astype(jnp.bfloat16)
        )
        summed.append(scatter_cores(projected[-1]))
    pieces = [scatter_chips(block) for block in summed]
    return jnp.concatenate(pieces, axis=0).reshape(spatial // head_groups, frames_here, -1)


def solution(mesh):
    in_specs = (
        P(None, "frames", "heads"),
        P(None, None, "frames", "heads"),
        P(),
        P(),
        P(None, None, "frames", "heads"),
        P("heads", None),
    )
    out_specs = P("heads", "frames", None)
    return jax.shard_map(local, mesh=mesh, in_specs=in_specs, out_specs=out_specs, check_vma=False)
```

```python
import functools

import jax
import jax.numpy as jnp
from jax import lax
from jax.experimental import pallas as pl
from jax.experimental.pallas import tpu as pltpu
from jax.sharding import PartitionSpec as P

HEAD_DIM = 128
TILE_ROWS = 16
HEAD_GROUPS = 2
VMEM_BYTES = 48 * 1024 * 1024


def after(block, *before):
    return lax.optimization_barrier((block, *before))[0] if before else block


def wide(block):
    return block.astype(jnp.float32)


def added(*blocks):
    return functools.reduce(jnp.add, [wide(block) for block in blocks]).astype(jnp.bfloat16)


def in_three(block):
    terms = []
    for _ in range(3):
        term = lax.reduce_precision(block, 8, 7)
        terms.append(term.astype(jnp.bfloat16))
        block = block - term
    return terms


def attend_columns(keys, values, queries, allowed):
    scale = HEAD_DIM ** (-0.5)
    scores = lax.dot_general(
        keys, queries, (((1,), (1,)), ((), ())), preferred_element_type=jnp.float32
    )
    scores = jnp.where(allowed, scores, -jnp.inf)
    peak = jnp.max(scores, axis=0, keepdims=True)
    weights = jnp.exp((scores - peak) * scale)
    totals = jnp.sum(weights, axis=0, keepdims=True)
    gathered = lax.dot_general(
        values, weights.astype(jnp.bfloat16), (((0,), (0,)), ((), ())),
        preferred_element_type=jnp.float32,
    )
    return gathered * (1.0 / totals), peak * scale + jnp.log(totals)


def bank_kernel(banks, live_ref, own_ref, far_ref, *refs):
    bank_refs = refs[:banks]
    head = pl.program_id(0)
    tokens = sum(bank.shape[2] for bank in bank_refs)
    second = lax.broadcasted_iota(jnp.int32, (2 * tokens, own_ref.shape[0]), 0) >= tokens
    for side, query_ref in enumerate((own_ref, far_ref)):
        out_ref, level_ref = refs[banks + 2 * side : banks + 2 * side + 2]
        keys, values = (
            jnp.concatenate([bank[which, 2 * side + slot] for slot in range(2) for bank in bank_refs], axis=0)
            for which in range(2)
        )
        allowed = jnp.logical_or(jnp.logical_not(second), live_ref[side, 1] > 0)
        gathered, level = attend_columns(keys, values, query_ref[...], allowed)
        rows = out_ref.shape[2]
        for part in range(out_ref.shape[0]):
            here = slice(part * rows, (part + 1) * rows)
            out_ref[part] = gathered[:, here].astype(out_ref.dtype)
            level_ref[part, pl.ds(head, 1), :] = level[:, here]


def attend_bank(group, parts, rows, live, own, far, banks):
    width = banks[0].shape[3]
    heads = width // HEAD_DIM
    keys_each = 2 * sum(bank.shape[2] for bank in banks)
    query_spec = pl.BlockSpec((parts * rows, HEAD_DIM), lambda h: (0, group * heads + h))
    out = jax.ShapeDtypeStruct((parts, width, rows), jnp.bfloat16)
    level = jax.ShapeDtypeStruct((parts, heads, rows), jnp.float32)
    out_spec = pl.BlockSpec((parts, HEAD_DIM, rows), lambda h: (0, h, 0))
    level_spec = pl.BlockSpec((parts, heads, rows), lambda h: (0, 0, 0))
    return pl.pallas_call(
        functools.partial(bank_kernel, len(banks)),
        grid=(heads,),
        in_specs=[pl.BlockSpec(memory_space=pltpu.SMEM), query_spec, query_spec]
        + [pl.BlockSpec((*bank.shape[:3], HEAD_DIM), lambda h: (0, 0, 0, h)) for bank in banks],
        out_specs=[out_spec, level_spec] * 2,
        out_shape=[out, level] * 2,
        compiler_params=pltpu.CompilerParams(vmem_limit_bytes=VMEM_BYTES),
        cost_estimate=pl.CostEstimate(
            flops=32 * parts * rows * width * keys_each,
            bytes_accessed=2 * (4 * parts * rows * width + sum(bank.size for bank in banks)),
            transcendentals=2 * parts * rows * heads * keys_each,
        ),
    )(live, own, far, *banks)


def frame_kernel(frames_here, query_ref, token_ref, out_ref):
    scale = HEAD_DIM ** (-0.5)
    pieces, _, parts, rows, _ = token_ref.shape
    size = pieces * rows
    query_spot = lax.broadcasted_iota(jnp.int32, (size, size), 0) % rows // frames_here
    key_spot = lax.broadcasted_iota(jnp.int32, (size, size), 1) % rows // frames_here
    same_spot = query_spot == key_spot
    for part in range(parts):
        queries, keys, values = (
            jnp.concatenate([source[piece, which, part] for piece in range(pieces)], axis=0)
            for source, which in ((query_ref, 0), (token_ref, 0), (token_ref, 1))
        )
        scores = lax.dot_general(
            queries, keys, (((1,), (1,)), ((), ())), preferred_element_type=jnp.float32
        )
        scores = jnp.where(same_spot, scores, -jnp.inf)
        weights = jnp.exp((scores - jnp.max(scores, axis=1, keepdims=True)) * scale)
        totals = jnp.sum(weights, axis=1, keepdims=True)
        gathered = jnp.dot(weights.astype(jnp.bfloat16), values, preferred_element_type=jnp.float32)
        gathered = (gathered / totals).astype(out_ref.dtype)
        for piece in range(pieces):
            out_ref[piece, part] = gathered[piece * rows : (piece + 1) * rows]


def attend_frames(frames_here, *tokens):
    pieces, _, parts, rows, width = tokens[0].shape
    return pl.pallas_call(
        functools.partial(frame_kernel, frames_here),
        grid=(width // HEAD_DIM,),
        in_specs=[pl.BlockSpec((*block.shape[:4], HEAD_DIM), lambda h: (0, 0, 0, 0, h)) for block in tokens],
        out_specs=pl.BlockSpec((pieces, parts, rows, HEAD_DIM), lambda h: (0, 0, 0, h)),
        out_shape=jax.ShapeDtypeStruct((pieces, parts, rows, width), jnp.bfloat16),
        compiler_params=pltpu.CompilerParams(vmem_limit_bytes=VMEM_BYTES),
        cost_estimate=pl.CostEstimate(
            flops=16 * parts * (pieces * rows) ** 2 * width,
            bytes_accessed=8 * pieces * parts * rows * width,
            transcendentals=parts * (pieces * rows) ** 2 * width // HEAD_DIM,
        ),
    )(*tokens)


def listed_kernel(place_ref, slots_ref, *refs):
    count = len(refs) // 2
    for source, target in zip(refs[:count], refs[count:]):
        target[...] = source[...]


def listed_banks(place, char_slots, char_bank, half, group, group_width):
    _, _, tokens, _ = char_bank.shape
    block = (2, 1, tokens, group_width)

    def source(step):
        def index(entry, place_ref, slots_ref):
            shard = place_ref[0] ^ step ^ (entry // 2 * half)
            return 0, slots_ref[shard * 2 + entry % 2], 0, group

        return pl.BlockSpec(block, index)

    return pl.pallas_call(
        listed_kernel,
        grid_spec=pltpu.PrefetchScalarGridSpec(
            num_scalar_prefetch=2,
            grid=(4,),
            in_specs=[source(step) for step in range(half)],
            out_specs=[pl.BlockSpec(block, lambda entry, *_: (0, entry, 0, 0)) for _ in range(half)],
        ),
        out_shape=[jax.ShapeDtypeStruct((2, 4, tokens, group_width), char_bank.dtype) for _ in range(half)],
        compiler_params=pltpu.CompilerParams(vmem_limit_bytes=VMEM_BYTES),
        cost_estimate=pl.CostEstimate(
            flops=0, bytes_accessed=32 * half * tokens * group_width, transcendentals=0
        ),
    )(place.reshape(1), char_slots.reshape(-1), *[char_bank] * half)


def local(bank_query, char_bank, char_slots, slot_live, frame_tokens, out_weight):
    spatial, frames_here, width = bank_query.shape
    heads_here = width // HEAD_DIM
    head_groups = lax.axis_size("heads")
    shards = lax.axis_size("frames")
    half = shards // 2
    place = lax.axis_index("frames")
    parts = max(1, spatial * frames_here // (TILE_ROWS * shards))
    across = shards // head_groups
    spots = spatial // (shards * parts)
    tile = spots * frames_here
    rows = shards * tile

    def swap(block, step):
        return lax.ppermute(block, "frames", [(a, a ^ step) for a in range(shards)])

    def by_part(block):
        cut = block.reshape(head_groups, parts, across, spots, frames_here, width)
        return jnp.moveaxis(cut, 1, 0).reshape(parts * rows, width)

    own = by_part(bank_query)
    far = swap(own, half)

    groups = HEAD_GROUPS if heads_here % HEAD_GROUPS == 0 else 1

    def banks_of(group, *before):
        blocks = listed_banks(
            place, after(char_slots, *before), char_bank, half, group, width // groups
        )
        blocks = [blocks[0]] + [swap(blocks[step], step) for step in range(1, half)]
        return blocks if char_bank.shape[2] % TILE_ROWS == 0 else [jnp.concatenate(blocks, axis=2)]

    banks = [banks_of(0)]
    tokens = frame_tokens.reshape(3, head_groups, parts, across, spots, frames_here, width)
    tokens = tokens.transpose(1, 3, 0, 2, 4, 5, 6).reshape(shards, 3, parts, tile, width)
    tokens = [
        lax.all_to_all(after(tokens[:, :1], far, *banks[0][:-1]), "frames", 0, 0, tiled=True),
        lax.all_to_all(after(tokens[:, 1:], far, *banks[0]), "frames", 0, 0, tiled=True),
    ]
    live = jnp.stack([slot_live[place], slot_live[place ^ half]])

    place_heads = lax.axis_index("heads")
    chips, core, chip = head_groups // 2, place_heads % 2, place_heads // 2

    def scatter_cores(block):
        block = block.reshape(chips, 2, -1, block.shape[-1])
        give = lax.dynamic_index_in_dim(block, 1 - core, 1, keepdims=False)
        keep = lax.dynamic_index_in_dim(block, core, 1, keepdims=False)
        return added(keep, lax.ppermute(give, "heads", [(h, h ^ 1) for h in range(head_groups)]))

    def scatter_chips(summed):
        parcels = [lax.dynamic_index_in_dim(summed, chip, 0, keepdims=False)]
        for step in range(1, chips):
            give = lax.dynamic_index_in_dim(summed, (chip + step) % chips, 0, keepdims=False)
            parcels.append(
                lax.ppermute(give, "heads", [(h, (h + 2 * step) % head_groups) for h in range(head_groups)])
            )
        return added(*parcels)

    split = (heads_here // groups, HEAD_DIM, rows)
    results = []
    for group in range(groups):
        near_out, near_level, far_out, far_level = attend_bank(group, parts, rows, live, own, far, banks[group])
        if group < groups - 1:
            banks.append(banks_of(group + 1, far_level))
        if group == 0:
            frame_parts = attend_frames(frames_here, after(tokens[0], far_level), tokens[1])
            back = lax.all_to_all(frame_parts, "frames", 0, 0, tiled=True)
            live = after(live, frame_parts)
        message = jnp.concatenate([far_out, *in_three(far_level)], axis=1)
        message = jnp.pad(message, ((0, 0), (0, -message.shape[1] % TILE_ROWS), (0, 0)))
        if group < groups - 1:
            got = swap(message, half)
        else:
            got = [swap(message[part], half) for part in range(parts)]
        results.append((near_out, near_level, got))
    results = [
        (near_out, near_level, after(got, results[-1][1]) if group < groups - 1 else got)
        for group, (near_out, near_level, got) in enumerate(results)
    ]

    def share_of(group, part, *before):
        near_out, near_level, got = results[group]
        got = after(got[part], *(before if group == groups - 1 else ()))
        size = heads_here // groups
        got_level = sum(wide(got[low : low + size]) for low in range(width // groups, width // groups + 3 * size, size))
        peak = jnp.maximum(near_level[part], got_level)
        near_share, got_share = jnp.exp(near_level[part] - peak), jnp.exp(got_level - peak)
        total = near_share + got_share
        return (
            wide(near_out[part].reshape(split)) * (near_share / total)[:, None, :]
            + wide(got[: width // groups].reshape(split)) * (got_share / total)[:, None, :]
        )

    projected, summed = [], []
    for part in range(parts):
        shares = [share_of(group, part, *projected[-1:]) for group in range(groups)]
        ref_out = jnp.concatenate(shares, axis=0).reshape(width, rows)
        frame_out = back[:, part].reshape(rows, width)
        combined = (ref_out + wide(frame_out.T)).astype(jnp.bfloat16)
        projected.append(
            lax.dot_general(
                after(combined, *summed[-1:]), out_weight, (((0,), (0,)), ((), ())),
                preferred_element_type=jnp.float32,
            ).astype(jnp.bfloat16)
        )
        summed.append(scatter_cores(projected[-1]))
    pieces = [scatter_chips(block) for block in summed]
    return jnp.concatenate(pieces, axis=0).reshape(spatial // head_groups, frames_here, -1)


def solution(mesh):
    in_specs = (
        P(None, "frames", "heads"),
        P(None, None, "frames", "heads"),
        P(),
        P(),
        P(None, None, "frames", "heads"),
        P("heads", None),
    )
    out_specs = P("heads", "frames", None)
    return jax.shard_map(local, mesh=mesh, in_specs=in_specs, out_specs=out_specs, check_vma=False)
```

```python
import functools

import jax
import jax.numpy as jnp
from jax import lax
from jax.experimental import pallas as pl
from jax.experimental.pallas import tpu as pltpu
from jax.sharding import PartitionSpec as P

HEAD_DIM = 128
TILE_ROWS = 16
PART_TILE = 32
HEAD_GROUPS = 2
VMEM_BYTES = 24 * 1024 * 1024


def after(block, *before):
    return lax.optimization_barrier((block, *before))[0] if before else block


def wide(block):
    return block.astype(jnp.float32)


def added(*blocks):
    return functools.reduce(jnp.add, [wide(block) for block in blocks]).astype(jnp.bfloat16)


def in_three(block):
    terms = []
    for _ in range(3):
        term = lax.reduce_precision(block, 8, 7)
        terms.append(term.astype(jnp.bfloat16))
        block = block - term
    return terms


def attend_columns(keys, values, queries, allowed):
    scale = HEAD_DIM ** (-0.5)
    scores = lax.dot_general(
        keys, queries, (((1,), (1,)), ((), ())), preferred_element_type=jnp.float32
    )
    scores = jnp.where(allowed, scores, -jnp.inf)
    peak = jnp.max(scores, axis=0, keepdims=True)
    weights = jnp.exp((scores - peak) * scale)
    totals = jnp.sum(weights, axis=0, keepdims=True)
    gathered = lax.dot_general(
        values, weights.astype(jnp.bfloat16), (((0,), (0,)), ((), ())),
        preferred_element_type=jnp.float32,
    )
    return gathered * (1.0 / totals), peak * scale + jnp.log(totals)


def bank_kernel(banks, live_ref, own_ref, far_ref, *refs):
    bank_refs = refs[:banks]
    head = pl.program_id(0)
    tokens = sum(bank.shape[2] for bank in bank_refs)
    second = lax.broadcasted_iota(jnp.int32, (2 * tokens, own_ref.shape[0]), 0) >= tokens
    for side, query_ref in enumerate((own_ref, far_ref)):
        out_ref, level_ref = refs[banks + 2 * side : banks + 2 * side + 2]
        keys, values = (
            jnp.concatenate([bank[which, 2 * side + slot] for slot in range(2) for bank in bank_refs], axis=0)
            for which in range(2)
        )
        allowed = jnp.logical_or(jnp.logical_not(second), live_ref[side, 1] > 0)
        gathered, level = attend_columns(keys, values, query_ref[...], allowed)
        rows = out_ref.shape[2]
        for part in range(out_ref.shape[0]):
            here = slice(part * rows, (part + 1) * rows)
            out_ref[part] = gathered[:, here].astype(out_ref.dtype)
            level_ref[part, pl.ds(head, 1), :] = level[:, here]


def attend_bank(group, parts, rows, live, own, far, banks):
    width = banks[0].shape[3]
    heads = width // HEAD_DIM
    keys_each = 2 * sum(bank.shape[2] for bank in banks)
    query_spec = pl.BlockSpec((parts * rows, HEAD_DIM), lambda h: (0, group * heads + h))
    out = jax.ShapeDtypeStruct((parts, width, rows), jnp.bfloat16)
    level = jax.ShapeDtypeStruct((parts, heads, rows), jnp.float32)
    out_spec = pl.BlockSpec((parts, HEAD_DIM, rows), lambda h: (0, h, 0))
    level_spec = pl.BlockSpec((parts, heads, rows), lambda h: (0, 0, 0))
    return pl.pallas_call(
        functools.partial(bank_kernel, len(banks)),
        grid=(heads,),
        in_specs=[pl.BlockSpec(memory_space=pltpu.SMEM), query_spec, query_spec]
        + [pl.BlockSpec((*bank.shape[:3], HEAD_DIM), lambda h: (0, 0, 0, h)) for bank in banks],
        out_specs=[out_spec, level_spec] * 2,
        out_shape=[out, level] * 2,
        compiler_params=pltpu.CompilerParams(vmem_limit_bytes=VMEM_BYTES),
        cost_estimate=pl.CostEstimate(
            flops=32 * parts * rows * width * keys_each,
            bytes_accessed=2 * (4 * parts * rows * width + sum(bank.size for bank in banks)),
            transcendentals=2 * parts * rows * heads * keys_each,
        ),
    )(live, own, far, *banks)


def frame_kernel(frames_here, token_ref, out_ref):
    scale = HEAD_DIM ** (-0.5)
    pieces, _, parts, rows, _ = token_ref.shape
    size = pieces * rows
    query_spot = lax.broadcasted_iota(jnp.int32, (size, size), 0) % rows // frames_here
    key_spot = lax.broadcasted_iota(jnp.int32, (size, size), 1) % rows // frames_here
    same_spot = query_spot == key_spot
    for part in range(parts):
        queries, keys, values = (
            jnp.concatenate([token_ref[piece, which, part] for piece in range(pieces)], axis=0)
            for which in range(3)
        )
        scores = lax.dot_general(
            queries, keys, (((1,), (1,)), ((), ())), preferred_element_type=jnp.float32
        )
        scores = jnp.where(same_spot, scores, -jnp.inf)
        weights = jnp.exp((scores - jnp.max(scores, axis=1, keepdims=True)) * scale)
        totals = jnp.sum(weights, axis=1, keepdims=True)
        gathered = jnp.dot(weights.astype(jnp.bfloat16), values, preferred_element_type=jnp.float32)
        gathered = (gathered / totals).astype(out_ref.dtype)
        for piece in range(pieces):
            out_ref[piece, part] = gathered[piece * rows : (piece + 1) * rows]


def attend_frames(frames_here, tokens):
    pieces, _, parts, rows, width = tokens.shape
    return pl.pallas_call(
        functools.partial(frame_kernel, frames_here),
        grid=(width // HEAD_DIM,),
        in_specs=[pl.BlockSpec((pieces, 3, parts, rows, HEAD_DIM), lambda h: (0, 0, 0, 0, h))],
        out_specs=pl.BlockSpec((pieces, parts, rows, HEAD_DIM), lambda h: (0, 0, 0, h)),
        out_shape=jax.ShapeDtypeStruct((pieces, parts, rows, width), jnp.bfloat16),
        compiler_params=pltpu.CompilerParams(vmem_limit_bytes=VMEM_BYTES),
        cost_estimate=pl.CostEstimate(
            flops=16 * parts * (pieces * rows) ** 2 * width,
            bytes_accessed=8 * pieces * parts * rows * width,
            transcendentals=parts * (pieces * rows) ** 2 * width // HEAD_DIM,
        ),
    )(tokens)


def listed_kernel(place_ref, slots_ref, *refs):
    count = len(refs) // 2
    for source, target in zip(refs[:count], refs[count:]):
        target[...] = source[...]


def listed_banks(place, char_slots, char_bank, half, group, group_width):
    _, _, tokens, _ = char_bank.shape
    block = (2, 1, tokens, group_width)

    def source(step):
        def index(entry, place_ref, slots_ref):
            shard = place_ref[0] ^ step ^ (entry // 2 * half)
            return 0, slots_ref[shard * 2 + entry % 2], 0, group

        return pl.BlockSpec(block, index)

    return pl.pallas_call(
        listed_kernel,
        grid_spec=pltpu.PrefetchScalarGridSpec(
            num_scalar_prefetch=2,
            grid=(4,),
            in_specs=[source(step) for step in range(half)],
            out_specs=[pl.BlockSpec(block, lambda entry, *_: (0, entry, 0, 0)) for _ in range(half)],
        ),
        out_shape=[jax.ShapeDtypeStruct((2, 4, tokens, group_width), char_bank.dtype) for _ in range(half)],
        compiler_params=pltpu.CompilerParams(vmem_limit_bytes=VMEM_BYTES),
        cost_estimate=pl.CostEstimate(
            flops=0, bytes_accessed=32 * half * tokens * group_width, transcendentals=0
        ),
    )(place.reshape(1), char_slots.reshape(-1), *[char_bank] * half)


def local(bank_query, char_bank, char_slots, slot_live, frame_tokens, out_weight):
    spatial, frames_here, width = bank_query.shape
    heads_here = width // HEAD_DIM
    head_groups = lax.axis_size("heads")
    shards = lax.axis_size("frames")
    half = shards // 2
    place = lax.axis_index("frames")
    parts = max(1, spatial * frames_here // (PART_TILE * shards))
    across = shards // head_groups
    spots = spatial // (shards * parts)
    tile = spots * frames_here
    rows = shards * tile

    def swap(block, step):
        return lax.ppermute(block, "frames", [(a, a ^ step) for a in range(shards)])

    def by_part(block):
        cut = block.reshape(head_groups, parts, across, spots, frames_here, width)
        return jnp.moveaxis(cut, 1, 0).reshape(parts * rows, width)

    own = by_part(bank_query)
    far = swap(own, half)

    groups = HEAD_GROUPS if heads_here % HEAD_GROUPS == 0 else 1

    def banks_of(group, *before):
        blocks = listed_banks(
            place, after(char_slots, *before), char_bank, half, group, width // groups
        )
        blocks = [blocks[0]] + [swap(blocks[step], step) for step in range(1, half)]
        return blocks if char_bank.shape[2] % TILE_ROWS == 0 else [jnp.concatenate(blocks, axis=2)]

    banks = [banks_of(0)]
    tokens = frame_tokens.reshape(3, head_groups, parts, across, spots, frames_here, width)
    tokens = tokens.transpose(1, 3, 0, 2, 4, 5, 6).reshape(shards, 3, parts, tile, width)
    tokens = lax.all_to_all(after(tokens, far, *banks[0]), "frames", 0, 0, tiled=True)
    live = jnp.stack([slot_live[place], slot_live[place ^ half]])

    place_heads = lax.axis_index("heads")
    chips, core, chip = head_groups // 2, place_heads % 2, place_heads // 2

    def scatter_cores(block):
        block = block.reshape(chips, 2, -1, block.shape[-1])
        give = lax.dynamic_index_in_dim(block, 1 - core, 1, keepdims=False)
        keep = lax.dynamic_index_in_dim(block, core, 1, keepdims=False)
        return added(keep, lax.ppermute(give, "heads", [(h, h ^ 1) for h in range(head_groups)]))

    def scatter_chips(summed):
        parcels = [lax.dynamic_index_in_dim(summed, chip, 0, keepdims=False)]
        for step in range(1, chips):
            give = lax.dynamic_index_in_dim(summed, (chip + step) % chips, 0, keepdims=False)
            parcels.append(
                lax.ppermute(give, "heads", [(h, (h + 2 * step) % head_groups) for h in range(head_groups)])
            )
        return added(*parcels)

    split = (heads_here // groups, HEAD_DIM, rows)
    results = []
    for group in range(groups):
        near_out, near_level, far_out, far_level = attend_bank(group, parts, rows, live, own, far, banks[group])
        if group < groups - 1:
            banks.append(banks_of(group + 1, far_level))
        if group == 0:
            frame_parts = attend_frames(frames_here, after(tokens, far_level))
            back = lax.all_to_all(frame_parts, "frames", 0, 0, tiled=True)
            live = after(live, frame_parts)
        message = jnp.concatenate([far_out, *in_three(far_level)], axis=1)
        message = jnp.pad(message, ((0, 0), (0, -message.shape[1] % TILE_ROWS), (0, 0)))
        if group < groups - 1:
            got = swap(message, half)
        else:
            got = [swap(message[part], half) for part in range(parts)]
        results.append((near_out, near_level, got))
    results = [
        (near_out, near_level, after(got, results[-1][1]) if group < groups - 1 else got)
        for group, (near_out, near_level, got) in enumerate(results)
    ]

    def share_of(group, part, *before):
        near_out, near_level, got = results[group]
        got = after(got[part], *(before if group == groups - 1 else ()))
        size = heads_here // groups
        got_level = sum(wide(got[low : low + size]) for low in range(width // groups, width // groups + 3 * size, size))
        peak = jnp.maximum(near_level[part], got_level)
        near_share, got_share = jnp.exp(near_level[part] - peak), jnp.exp(got_level - peak)
        total = near_share + got_share
        return (
            wide(near_out[part].reshape(split)) * (near_share / total)[:, None, :]
            + wide(got[: width // groups].reshape(split)) * (got_share / total)[:, None, :]
        )

    projected, summed = [], []
    for part in range(parts):
        shares = [share_of(group, part, *projected[-1:]) for group in range(groups)]
        ref_out = jnp.concatenate(shares, axis=0).reshape(width, rows)
        frame_out = back[:, part].reshape(rows, width)
        combined = (ref_out + wide(frame_out.T)).astype(jnp.bfloat16)
        projected.append(
            lax.dot_general(
                after(combined, *summed[-1:]), out_weight, (((0,), (0,)), ((), ())),
                preferred_element_type=jnp.float32,
            ).astype(jnp.bfloat16)
        )
        summed.append(scatter_cores(projected[-1]))
    pieces = [scatter_chips(block) for block in summed]
    return jnp.concatenate(pieces, axis=0).reshape(spatial // head_groups, frames_here, -1)


def solution(mesh):
    in_specs = (
        P(None, "frames", "heads"),
        P(None, None, "frames", "heads"),
        P(),
        P(),
        P(None, None, "frames", "heads"),
        P("heads", None),
    )
    out_specs = P("heads", "frames", None)
    return jax.shard_map(local, mesh=mesh, in_specs=in_specs, out_specs=out_specs, check_vma=False)
```

```python
import functools

import jax
import jax.numpy as jnp
from jax import lax
from jax.experimental import pallas as pl
from jax.experimental.pallas import tpu as pltpu
from jax.sharding import PartitionSpec as P

HEAD_DIM = 128
TILE_ROWS = 16
PART_TILE = 32
HEAD_GROUPS = 2
VMEM_BYTES = 24 * 1024 * 1024


def after(block, *before):
    return lax.optimization_barrier((block, *before))[0] if before else block


def wide(block):
    return block.astype(jnp.float32)


def added(*blocks):
    return functools.reduce(jnp.add, [wide(block) for block in blocks]).astype(jnp.bfloat16)


def in_three(block):
    terms = []
    for _ in range(3):
        term = lax.reduce_precision(block, 8, 7)
        terms.append(term.astype(jnp.bfloat16))
        block = block - term
    return terms


def attend_columns(keys, values, queries, allowed):
    scale = HEAD_DIM ** (-0.5)
    scores = lax.dot_general(
        keys, queries, (((1,), (1,)), ((), ())), preferred_element_type=jnp.float32
    )
    scores = jnp.where(allowed, scores, -jnp.inf)
    peak = jnp.max(scores, axis=0, keepdims=True)
    weights = jnp.exp((scores - peak) * scale)
    totals = jnp.sum(weights, axis=0, keepdims=True)
    gathered = lax.dot_general(
        values, weights.astype(jnp.bfloat16), (((0,), (0,)), ((), ())),
        preferred_element_type=jnp.float32,
    )
    return gathered * (1.0 / totals), peak * scale + jnp.log(totals)


def bank_kernel(banks, live_ref, own_ref, far_ref, *refs):
    bank_refs = refs[:banks]
    head = pl.program_id(0)
    tokens = sum(bank.shape[2] for bank in bank_refs)
    second = lax.broadcasted_iota(jnp.int32, (2 * tokens, own_ref.shape[0]), 0) >= tokens
    for side, query_ref in enumerate((own_ref, far_ref)):
        out_ref, level_ref = refs[banks + 2 * side : banks + 2 * side + 2]
        keys, values = (
            jnp.concatenate([bank[which, 2 * side + slot] for slot in range(2) for bank in bank_refs], axis=0)
            for which in range(2)
        )
        allowed = jnp.logical_or(jnp.logical_not(second), live_ref[side, 1] > 0)
        gathered, level = attend_columns(keys, values, query_ref[...], allowed)
        rows = out_ref.shape[2]
        for part in range(out_ref.shape[0]):
            here = slice(part * rows, (part + 1) * rows)
            out_ref[part] = gathered[:, here].astype(out_ref.dtype)
            level_ref[part, pl.ds(head, 1), :] = level[:, here]


def attend_bank(group, parts, rows, live, own, far, banks):
    width = banks[0].shape[3]
    heads = width // HEAD_DIM
    keys_each = 2 * sum(bank.shape[2] for bank in banks)
    query_spec = pl.BlockSpec((parts * rows, HEAD_DIM), lambda h: (0, group * heads + h))
    out = jax.ShapeDtypeStruct((parts, width, rows), jnp.bfloat16)
    level = jax.ShapeDtypeStruct((parts, heads, rows), jnp.float32)
    out_spec = pl.BlockSpec((parts, HEAD_DIM, rows), lambda h: (0, h, 0))
    level_spec = pl.BlockSpec((parts, heads, rows), lambda h: (0, 0, 0))
    return pl.pallas_call(
        functools.partial(bank_kernel, len(banks)),
        grid=(heads,),
        in_specs=[pl.BlockSpec(memory_space=pltpu.SMEM), query_spec, query_spec]
        + [pl.BlockSpec((*bank.shape[:3], HEAD_DIM), lambda h: (0, 0, 0, h)) for bank in banks],
        out_specs=[out_spec, level_spec] * 2,
        out_shape=[out, level] * 2,
        compiler_params=pltpu.CompilerParams(vmem_limit_bytes=VMEM_BYTES),
        cost_estimate=pl.CostEstimate(
            flops=32 * parts * rows * width * keys_each,
            bytes_accessed=2 * (4 * parts * rows * width + sum(bank.size for bank in banks)),
            transcendentals=2 * parts * rows * heads * keys_each,
        ),
    )(live, own, far, *banks)


def frame_kernel(frames_here, token_ref, out_ref):
    scale = HEAD_DIM ** (-0.5)
    pieces, _, parts, rows, _ = token_ref.shape
    size = pieces * rows
    query_spot = lax.broadcasted_iota(jnp.int32, (size, size), 0) % rows // frames_here
    key_spot = lax.broadcasted_iota(jnp.int32, (size, size), 1) % rows // frames_here
    same_spot = query_spot == key_spot
    for part in range(parts):
        queries, keys, values = (
            jnp.concatenate([token_ref[piece, which, part] for piece in range(pieces)], axis=0)
            for which in range(3)
        )
        scores = lax.dot_general(
            queries, keys, (((1,), (1,)), ((), ())), preferred_element_type=jnp.float32
        )
        scores = jnp.where(same_spot, scores, -jnp.inf)
        weights = jnp.exp((scores - jnp.max(scores, axis=1, keepdims=True)) * scale)
        totals = jnp.sum(weights, axis=1, keepdims=True)
        gathered = jnp.dot(weights.astype(jnp.bfloat16), values, preferred_element_type=jnp.float32)
        gathered = (gathered / totals).astype(out_ref.dtype)
        for piece in range(pieces):
            out_ref[piece, part] = gathered[piece * rows : (piece + 1) * rows]


def attend_frames(frames_here, tokens):
    pieces, _, parts, rows, width = tokens.shape
    return pl.pallas_call(
        functools.partial(frame_kernel, frames_here),
        grid=(width // HEAD_DIM,),
        in_specs=[pl.BlockSpec((pieces, 3, parts, rows, HEAD_DIM), lambda h: (0, 0, 0, 0, h))],
        out_specs=pl.BlockSpec((pieces, parts, rows, HEAD_DIM), lambda h: (0, 0, 0, h)),
        out_shape=jax.ShapeDtypeStruct((pieces, parts, rows, width), jnp.bfloat16),
        compiler_params=pltpu.CompilerParams(vmem_limit_bytes=VMEM_BYTES),
        cost_estimate=pl.CostEstimate(
            flops=16 * parts * (pieces * rows) ** 2 * width,
            bytes_accessed=8 * pieces * parts * rows * width,
            transcendentals=parts * (pieces * rows) ** 2 * width // HEAD_DIM,
        ),
    )(tokens)


def listed_kernel(place_ref, slots_ref, *refs):
    count = len(refs) // 2
    for source, target in zip(refs[:count], refs[count:]):
        target[...] = source[...]


def listed_banks(place, char_slots, char_bank, half, group, group_width):
    _, _, tokens, _ = char_bank.shape
    block = (2, 1, tokens, group_width)

    def source(step):
        def index(entry, place_ref, slots_ref):
            shard = place_ref[0] ^ step ^ (entry // 2 * half)
            return 0, slots_ref[shard * 2 + entry % 2], 0, group

        return pl.BlockSpec(block, index)

    return pl.pallas_call(
        listed_kernel,
        grid_spec=pltpu.PrefetchScalarGridSpec(
            num_scalar_prefetch=2,
            grid=(4,),
            in_specs=[source(step) for step in range(half)],
            out_specs=[pl.BlockSpec(block, lambda entry, *_: (0, entry, 0, 0)) for _ in range(half)],
        ),
        out_shape=[jax.ShapeDtypeStruct((2, 4, tokens, group_width), char_bank.dtype) for _ in range(half)],
        compiler_params=pltpu.CompilerParams(vmem_limit_bytes=VMEM_BYTES),
        cost_estimate=pl.CostEstimate(
            flops=0, bytes_accessed=32 * half * tokens * group_width, transcendentals=0
        ),
    )(place.reshape(1), char_slots.reshape(-1), *[char_bank] * half)


def local(bank_query, char_bank, char_slots, slot_live, frame_tokens, out_weight):
    spatial, frames_here, width = bank_query.shape
    heads_here = width // HEAD_DIM
    head_groups = lax.axis_size("heads")
    shards = lax.axis_size("frames")
    half = shards // 2
    place = lax.axis_index("frames")
    parts = max(1, spatial * frames_here // (PART_TILE * shards))
    across = shards // head_groups
    spots = spatial // (shards * parts)
    tile = spots * frames_here
    rows = shards * tile

    def swap(block, step):
        return lax.ppermute(block, "frames", [(a, a ^ step) for a in range(shards)])

    def by_part(block):
        cut = block.reshape(head_groups, parts, across, spots, frames_here, width)
        return jnp.moveaxis(cut, 1, 0).reshape(parts * rows, width)

    own = by_part(bank_query)
    far = swap(own, half)

    groups = HEAD_GROUPS if heads_here % HEAD_GROUPS == 0 else 1

    def banks_of(group, *before):
        blocks = listed_banks(
            place, after(char_slots, *before), char_bank, half, group, width // groups
        )
        blocks = [blocks[0]] + [swap(blocks[step], step) for step in range(1, half)]
        return blocks if char_bank.shape[2] % TILE_ROWS == 0 else [jnp.concatenate(blocks, axis=2)]

    banks = [banks_of(0)]
    tokens = frame_tokens.reshape(3, head_groups, parts, across, spots, frames_here, width)
    tokens = tokens.transpose(1, 3, 0, 2, 4, 5, 6).reshape(shards, 3, parts, tile, width)
    tokens = lax.all_to_all(after(tokens, far, *banks[0]), "frames", 0, 0, tiled=True)
    live = jnp.stack([slot_live[place], slot_live[place ^ half]])

    place_heads = lax.axis_index("heads")
    chips, core, chip = head_groups // 2, place_heads % 2, place_heads // 2

    def scatter_cores(block):
        block = block.reshape(chips, 2, -1, block.shape[-1])
        give = lax.dynamic_index_in_dim(block, 1 - core, 1, keepdims=False)
        keep = lax.dynamic_index_in_dim(block, core, 1, keepdims=False)
        return added(keep, lax.ppermute(give, "heads", [(h, h ^ 1) for h in range(head_groups)]))

    def scatter_chips(summed):
        parcels = [lax.dynamic_index_in_dim(summed, chip, 0, keepdims=False)]
        for step in range(1, chips):
            give = lax.dynamic_index_in_dim(summed, (chip + step) % chips, 0, keepdims=False)
            parcels.append(
                lax.ppermute(give, "heads", [(h, (h + 2 * step) % head_groups) for h in range(head_groups)])
            )
        return added(*parcels)

    split = (heads_here // groups, HEAD_DIM, rows)
    results = []
    for group in range(groups):
        near_out, near_level, far_out, far_level = attend_bank(group, parts, rows, live, own, far, banks[group])
        if group < groups - 1:
            banks.append(banks_of(group + 1, far_level))
        if group == 0:
            frame_parts = attend_frames(frames_here, after(tokens, far_level))
            back = lax.all_to_all(frame_parts, "frames", 0, 0, tiled=True)
            live = after(live, frame_parts)
        message = jnp.concatenate([far_out, *in_three(far_level)], axis=1)
        message = jnp.pad(message, ((0, 0), (0, -message.shape[1] % TILE_ROWS), (0, 0)))
        if group < groups - 1:
            got = swap(message, half)
        else:
            got = [swap(message[part], half) for part in range(parts)]
        results.append((near_out, near_level, got))
    results = [
        (near_out, near_level, after(got, results[-1][1]) if group < groups - 1 else got)
        for group, (near_out, near_level, got) in enumerate(results)
    ]

    def share_of(group, part, *before):
        near_out, near_level, got = results[group]
        got = after(got[part], *(before if group == groups - 1 else ()))
        size = heads_here // groups
        got_level = sum(wide(got[low : low + size]) for low in range(width // groups, width // groups + 3 * size, size))
        peak = jnp.maximum(near_level[part], got_level)
        near_share, got_share = jnp.exp(near_level[part] - peak), jnp.exp(got_level - peak)
        total = near_share + got_share
        return (
            wide(near_out[part].reshape(split)) * (near_share / total)[:, None, :]
            + wide(got[: width // groups].reshape(split)) * (got_share / total)[:, None, :]
        )

    def project(group, part, *before):
        low, high = group * width // groups, (group + 1) * width // groups
        frame_out = back[:, part].reshape(rows, width)[:, low:high]
        combined = share_of(group, part, *before).reshape(width // groups, rows) + wide(frame_out.T)
        return lax.dot_general(
            combined.astype(jnp.bfloat16), out_weight[low:high], (((0,), (0,)), ((), ())),
            preferred_element_type=jnp.float32,
        )

    early = [[project(group, part) for group in range(groups - 1)] for part in range(parts)]
    projected, pieces = [], []
    for part in range(parts):
        total = project(groups - 1, part, *early[-1], *early[0], *projected[-1:])
        projected.append(functools.reduce(jnp.add, [*early[part], total]).astype(jnp.bfloat16))
        pieces.append(scatter_chips(after(scatter_cores(projected[-1]), *pieces[-1:])))
    return jnp.concatenate(pieces, axis=0).reshape(spatial // head_groups, frames_here, -1)


def solution(mesh):
    in_specs = (
        P(None, "frames", "heads"),
        P(None, None, "frames", "heads"),
        P(),
        P(),
        P(None, None, "frames", "heads"),
        P("heads", None),
    )
    out_specs = P("heads", "frames", None)
    return jax.shard_map(local, mesh=mesh, in_specs=in_specs, out_specs=out_specs, check_vma=False)
```

```python
import functools

import jax
import jax.numpy as jnp
from jax import lax
from jax.experimental import pallas as pl
from jax.experimental.pallas import tpu as pltpu
from jax.sharding import PartitionSpec as P

HEAD_DIM = 128
TILE_ROWS = 16
PART_TILE = 32
HEAD_GROUPS = 2
VMEM_BYTES = 60 * 1024 * 1024


def after(block, *before):
    return lax.optimization_barrier((block, *before))[0] if before else block


def wide(block):
    return block.astype(jnp.float32)


def added(*blocks):
    return functools.reduce(jnp.add, [wide(block) for block in blocks]).astype(jnp.bfloat16)


def in_three(block):
    terms = []
    for _ in range(3):
        term = lax.reduce_precision(block, 8, 7)
        terms.append(term.astype(jnp.bfloat16))
        block = block - term
    return terms


def attend_columns(keys, values, queries, allowed):
    scale = HEAD_DIM ** (-0.5)
    scores = lax.dot_general(
        keys, queries, (((1,), (1,)), ((), ())), preferred_element_type=jnp.float32
    )
    scores = jnp.where(allowed, scores, -jnp.inf)
    peak = jnp.max(scores, axis=0, keepdims=True)
    weights = jnp.exp((scores - peak) * scale)
    totals = jnp.sum(weights, axis=0, keepdims=True)
    gathered = lax.dot_general(
        values, weights.astype(jnp.bfloat16), (((0,), (0,)), ((), ())),
        preferred_element_type=jnp.float32,
    )
    return gathered * (1.0 / totals), peak * scale + jnp.log(totals)


def bank_kernel(banks, live_ref, own_ref, far_ref, *refs):
    bank_refs = refs[:banks]
    head = pl.program_id(0)
    tokens = sum(bank.shape[2] for bank in bank_refs)
    second = lax.broadcasted_iota(jnp.int32, (2 * tokens, own_ref.shape[0]), 0) >= tokens
    for side, query_ref in enumerate((own_ref, far_ref)):
        out_ref, level_ref = refs[banks + 2 * side : banks + 2 * side + 2]
        keys, values = (
            jnp.concatenate([bank[which, 2 * side + slot] for slot in range(2) for bank in bank_refs], axis=0)
            for which in range(2)
        )
        allowed = jnp.logical_or(jnp.logical_not(second), live_ref[side, 1] > 0)
        gathered, level = attend_columns(keys, values, query_ref[...], allowed)
        rows = out_ref.shape[2]
        for part in range(out_ref.shape[0]):
            here = slice(part * rows, (part + 1) * rows)
            out_ref[part] = gathered[:, here].astype(out_ref.dtype)
            level_ref[part, pl.ds(head, 1), :] = level[:, here]


def attend_bank(group, parts, rows, live, own, far, banks):
    width = banks[0].shape[3]
    heads = width // HEAD_DIM
    keys_each = 2 * sum(bank.shape[2] for bank in banks)
    query_spec = pl.BlockSpec((parts * rows, HEAD_DIM), lambda h: (0, group * heads + h))
    out = jax.ShapeDtypeStruct((parts, width, rows), jnp.bfloat16)
    level = jax.ShapeDtypeStruct((parts, heads, rows), jnp.float32)
    out_spec = pl.BlockSpec((parts, HEAD_DIM, rows), lambda h: (0, h, 0))
    level_spec = pl.BlockSpec((parts, heads, rows), lambda h: (0, 0, 0))
    return pl.pallas_call(
        functools.partial(bank_kernel, len(banks)),
        grid=(heads,),
        in_specs=[pl.BlockSpec(memory_space=pltpu.SMEM), query_spec, query_spec]
        + [pl.BlockSpec((*bank.shape[:3], HEAD_DIM), lambda h: (0, 0, 0, h)) for bank in banks],
        out_specs=[out_spec, level_spec] * 2,
        out_shape=[out, level] * 2,
        compiler_params=pltpu.CompilerParams(vmem_limit_bytes=VMEM_BYTES),
        cost_estimate=pl.CostEstimate(
            flops=32 * parts * rows * width * keys_each,
            bytes_accessed=2 * (4 * parts * rows * width + sum(bank.size for bank in banks)),
            transcendentals=2 * parts * rows * heads * keys_each,
        ),
    )(live, own, far, *banks)


def frame_kernel(frames_here, token_ref, out_ref):
    scale = HEAD_DIM ** (-0.5)
    pieces, _, parts, rows, _ = token_ref.shape
    size = pieces * rows
    query_spot = lax.broadcasted_iota(jnp.int32, (size, size), 0) % rows // frames_here
    key_spot = lax.broadcasted_iota(jnp.int32, (size, size), 1) % rows // frames_here
    same_spot = query_spot == key_spot
    for part in range(parts):
        queries, keys, values = (
            jnp.concatenate([token_ref[piece, which, part] for piece in range(pieces)], axis=0)
            for which in range(3)
        )
        scores = lax.dot_general(
            queries, keys, (((1,), (1,)), ((), ())), preferred_element_type=jnp.float32
        )
        scores = jnp.where(same_spot, scores, -jnp.inf)
        weights = jnp.exp((scores - jnp.max(scores, axis=1, keepdims=True)) * scale)
        totals = jnp.sum(weights, axis=1, keepdims=True)
        gathered = jnp.dot(weights.astype(jnp.bfloat16), values, preferred_element_type=jnp.float32)
        gathered = (gathered / totals).astype(out_ref.dtype)
        for piece in range(pieces):
            out_ref[piece, part] = gathered[piece * rows : (piece + 1) * rows]


def attend_frames(frames_here, tokens):
    pieces, _, parts, rows, width = tokens.shape
    return pl.pallas_call(
        functools.partial(frame_kernel, frames_here),
        grid=(width // HEAD_DIM,),
        in_specs=[pl.BlockSpec((pieces, 3, parts, rows, HEAD_DIM), lambda h: (0, 0, 0, 0, h))],
        out_specs=pl.BlockSpec((pieces, parts, rows, HEAD_DIM), lambda h: (0, 0, 0, h)),
        out_shape=jax.ShapeDtypeStruct((pieces, parts, rows, width), jnp.bfloat16),
        compiler_params=pltpu.CompilerParams(vmem_limit_bytes=VMEM_BYTES),
        cost_estimate=pl.CostEstimate(
            flops=16 * parts * (pieces * rows) ** 2 * width,
            bytes_accessed=8 * pieces * parts * rows * width,
            transcendentals=parts * (pieces * rows) ** 2 * width // HEAD_DIM,
        ),
    )(tokens)


def listed_kernel(place_ref, slots_ref, *refs):
    count = len(refs) // 2
    for source, target in zip(refs[:count], refs[count:]):
        target[...] = source[...]


def listed_banks(place, char_slots, char_bank, half, group, group_width):
    _, _, tokens, _ = char_bank.shape
    block = (2, 1, tokens, group_width)

    def source(step):
        def index(entry, place_ref, slots_ref):
            shard = place_ref[0] ^ step ^ (entry // 2 * half)
            return 0, slots_ref[shard * 2 + entry % 2], 0, group

        return pl.BlockSpec(block, index)

    return pl.pallas_call(
        listed_kernel,
        grid_spec=pltpu.PrefetchScalarGridSpec(
            num_scalar_prefetch=2,
            grid=(4,),
            in_specs=[source(step) for step in range(half)],
            out_specs=[pl.BlockSpec(block, lambda entry, *_: (0, entry, 0, 0)) for _ in range(half)],
        ),
        out_shape=[jax.ShapeDtypeStruct((2, 4, tokens, group_width), char_bank.dtype) for _ in range(half)],
        compiler_params=pltpu.CompilerParams(vmem_limit_bytes=VMEM_BYTES),
        cost_estimate=pl.CostEstimate(
            flops=0, bytes_accessed=32 * half * tokens * group_width, transcendentals=0
        ),
    )(place.reshape(1), char_slots.reshape(-1), *[char_bank] * half)


def local(bank_query, char_bank, char_slots, slot_live, frame_tokens, out_weight):
    spatial, frames_here, width = bank_query.shape
    heads_here = width // HEAD_DIM
    head_groups = lax.axis_size("heads")
    shards = lax.axis_size("frames")
    half = shards // 2
    place = lax.axis_index("frames")
    parts = max(1, spatial * frames_here // (PART_TILE * shards))
    across = shards // head_groups
    spots = spatial // (shards * parts)
    tile = spots * frames_here
    rows = shards * tile

    def swap(block, step):
        return lax.ppermute(block, "frames", [(a, a ^ step) for a in range(shards)])

    def by_part(block):
        cut = block.reshape(head_groups, parts, across, spots, frames_here, width)
        return jnp.moveaxis(cut, 1, 0).reshape(parts * rows, width)

    own = by_part(bank_query)
    far = swap(own, half)

    groups = HEAD_GROUPS if heads_here % HEAD_GROUPS == 0 else 1

    def banks_of(group, *before):
        blocks = listed_banks(
            place, after(char_slots, *before), char_bank, half, group, width // groups
        )
        blocks = [blocks[0]] + [swap(blocks[step], step) for step in range(1, half)]
        return blocks if char_bank.shape[2] % TILE_ROWS == 0 else [jnp.concatenate(blocks, axis=2)]

    banks = [banks_of(0)]
    tokens = frame_tokens.reshape(3, head_groups, parts, across, spots, frames_here, width)
    tokens = tokens.transpose(1, 3, 0, 2, 4, 5, 6).reshape(shards, 3, parts, tile, width)
    tokens = lax.all_to_all(after(tokens, far, *banks[0]), "frames", 0, 0, tiled=True)
    live = jnp.stack([slot_live[place], slot_live[place ^ half]])

    place_heads = lax.axis_index("heads")
    chips, core, chip = head_groups // 2, place_heads % 2, place_heads // 2

    def scatter_cores(block):
        block = block.reshape(chips, 2, -1, block.shape[-1])
        give = lax.dynamic_index_in_dim(block, 1 - core, 1, keepdims=False)
        keep = lax.dynamic_index_in_dim(block, core, 1, keepdims=False)
        return added(keep, lax.ppermute(give, "heads", [(h, h ^ 1) for h in range(head_groups)]))

    def scatter_chips(summed):
        parcels = [lax.dynamic_index_in_dim(summed, chip, 0, keepdims=False)]
        for step in range(1, chips):
            give = lax.dynamic_index_in_dim(summed, (chip + step) % chips, 0, keepdims=False)
            parcels.append(
                lax.ppermute(give, "heads", [(h, (h + 2 * step) % head_groups) for h in range(head_groups)])
            )
        return added(*parcels)

    split = (heads_here // groups, HEAD_DIM, rows)
    results = []
    for group in range(groups):
        near_out, near_level, far_out, far_level = attend_bank(group, parts, rows, live, own, far, banks[group])
        if group < groups - 1:
            banks.append(banks_of(group + 1, far_level))
        if group == 0:
            frame_parts = attend_frames(frames_here, after(tokens, far_level))
            back = lax.all_to_all(frame_parts, "frames", 0, 0, tiled=True)
            live = after(live, frame_parts)
        message = jnp.concatenate([far_out, *in_three(far_level)], axis=1)
        message = jnp.pad(message, ((0, 0), (0, -message.shape[1] % TILE_ROWS), (0, 0)))
        if group < groups - 1:
            got = swap(message, half)
        else:
            got = [swap(message[part], half) for part in range(parts)]
        results.append((near_out, near_level, got))
    results = [
        (near_out, near_level, after(got, results[-1][1]) if group < groups - 1 else got)
        for group, (near_out, near_level, got) in enumerate(results)
    ]

    def share_of(group, part, *before):
        near_out, near_level, got = results[group]
        got = after(got[part], *(before if group == groups - 1 else ()))
        size = heads_here // groups
        got_level = sum(wide(got[low : low + size]) for low in range(width // groups, width // groups + 3 * size, size))
        peak = jnp.maximum(near_level[part], got_level)
        near_share, got_share = jnp.exp(near_level[part] - peak), jnp.exp(got_level - peak)
        total = near_share + got_share
        return (
            wide(near_out[part].reshape(split)) * (near_share / total)[:, None, :]
            + wide(got[: width // groups].reshape(split)) * (got_share / total)[:, None, :]
        )

    projected, summed = [], []
    for part in range(parts):
        shares = [share_of(group, part, *projected[-1:]) for group in range(groups)]
        ref_out = jnp.concatenate(shares, axis=0).reshape(width, rows)
        frame_out = back[:, part].reshape(rows, width)
        combined = (ref_out + wide(frame_out.T)).astype(jnp.bfloat16)
        projected.append(
            lax.dot_general(
                after(combined, *summed[-1:]), out_weight, (((0,), (0,)), ((), ())),
                preferred_element_type=jnp.float32,
            ).astype(jnp.bfloat16)
        )
        summed.append(scatter_cores(projected[-1]))
    pieces = []
    for block in summed:
        pieces.append(scatter_chips(after(block, *pieces[-1:])))
    return jnp.concatenate(pieces, axis=0).reshape(spatial // head_groups, frames_here, -1)


def solution(mesh):
    in_specs = (
        P(None, "frames", "heads"),
        P(None, None, "frames", "heads"),
        P(),
        P(),
        P(None, None, "frames", "heads"),
        P("heads", None),
    )
    out_specs = P("heads", "frames", None)
    return jax.shard_map(local, mesh=mesh, in_specs=in_specs, out_specs=out_specs, check_vma=False)
```

```python
import functools

import jax
import jax.numpy as jnp
from jax import lax
from jax.experimental import pallas as pl
from jax.experimental.pallas import tpu as pltpu
from jax.sharding import PartitionSpec as P

HEAD_DIM = 128
TILE_ROWS = 16
PART_TILE = 32
HEAD_FIFTHS = ((4, 1), (2, 2), (0, 2))
VMEM_BYTES = 60 * 1024 * 1024


def after(block, *before):
    return lax.optimization_barrier((block, *before))[0] if before else block


def wide(block):
    return block.astype(jnp.float32)


def added(*blocks):
    return functools.reduce(jnp.add, [wide(block) for block in blocks]).astype(jnp.bfloat16)


def in_three(block):
    terms = []
    for _ in range(3):
        term = lax.reduce_precision(block, 8, 7)
        terms.append(term.astype(jnp.bfloat16))
        block = block - term
    return terms


def attend_columns(keys, values, queries, allowed):
    scale = HEAD_DIM ** (-0.5)
    scores = lax.dot_general(
        keys, queries, (((1,), (1,)), ((), ())), preferred_element_type=jnp.float32
    )
    scores = jnp.where(allowed, scores, -jnp.inf)
    peak = jnp.max(scores, axis=0, keepdims=True)
    weights = jnp.exp((scores - peak) * scale)
    totals = jnp.sum(weights, axis=0, keepdims=True)
    gathered = lax.dot_general(
        values, weights.astype(jnp.bfloat16), (((0,), (0,)), ((), ())),
        preferred_element_type=jnp.float32,
    )
    return gathered * (1.0 / totals), peak * scale + jnp.log(totals)


def bank_kernel(banks, live_ref, own_ref, far_ref, *refs):
    bank_refs = refs[:banks]
    head = pl.program_id(0)
    tokens = sum(bank.shape[2] for bank in bank_refs)
    second = lax.broadcasted_iota(jnp.int32, (2 * tokens, own_ref.shape[0]), 0) >= tokens
    for side, query_ref in enumerate((own_ref, far_ref)):
        out_ref, level_ref = refs[banks + 2 * side : banks + 2 * side + 2]
        keys, values = (
            jnp.concatenate([bank[which, 2 * side + slot] for slot in range(2) for bank in bank_refs], axis=0)
            for which in range(2)
        )
        allowed = jnp.logical_or(jnp.logical_not(second), live_ref[side, 1] > 0)
        gathered, level = attend_columns(keys, values, query_ref[...], allowed)
        rows = out_ref.shape[2]
        for part in range(out_ref.shape[0]):
            here = slice(part * rows, (part + 1) * rows)
            out_ref[part] = gathered[:, here].astype(out_ref.dtype)
            level_ref[part, pl.ds(head, 1), :] = level[:, here]


def attend_bank(first, parts, rows, live, own, far, banks):
    width = banks[0].shape[3]
    heads = width // HEAD_DIM
    keys_each = 2 * sum(bank.shape[2] for bank in banks)
    query_spec = pl.BlockSpec((parts * rows, HEAD_DIM), lambda h: (0, first + h))
    out = jax.ShapeDtypeStruct((parts, width, rows), jnp.bfloat16)
    level = jax.ShapeDtypeStruct((parts, heads, rows), jnp.float32)
    out_spec = pl.BlockSpec((parts, HEAD_DIM, rows), lambda h: (0, h, 0))
    level_spec = pl.BlockSpec((parts, heads, rows), lambda h: (0, 0, 0))
    return pl.pallas_call(
        functools.partial(bank_kernel, len(banks)),
        grid=(heads,),
        in_specs=[pl.BlockSpec(memory_space=pltpu.SMEM), query_spec, query_spec]
        + [pl.BlockSpec((*bank.shape[:3], HEAD_DIM), lambda h: (0, 0, 0, h)) for bank in banks],
        out_specs=[out_spec, level_spec] * 2,
        out_shape=[out, level] * 2,
        compiler_params=pltpu.CompilerParams(vmem_limit_bytes=VMEM_BYTES),
        cost_estimate=pl.CostEstimate(
            flops=32 * parts * rows * width * keys_each,
            bytes_accessed=2 * (4 * parts * rows * width + sum(bank.size for bank in banks)),
            transcendentals=2 * parts * rows * heads * keys_each,
        ),
    )(live, own, far, *banks)


def frame_kernel(frames_here, token_ref, out_ref):
    scale = HEAD_DIM ** (-0.5)
    pieces, _, parts, rows, _ = token_ref.shape
    size = pieces * rows
    query_spot = lax.broadcasted_iota(jnp.int32, (size, size), 0) % rows // frames_here
    key_spot = lax.broadcasted_iota(jnp.int32, (size, size), 1) % rows // frames_here
    same_spot = query_spot == key_spot
    for part in range(parts):
        queries, keys, values = (
            jnp.concatenate([token_ref[piece, which, part] for piece in range(pieces)], axis=0)
            for which in range(3)
        )
        scores = lax.dot_general(
            queries, keys, (((1,), (1,)), ((), ())), preferred_element_type=jnp.float32
        )
        scores = jnp.where(same_spot, scores, -jnp.inf)
        weights = jnp.exp((scores - jnp.max(scores, axis=1, keepdims=True)) * scale)
        totals = jnp.sum(weights, axis=1, keepdims=True)
        gathered = jnp.dot(weights.astype(jnp.bfloat16), values, preferred_element_type=jnp.float32)
        gathered = (gathered / totals).astype(out_ref.dtype)
        for piece in range(pieces):
            out_ref[piece, part] = gathered[piece * rows : (piece + 1) * rows]


def attend_frames(frames_here, tokens):
    pieces, _, parts, rows, width = tokens.shape
    return pl.pallas_call(
        functools.partial(frame_kernel, frames_here),
        grid=(width // HEAD_DIM,),
        in_specs=[pl.BlockSpec((pieces, 3, parts, rows, HEAD_DIM), lambda h: (0, 0, 0, 0, h))],
        out_specs=pl.BlockSpec((pieces, parts, rows, HEAD_DIM), lambda h: (0, 0, 0, h)),
        out_shape=jax.ShapeDtypeStruct((pieces, parts, rows, width), jnp.bfloat16),
        compiler_params=pltpu.CompilerParams(vmem_limit_bytes=VMEM_BYTES),
        cost_estimate=pl.CostEstimate(
            flops=16 * parts * (pieces * rows) ** 2 * width,
            bytes_accessed=8 * pieces * parts * rows * width,
            transcendentals=parts * (pieces * rows) ** 2 * width // HEAD_DIM,
        ),
    )(tokens)


def listed_kernel(place_ref, slots_ref, *refs):
    count = len(refs) // 2
    for source, target in zip(refs[:count], refs[count:]):
        target[...] = source[...]


def listed_banks(place, char_slots, char_bank, half, column, group_width):
    _, _, tokens, _ = char_bank.shape
    block = (2, 1, tokens, group_width)

    def source(step):
        def index(entry, place_ref, slots_ref):
            shard = place_ref[0] ^ step ^ (entry // 2 * half)
            return 0, slots_ref[shard * 2 + entry % 2], 0, column

        return pl.BlockSpec(block, index)

    return pl.pallas_call(
        listed_kernel,
        grid_spec=pltpu.PrefetchScalarGridSpec(
            num_scalar_prefetch=2,
            grid=(4,),
            in_specs=[source(step) for step in range(half)],
            out_specs=[pl.BlockSpec(block, lambda entry, *_: (0, entry, 0, 0)) for _ in range(half)],
        ),
        out_shape=[jax.ShapeDtypeStruct((2, 4, tokens, group_width), char_bank.dtype) for _ in range(half)],
        compiler_params=pltpu.CompilerParams(vmem_limit_bytes=VMEM_BYTES),
        cost_estimate=pl.CostEstimate(
            flops=0, bytes_accessed=32 * half * tokens * group_width, transcendentals=0
        ),
    )(place.reshape(1), char_slots.reshape(-1), *[char_bank] * half)


def local(bank_query, char_bank, char_slots, slot_live, frame_tokens, out_weight):
    spatial, frames_here, width = bank_query.shape
    heads_here = width // HEAD_DIM
    head_groups = lax.axis_size("heads")
    shards = lax.axis_size("frames")
    half = shards // 2
    place = lax.axis_index("frames")
    parts = max(1, spatial * frames_here // (PART_TILE * shards))
    across = shards // head_groups
    spots = spatial // (shards * parts)
    tile = spots * frames_here
    rows = shards * tile

    def swap(block, step):
        return lax.ppermute(block, "frames", [(a, a ^ step) for a in range(shards)])

    def by_part(block):
        cut = block.reshape(head_groups, parts, across, spots, frames_here, width)
        return jnp.moveaxis(cut, 1, 0).reshape(parts * rows, width)

    own = by_part(bank_query)
    far = swap(own, half)

    fifth = heads_here // 5
    spans = [(low * fifth, size * fifth) for low, size in HEAD_FIFTHS]
    if heads_here % 5:
        spans = [(0, heads_here)]
    groups = len(spans)

    def banks_of(group, *before):
        first, size = spans[group]
        blocks = listed_banks(
            place, after(char_slots, *before), char_bank, half, first // size, size * HEAD_DIM
        )
        blocks = [blocks[0]] + [swap(blocks[step], step) for step in range(1, half)]
        return blocks if char_bank.shape[2] % TILE_ROWS == 0 else [jnp.concatenate(blocks, axis=2)]

    banks = [banks_of(0)]
    tokens = frame_tokens.reshape(3, head_groups, parts, across, spots, frames_here, width)
    tokens = tokens.transpose(1, 3, 0, 2, 4, 5, 6).reshape(shards, 3, parts, tile, width)
    tokens = lax.all_to_all(after(tokens, far, *banks[0]), "frames", 0, 0, tiled=True)
    live = jnp.stack([slot_live[place], slot_live[place ^ half]])

    place_heads = lax.axis_index("heads")
    chips, core, chip = head_groups // 2, place_heads % 2, place_heads // 2

    def scatter_cores(block):
        block = block.reshape(chips, 2, -1, block.shape[-1])
        give = lax.dynamic_index_in_dim(block, 1 - core, 1, keepdims=False)
        keep = lax.dynamic_index_in_dim(block, core, 1, keepdims=False)
        return added(keep, lax.ppermute(give, "heads", [(h, h ^ 1) for h in range(head_groups)]))

    def scatter_chips(summed):
        parcels = [lax.dynamic_index_in_dim(summed, chip, 0, keepdims=False)]
        for step in range(1, chips):
            give = lax.dynamic_index_in_dim(summed, (chip + step) % chips, 0, keepdims=False)
            parcels.append(
                lax.ppermute(give, "heads", [(h, (h + 2 * step) % head_groups) for h in range(head_groups)])
            )
        return added(*parcels)

    results = []
    for group, (first, _) in enumerate(spans):
        near_out, near_level, far_out, far_level = attend_bank(first, parts, rows, live, own, far, banks[group])
        if group == 0:
            if groups > 1:
                banks.append(banks_of(1, far_level))
            frame_parts = attend_frames(frames_here, after(tokens, far_level))
            back = lax.all_to_all(frame_parts, "frames", 0, 0, tiled=True)
            live = after(live, frame_parts)
            banks += [banks_of(later, tokens) for later in range(2, groups)]
        message = jnp.concatenate([far_out, *in_three(far_level)], axis=1)
        message = jnp.pad(message, ((0, 0), (0, -message.shape[1] % TILE_ROWS), (0, 0)))
        if group < groups - 1:
            got = swap(message, half)
        else:
            got = [swap(message[part], half) for part in range(parts)]
        results.append((near_out, near_level, got))
    results = [
        (near_out, near_level, after(got, results[-1][1]) if group < groups - 1 else got)
        for group, (near_out, near_level, got) in enumerate(results)
    ]

    def share_of(group, part, *before):
        near_out, near_level, got = results[group]
        got = after(got[part], *(before if group == groups - 1 else ()))
        size = spans[group][1]
        deep, split = size * HEAD_DIM, (size, HEAD_DIM, rows)
        got_level = sum(wide(got[low : low + size]) for low in range(deep, deep + 3 * size, size))
        peak = jnp.maximum(near_level[part], got_level)
        near_share, got_share = jnp.exp(near_level[part] - peak), jnp.exp(got_level - peak)
        total = near_share + got_share
        return (
            wide(near_out[part].reshape(split)) * (near_share / total)[:, None, :]
            + wide(got[:deep].reshape(split)) * (got_share / total)[:, None, :]
        )

    in_order = sorted(range(groups), key=lambda group: spans[group][0])
    projected, summed = [], []
    for part in range(parts):
        shares = [share_of(group, part, *projected[-1:]) for group in in_order]
        ref_out = jnp.concatenate(shares, axis=0).reshape(width, rows)
        frame_out = back[:, part].reshape(rows, width)
        combined = (ref_out + wide(frame_out.T)).astype(jnp.bfloat16)
        projected.append(
            lax.dot_general(
                after(combined, *summed[-1:]), out_weight, (((0,), (0,)), ((), ())),
                preferred_element_type=jnp.float32,
            ).astype(jnp.bfloat16)
        )
        summed.append(scatter_cores(projected[-1]))
    pieces = []
    for block in summed:
        pieces.append(scatter_chips(after(block, *pieces[-1:])))
    return jnp.concatenate(pieces, axis=0).reshape(spatial // head_groups, frames_here, -1)


def solution(mesh):
    in_specs = (
        P(None, "frames", "heads"),
        P(None, None, "frames", "heads"),
        P(),
        P(),
        P(None, None, "frames", "heads"),
        P("heads", None),
    )
    out_specs = P("heads", "frames", None)
    return jax.shard_map(local, mesh=mesh, in_specs=in_specs, out_specs=out_specs, check_vma=False)
```

```python
import functools

import jax
import jax.numpy as jnp
from jax import lax
from jax.experimental import pallas as pl
from jax.experimental.pallas import tpu as pltpu
from jax.sharding import PartitionSpec as P

HEAD_DIM = 128
TILE_ROWS = 16
PART_TILE = 32
HEAD_FIFTHS = ((4, 1), (2, 2), (0, 2))
VMEM_BYTES = 60 * 1024 * 1024


def after(block, *before):
    return lax.optimization_barrier((block, *before))[0] if before else block


def wide(block):
    return block.astype(jnp.float32)


def added(*blocks):
    return functools.reduce(jnp.add, [wide(block) for block in blocks]).astype(jnp.bfloat16)


def in_three(block):
    terms = []
    for _ in range(3):
        term = lax.reduce_precision(block, 8, 7)
        terms.append(term.astype(jnp.bfloat16))
        block = block - term
    return terms


def attend_columns(keys, values, queries, allowed):
    scale = HEAD_DIM ** (-0.5)
    scores = lax.dot_general(
        keys, queries, (((1,), (1,)), ((), ())), preferred_element_type=jnp.float32
    )
    scores = jnp.where(allowed, scores, -jnp.inf)
    peak = jnp.max(scores, axis=0, keepdims=True)
    weights = jnp.exp((scores - peak) * scale)
    totals = jnp.sum(weights, axis=0, keepdims=True)
    gathered = lax.dot_general(
        values, weights.astype(jnp.bfloat16), (((0,), (0,)), ((), ())),
        preferred_element_type=jnp.float32,
    )
    return gathered * (1.0 / totals), peak * scale + jnp.log(totals)


def bank_kernel(banks, live_ref, own_ref, far_ref, *refs):
    bank_refs = refs[:banks]
    head = pl.program_id(0)
    tokens = sum(bank.shape[2] for bank in bank_refs)
    second = lax.broadcasted_iota(jnp.int32, (2 * tokens, own_ref.shape[0]), 0) >= tokens
    for side, query_ref in enumerate((own_ref, far_ref)):
        out_ref, level_ref = refs[banks + 2 * side : banks + 2 * side + 2]
        keys, values = (
            jnp.concatenate([bank[which, 2 * side + slot] for slot in range(2) for bank in bank_refs], axis=0)
            for which in range(2)
        )
        allowed = jnp.logical_or(jnp.logical_not(second), live_ref[side, 1] > 0)
        gathered, level = attend_columns(keys, values, query_ref[...], allowed)
        rows = out_ref.shape[2]
        for part in range(out_ref.shape[0]):
            here = slice(part * rows, (part + 1) * rows)
            out_ref[part] = gathered[:, here].astype(out_ref.dtype)
            level_ref[part, pl.ds(head, 1), :] = level[:, here]


def attend_bank(first, parts, rows, live, own, far, banks):
    width = banks[0].shape[3]
    heads = width // HEAD_DIM
    keys_each = 2 * sum(bank.shape[2] for bank in banks)
    query_spec = pl.BlockSpec((parts * rows, HEAD_DIM), lambda h: (0, first + h))
    out = jax.ShapeDtypeStruct((parts, width, rows), jnp.bfloat16)
    level = jax.ShapeDtypeStruct((parts, heads, rows), jnp.float32)
    out_spec = pl.BlockSpec((parts, HEAD_DIM, rows), lambda h: (0, h, 0))
    level_spec = pl.BlockSpec((parts, heads, rows), lambda h: (0, 0, 0))
    return pl.pallas_call(
        functools.partial(bank_kernel, len(banks)),
        grid=(heads,),
        in_specs=[pl.BlockSpec(memory_space=pltpu.SMEM), query_spec, query_spec]
        + [pl.BlockSpec((*bank.shape[:3], HEAD_DIM), lambda h: (0, 0, 0, h)) for bank in banks],
        out_specs=[out_spec, level_spec] * 2,
        out_shape=[out, level] * 2,
        compiler_params=pltpu.CompilerParams(vmem_limit_bytes=VMEM_BYTES),
        cost_estimate=pl.CostEstimate(
            flops=32 * parts * rows * width * keys_each,
            bytes_accessed=2 * (4 * parts * rows * width + sum(bank.size for bank in banks)),
            transcendentals=2 * parts * rows * heads * keys_each,
        ),
    )(live, own, far, *banks)


def frame_kernel(frames_here, token_ref, out_ref):
    scale = HEAD_DIM ** (-0.5)
    pieces, _, parts, rows, _ = token_ref.shape
    size = pieces * rows
    query_spot = lax.broadcasted_iota(jnp.int32, (size, size), 0) % rows // frames_here
    key_spot = lax.broadcasted_iota(jnp.int32, (size, size), 1) % rows // frames_here
    same_spot = query_spot == key_spot
    for part in range(parts):
        queries, keys, values = (
            jnp.concatenate([token_ref[piece, which, part] for piece in range(pieces)], axis=0)
            for which in range(3)
        )
        scores = lax.dot_general(
            queries, keys, (((1,), (1,)), ((), ())), preferred_element_type=jnp.float32
        )
        scores = jnp.where(same_spot, scores, -jnp.inf)
        weights = jnp.exp((scores - jnp.max(scores, axis=1, keepdims=True)) * scale)
        totals = jnp.sum(weights, axis=1, keepdims=True)
        gathered = jnp.dot(weights.astype(jnp.bfloat16), values, preferred_element_type=jnp.float32)
        gathered = (gathered / totals).astype(out_ref.dtype)
        for piece in range(pieces):
            out_ref[piece, part] = gathered[piece * rows : (piece + 1) * rows]


def attend_frames(frames_here, tokens):
    pieces, _, parts, rows, width = tokens.shape
    return pl.pallas_call(
        functools.partial(frame_kernel, frames_here),
        grid=(width // HEAD_DIM,),
        in_specs=[pl.BlockSpec((pieces, 3, parts, rows, HEAD_DIM), lambda h: (0, 0, 0, 0, h))],
        out_specs=pl.BlockSpec((pieces, parts, rows, HEAD_DIM), lambda h: (0, 0, 0, h)),
        out_shape=jax.ShapeDtypeStruct((pieces, parts, rows, width), jnp.bfloat16),
        compiler_params=pltpu.CompilerParams(vmem_limit_bytes=VMEM_BYTES),
        cost_estimate=pl.CostEstimate(
            flops=16 * parts * (pieces * rows) ** 2 * width,
            bytes_accessed=8 * pieces * parts * rows * width,
            transcendentals=parts * (pieces * rows) ** 2 * width // HEAD_DIM,
        ),
    )(tokens)


def listed_kernel(place_ref, slots_ref, *refs):
    count = len(refs) // 2
    for source, target in zip(refs[:count], refs[count:]):
        target[...] = source[...]


def listed_banks(place, char_slots, char_bank, half, column, group_width):
    _, _, tokens, _ = char_bank.shape
    block = (2, 1, tokens, group_width)

    def source(step):
        def index(entry, place_ref, slots_ref):
            shard = place_ref[0] ^ step ^ (entry // 2 * half)
            return 0, slots_ref[shard * 2 + entry % 2], 0, column

        return pl.BlockSpec(block, index)

    return pl.pallas_call(
        listed_kernel,
        grid_spec=pltpu.PrefetchScalarGridSpec(
            num_scalar_prefetch=2,
            grid=(4,),
            in_specs=[source(step) for step in range(half)],
            out_specs=[pl.BlockSpec(block, lambda entry, *_: (0, entry, 0, 0)) for _ in range(half)],
        ),
        out_shape=[jax.ShapeDtypeStruct((2, 4, tokens, group_width), char_bank.dtype) for _ in range(half)],
        compiler_params=pltpu.CompilerParams(vmem_limit_bytes=VMEM_BYTES),
        cost_estimate=pl.CostEstimate(
            flops=0, bytes_accessed=32 * half * tokens * group_width, transcendentals=0
        ),
    )(place.reshape(1), char_slots.reshape(-1), *[char_bank] * half)


def local(bank_query, char_bank, char_slots, slot_live, frame_tokens, out_weight):
    spatial, frames_here, width = bank_query.shape
    heads_here = width // HEAD_DIM
    head_groups = lax.axis_size("heads")
    shards = lax.axis_size("frames")
    half = shards // 2
    place = lax.axis_index("frames")
    parts = max(1, spatial * frames_here // (PART_TILE * shards))
    across = shards // head_groups
    spots = spatial // (shards * parts)
    tile = spots * frames_here
    rows = shards * tile

    def swap(block, step):
        return lax.ppermute(block, "frames", [(a, a ^ step) for a in range(shards)])

    def by_part(block):
        cut = block.reshape(head_groups, parts, across, spots, frames_here, width)
        return jnp.moveaxis(cut, 1, 0).reshape(parts * rows, width)

    own = by_part(bank_query)
    far = swap(own, half)

    fifth = heads_here // 5
    spans = [(low * fifth, size * fifth) for low, size in HEAD_FIFTHS]
    if heads_here % 5:
        spans = [(0, heads_here)]
    groups = len(spans)

    def banks_of(group, before=(), before_near=()):
        first, size = spans[group]
        blocks = listed_banks(
            place, after(char_slots, *before), char_bank, half, first // size, size * HEAD_DIM
        )
        blocks = [blocks[0]] + [
            swap(after(blocks[step], *(before_near if step == 1 else ())), step) for step in range(1, half)
        ]
        return blocks if char_bank.shape[2] % TILE_ROWS == 0 else [jnp.concatenate(blocks, axis=2)]

    banks = [banks_of(0)]
    tokens = frame_tokens.reshape(3, head_groups, parts, across, spots, frames_here, width)
    tokens = tokens.transpose(1, 3, 0, 2, 4, 5, 6).reshape(shards, 3, parts, tile, width)
    tokens = lax.all_to_all(after(tokens, far, *banks[0]), "frames", 0, 0, tiled=True)
    live = jnp.stack([slot_live[place], slot_live[place ^ half]])

    place_heads = lax.axis_index("heads")
    chips, core, chip = head_groups // 2, place_heads % 2, place_heads // 2

    def scatter_cores(block):
        block = block.reshape(chips, 2, -1, block.shape[-1])
        give = lax.dynamic_index_in_dim(block, 1 - core, 1, keepdims=False)
        keep = lax.dynamic_index_in_dim(block, core, 1, keepdims=False)
        return added(keep, lax.ppermute(give, "heads", [(h, h ^ 1) for h in range(head_groups)]))

    def scatter_chips(summed):
        parcels = [lax.dynamic_index_in_dim(summed, chip, 0, keepdims=False)]
        for step in range(1, chips):
            give = lax.dynamic_index_in_dim(summed, (chip + step) % chips, 0, keepdims=False)
            parcels.append(
                lax.ppermute(give, "heads", [(h, (h + 2 * step) % head_groups) for h in range(head_groups)])
            )
        return added(*parcels)

    results = []
    for group, (first, _) in enumerate(spans):
        near_out, near_level, far_out, far_level = attend_bank(first, parts, rows, live, own, far, banks[group])
        if group == 0:
            if groups > 1:
                banks.append(banks_of(1, [far_level]))
                banks += [banks_of(later, [far_level], [tokens]) for later in range(2, groups)]
            frame_parts = attend_frames(frames_here, after(tokens, far_level))
            back = lax.all_to_all(frame_parts, "frames", 0, 0, tiled=True)
            live = after(live, frame_parts)
        message = jnp.concatenate([far_out, *in_three(far_level)], axis=1)
        message = jnp.pad(message, ((0, 0), (0, -message.shape[1] % TILE_ROWS), (0, 0)))
        if group < groups - 1:
            got = swap(message, half)
        else:
            got = [swap(message[part], half) for part in range(parts)]
        results.append((near_out, near_level, got))
    results = [
        (near_out, near_level, after(got, results[-1][1]) if group < groups - 1 else got)
        for group, (near_out, near_level, got) in enumerate(results)
    ]

    def share_of(group, part, *before):
        near_out, near_level, got = results[group]
        got = after(got[part], *(before if group == groups - 1 else ()))
        size = spans[group][1]
        deep, split = size * HEAD_DIM, (size, HEAD_DIM, rows)
        got_level = sum(wide(got[low : low + size]) for low in range(deep, deep + 3 * size, size))
        peak = jnp.maximum(near_level[part], got_level)
        near_share, got_share = jnp.exp(near_level[part] - peak), jnp.exp(got_level - peak)
        total = near_share + got_share
        return (
            wide(near_out[part].reshape(split)) * (near_share / total)[:, None, :]
            + wide(got[:deep].reshape(split)) * (got_share / total)[:, None, :]
        )

    in_order = sorted(range(groups), key=lambda group: spans[group][0])
    projected, summed = [], []
    for part in range(parts):
        shares = [share_of(group, part, *projected[-1:]) for group in in_order]
        ref_out = jnp.concatenate(shares, axis=0).reshape(width, rows)
        frame_out = back[:, part].reshape(rows, width)
        combined = (ref_out + wide(frame_out.T)).astype(jnp.bfloat16)
        projected.append(
            lax.dot_general(
                after(combined, *summed[-1:]), out_weight, (((0,), (0,)), ((), ())),
                preferred_element_type=jnp.float32,
            ).astype(jnp.bfloat16)
        )
        summed.append(scatter_cores(projected[-1]))
    pieces = []
    for block in summed:
        pieces.append(scatter_chips(after(block, *pieces[-1:])))
    return jnp.concatenate(pieces, axis=0).reshape(spatial // head_groups, frames_here, -1)


def solution(mesh):
    in_specs = (
        P(None, "frames", "heads"),
        P(None, None, "frames", "heads"),
        P(),
        P(),
        P(None, None, "frames", "heads"),
        P("heads", None),
    )
    out_specs = P("heads", "frames", None)
    return jax.shard_map(local, mesh=mesh, in_specs=in_specs, out_specs=out_specs, check_vma=False)
```

```python
import functools

import jax
import jax.numpy as jnp
from jax import lax
from jax.experimental import pallas as pl
from jax.experimental.pallas import tpu as pltpu
from jax.sharding import PartitionSpec as P

HEAD_DIM = 128
TILE_ROWS = 16
PART_TILE = 32
HEAD_GROUPS = 2
VMEM_BYTES = 60 * 1024 * 1024


def after(block, *before):
    return lax.optimization_barrier((block, *before))[0] if before else block


def wide(block):
    return block.astype(jnp.float32)


def added(*blocks):
    return functools.reduce(jnp.add, [wide(block) for block in blocks]).astype(jnp.bfloat16)


def in_three(block):
    terms = []
    for _ in range(3):
        term = lax.reduce_precision(block, 8, 7)
        terms.append(term.astype(jnp.bfloat16))
        block = block - term
    return terms


def attend_columns(keys, values, queries, allowed):
    scale = HEAD_DIM ** (-0.5)
    scores = lax.dot_general(
        keys, queries, (((1,), (1,)), ((), ())), preferred_element_type=jnp.float32
    )
    scores = jnp.where(allowed, scores, -jnp.inf)
    peak = jnp.max(scores, axis=0, keepdims=True)
    weights = jnp.exp((scores - peak) * scale)
    totals = jnp.sum(weights, axis=0, keepdims=True)
    gathered = lax.dot_general(
        values, weights.astype(jnp.bfloat16), (((0,), (0,)), ((), ())),
        preferred_element_type=jnp.float32,
    )
    return gathered * (1.0 / totals), peak * scale + jnp.log(totals)


def bank_kernel(banks, live_ref, own_ref, far_ref, *refs):
    bank_refs = refs[:banks]
    head = pl.program_id(0)
    tokens = sum(bank.shape[2] for bank in bank_refs)
    second = lax.broadcasted_iota(jnp.int32, (2 * tokens, own_ref.shape[0]), 0) >= tokens
    for side, query_ref in enumerate((own_ref, far_ref)):
        out_ref, level_ref = refs[banks + 2 * side : banks + 2 * side + 2]
        keys, values = (
            jnp.concatenate([bank[which, 2 * side + slot] for slot in range(2) for bank in bank_refs], axis=0)
            for which in range(2)
        )
        allowed = jnp.logical_or(jnp.logical_not(second), live_ref[side, 1] > 0)
        gathered, level = attend_columns(keys, values, query_ref[...], allowed)
        rows = out_ref.shape[2]
        for part in range(out_ref.shape[0]):
            here = slice(part * rows, (part + 1) * rows)
            out_ref[part] = gathered[:, here].astype(out_ref.dtype)
            level_ref[part, pl.ds(head, 1), :] = level[:, here]


def attend_bank(group, parts, rows, live, own, far, banks):
    width = banks[0].shape[3]
    heads = width // HEAD_DIM
    keys_each = 2 * sum(bank.shape[2] for bank in banks)
    query_spec = pl.BlockSpec((parts * rows, HEAD_DIM), lambda h: (0, group * heads + h))
    out = jax.ShapeDtypeStruct((parts, width, rows), jnp.bfloat16)
    level = jax.ShapeDtypeStruct((parts, heads, rows), jnp.float32)
    out_spec = pl.BlockSpec((parts, HEAD_DIM, rows), lambda h: (0, h, 0))
    level_spec = pl.BlockSpec((parts, heads, rows), lambda h: (0, 0, 0))
    return pl.pallas_call(
        functools.partial(bank_kernel, len(banks)),
        grid=(heads,),
        in_specs=[pl.BlockSpec(memory_space=pltpu.SMEM), query_spec, query_spec]
        + [pl.BlockSpec((*bank.shape[:3], HEAD_DIM), lambda h: (0, 0, 0, h)) for bank in banks],
        out_specs=[out_spec, level_spec] * 2,
        out_shape=[out, level] * 2,
        compiler_params=pltpu.CompilerParams(vmem_limit_bytes=VMEM_BYTES),
        cost_estimate=pl.CostEstimate(
            flops=32 * parts * rows * width * keys_each,
            bytes_accessed=2 * (4 * parts * rows * width + sum(bank.size for bank in banks)),
            transcendentals=2 * parts * rows * heads * keys_each,
        ),
    )(live, own, far, *banks)


def frame_kernel(frames_here, token_ref, out_ref):
    scale = HEAD_DIM ** (-0.5)
    pieces, _, parts, rows, _ = token_ref.shape
    size = pieces * rows
    query_spot = lax.broadcasted_iota(jnp.int32, (size, size), 0) % rows // frames_here
    key_spot = lax.broadcasted_iota(jnp.int32, (size, size), 1) % rows // frames_here
    same_spot = query_spot == key_spot
    for part in range(parts):
        queries, keys, values = (
            jnp.concatenate([token_ref[piece, which, part] for piece in range(pieces)], axis=0)
            for which in range(3)
        )
        scores = lax.dot_general(
            queries, keys, (((1,), (1,)), ((), ())), preferred_element_type=jnp.float32
        )
        scores = jnp.where(same_spot, scores, -jnp.inf)
        weights = jnp.exp((scores - jnp.max(scores, axis=1, keepdims=True)) * scale)
        totals = jnp.sum(weights, axis=1, keepdims=True)
        gathered = jnp.dot(weights.astype(jnp.bfloat16), values, preferred_element_type=jnp.float32)
        gathered = (gathered / totals).astype(out_ref.dtype)
        for piece in range(pieces):
            out_ref[piece, part] = gathered[piece * rows : (piece + 1) * rows]


def attend_frames(frames_here, tokens):
    pieces, _, parts, rows, width = tokens.shape
    return pl.pallas_call(
        functools.partial(frame_kernel, frames_here),
        grid=(width // HEAD_DIM,),
        in_specs=[pl.BlockSpec((pieces, 3, parts, rows, HEAD_DIM), lambda h: (0, 0, 0, 0, h))],
        out_specs=pl.BlockSpec((pieces, parts, rows, HEAD_DIM), lambda h: (0, 0, 0, h)),
        out_shape=jax.ShapeDtypeStruct((pieces, parts, rows, width), jnp.bfloat16),
        compiler_params=pltpu.CompilerParams(vmem_limit_bytes=VMEM_BYTES),
        cost_estimate=pl.CostEstimate(
            flops=16 * parts * (pieces * rows) ** 2 * width,
            bytes_accessed=8 * pieces * parts * rows * width,
            transcendentals=parts * (pieces * rows) ** 2 * width // HEAD_DIM,
        ),
    )(tokens)


def listed_kernel(place_ref, slots_ref, *refs):
    count = len(refs) // 2
    for source, target in zip(refs[:count], refs[count:]):
        target[...] = source[...]


def listed_banks(place, char_slots, char_bank, half, group, group_width):
    _, _, tokens, _ = char_bank.shape
    block = (2, 1, tokens, group_width)

    def source(step):
        def index(entry, place_ref, slots_ref):
            shard = place_ref[0] ^ step ^ (entry // 2 * half)
            return 0, slots_ref[shard * 2 + entry % 2], 0, group

        return pl.BlockSpec(block, index)

    return pl.pallas_call(
        listed_kernel,
        grid_spec=pltpu.PrefetchScalarGridSpec(
            num_scalar_prefetch=2,
            grid=(4,),
            in_specs=[source(step) for step in range(half)],
            out_specs=[pl.BlockSpec(block, lambda entry, *_: (0, entry, 0, 0)) for _ in range(half)],
        ),
        out_shape=[jax.ShapeDtypeStruct((2, 4, tokens, group_width), char_bank.dtype) for _ in range(half)],
        compiler_params=pltpu.CompilerParams(vmem_limit_bytes=VMEM_BYTES),
        cost_estimate=pl.CostEstimate(
            flops=0, bytes_accessed=32 * half * tokens * group_width, transcendentals=0
        ),
    )(place.reshape(1), char_slots.reshape(-1), *[char_bank] * half)


def local(bank_query, char_bank, char_slots, slot_live, frame_tokens, out_weight):
    spatial, frames_here, width = bank_query.shape
    heads_here = width // HEAD_DIM
    head_groups = lax.axis_size("heads")
    shards = lax.axis_size("frames")
    half = shards // 2
    place = lax.axis_index("frames")
    parts = max(1, spatial * frames_here // (PART_TILE * shards))
    across = shards // head_groups
    spots = spatial // (shards * parts)
    tile = spots * frames_here
    rows = shards * tile

    def swap(block, step):
        return lax.ppermute(block, "frames", [(a, a ^ step) for a in range(shards)])

    def by_part(block):
        cut = block.reshape(head_groups, parts, across, spots, frames_here, width)
        return jnp.moveaxis(cut, 1, 0).reshape(parts * rows, width)

    own = by_part(bank_query)
    far = swap(own, half)

    groups = HEAD_GROUPS if heads_here % HEAD_GROUPS == 0 else 1

    def banks_of(group, *before):
        blocks = listed_banks(
            place, after(char_slots, *before), char_bank, half, group, width // groups
        )
        blocks = [blocks[0]] + [swap(blocks[step], step) for step in range(1, half)]
        return blocks if char_bank.shape[2] % TILE_ROWS == 0 else [jnp.concatenate(blocks, axis=2)]

    banks = [banks_of(0)]
    tokens = frame_tokens.reshape(3, head_groups, parts, across, spots, frames_here, width)
    tokens = tokens.transpose(1, 3, 0, 2, 4, 5, 6).reshape(shards, 3, parts, tile, width)
    tokens = lax.all_to_all(after(tokens, far, *banks[0][:-1]), "frames", 0, 0, tiled=True)
    live = jnp.stack([slot_live[place], slot_live[place ^ half]])

    place_heads = lax.axis_index("heads")
    chips, core, chip = head_groups // 2, place_heads % 2, place_heads // 2

    def scatter_cores(block):
        block = block.reshape(chips, 2, -1, block.shape[-1])
        give = lax.dynamic_index_in_dim(block, 1 - core, 1, keepdims=False)
        keep = lax.dynamic_index_in_dim(block, core, 1, keepdims=False)
        return added(keep, lax.ppermute(give, "heads", [(h, h ^ 1) for h in range(head_groups)]))

    def scatter_chips(summed):
        parcels = [lax.dynamic_index_in_dim(summed, chip, 0, keepdims=False)]
        for step in range(1, chips):
            give = lax.dynamic_index_in_dim(summed, (chip + step) % chips, 0, keepdims=False)
            parcels.append(
                lax.ppermute(give, "heads", [(h, (h + 2 * step) % head_groups) for h in range(head_groups)])
            )
        return added(*parcels)

    split = (heads_here // groups, HEAD_DIM, rows)
    results = []
    for group in range(groups):
        near_out, near_level, far_out, far_level = attend_bank(group, parts, rows, live, own, far, banks[group])
        if group < groups - 1:
            banks.append(banks_of(group + 1, *banks[0][-2:-1]))
        if group == 0:
            frame_parts = attend_frames(frames_here, after(tokens, far_level))
            back = lax.all_to_all(frame_parts, "frames", 0, 0, tiled=True)
            live = after(live, frame_parts)
        message = jnp.concatenate([far_out, *in_three(far_level)], axis=1)
        message = jnp.pad(message, ((0, 0), (0, -message.shape[1] % TILE_ROWS), (0, 0)))
        if group < groups - 1:
            got = swap(message, half)
        else:
            got = [swap(message[part], half) for part in range(parts)]
        results.append((near_out, near_level, got))
    results = [
        (near_out, near_level, after(got, results[-1][1]) if group < groups - 1 else got)
        for group, (near_out, near_level, got) in enumerate(results)
    ]

    def share_of(group, part, *before):
        near_out, near_level, got = results[group]
        got = after(got[part], *(before if group == groups - 1 else ()))
        size = heads_here // groups
        got_level = sum(wide(got[low : low + size]) for low in range(width // groups, width // groups + 3 * size, size))
        peak = jnp.maximum(near_level[part], got_level)
        near_share, got_share = jnp.exp(near_level[part] - peak), jnp.exp(got_level - peak)
        total = near_share + got_share
        return (
            wide(near_out[part].reshape(split)) * (near_share / total)[:, None, :]
            + wide(got[: width // groups].reshape(split)) * (got_share / total)[:, None, :]
        )

    projected, summed = [], []
    for part in range(parts):
        shares = [share_of(group, part, *projected[-1:]) for group in range(groups)]
        ref_out = jnp.concatenate(shares, axis=0).reshape(width, rows)
        frame_out = back[:, part].reshape(rows, width)
        combined = (ref_out + wide(frame_out.T)).astype(jnp.bfloat16)
        projected.append(
            lax.dot_general(
                after(combined, *summed[-1:]), out_weight, (((0,), (0,)), ((), ())),
                preferred_element_type=jnp.float32,
            ).astype(jnp.bfloat16)
        )
        summed.append(scatter_cores(projected[-1]))
    pieces = []
    for block in summed:
        pieces.append(scatter_chips(after(block, *pieces[-1:])))
    return jnp.concatenate(pieces, axis=0).reshape(spatial // head_groups, frames_here, -1)


def solution(mesh):
    in_specs = (
        P(None, "frames", "heads"),
        P(None, None, "frames", "heads"),
        P(),
        P(),
        P(None, None, "frames", "heads"),
        P("heads", None),
    )
    out_specs = P("heads", "frames", None)
    return jax.shard_map(local, mesh=mesh, in_specs=in_specs, out_specs=out_specs, check_vma=False)
```

```python
import functools

import jax
import jax.numpy as jnp
from jax import lax
from jax.experimental import pallas as pl
from jax.experimental.pallas import tpu as pltpu
from jax.sharding import PartitionSpec as P

HEAD_DIM = 128
TILE_ROWS = 16
PART_TILE = 32
HEAD_GROUPS = 2
VMEM_BYTES = 60 * 1024 * 1024


def after(block, *before):
    return lax.optimization_barrier((block, *before))[0] if before else block


def wide(block):
    return block.astype(jnp.float32)


def added(*blocks):
    return functools.reduce(jnp.add, [wide(block) for block in blocks]).astype(jnp.bfloat16)


def in_three(block):
    terms = []
    for _ in range(3):
        term = lax.reduce_precision(block, 8, 7)
        terms.append(term.astype(jnp.bfloat16))
        block = block - term
    return terms


def attend_columns(keys, values, queries, allowed):
    scale = HEAD_DIM ** (-0.5)
    scores = lax.dot_general(
        keys, queries, (((1,), (1,)), ((), ())), preferred_element_type=jnp.float32
    )
    scores = jnp.where(allowed, scores, -jnp.inf)
    peak = jnp.max(scores, axis=0, keepdims=True)
    weights = jnp.exp((scores - peak) * scale)
    totals = jnp.sum(weights, axis=0, keepdims=True)
    gathered = lax.dot_general(
        values, weights.astype(jnp.bfloat16), (((0,), (0,)), ((), ())),
        preferred_element_type=jnp.float32,
    )
    return gathered * (1.0 / totals), peak * scale + jnp.log(totals)


def bank_kernel(banks, live_ref, own_ref, far_ref, *refs):
    bank_refs = refs[:banks]
    head = pl.program_id(0)
    tokens = sum(bank.shape[2] for bank in bank_refs)
    second = lax.broadcasted_iota(jnp.int32, (2 * tokens, own_ref.shape[0]), 0) >= tokens
    for side, query_ref in enumerate((own_ref, far_ref)):
        out_ref, level_ref = refs[banks + 2 * side : banks + 2 * side + 2]
        keys, values = (
            jnp.concatenate([bank[which, 2 * side + slot] for slot in range(2) for bank in bank_refs], axis=0)
            for which in range(2)
        )
        allowed = jnp.logical_or(jnp.logical_not(second), live_ref[side, 1] > 0)
        gathered, level = attend_columns(keys, values, query_ref[...], allowed)
        rows = out_ref.shape[2]
        for part in range(out_ref.shape[0]):
            here = slice(part * rows, (part + 1) * rows)
            out_ref[part] = gathered[:, here].astype(out_ref.dtype)
            level_ref[part, pl.ds(head, 1), :] = level[:, here]


def attend_bank(group, parts, rows, live, own, far, banks):
    width = banks[0].shape[3]
    heads = width // HEAD_DIM
    keys_each = 2 * sum(bank.shape[2] for bank in banks)
    query_spec = pl.BlockSpec((parts * rows, HEAD_DIM), lambda h: (0, group * heads + h))
    out = jax.ShapeDtypeStruct((parts, width, rows), jnp.bfloat16)
    level = jax.ShapeDtypeStruct((parts, heads, rows), jnp.float32)
    out_spec = pl.BlockSpec((parts, HEAD_DIM, rows), lambda h: (0, h, 0))
    level_spec = pl.BlockSpec((parts, heads, rows), lambda h: (0, 0, 0))
    return pl.pallas_call(
        functools.partial(bank_kernel, len(banks)),
        grid=(heads,),
        in_specs=[pl.BlockSpec(memory_space=pltpu.SMEM), query_spec, query_spec]
        + [pl.BlockSpec((*bank.shape[:3], HEAD_DIM), lambda h: (0, 0, 0, h)) for bank in banks],
        out_specs=[out_spec, level_spec] * 2,
        out_shape=[out, level] * 2,
        compiler_params=pltpu.CompilerParams(vmem_limit_bytes=VMEM_BYTES),
        cost_estimate=pl.CostEstimate(
            flops=32 * parts * rows * width * keys_each,
            bytes_accessed=2 * (4 * parts * rows * width + sum(bank.size for bank in banks)),
            transcendentals=2 * parts * rows * heads * keys_each,
        ),
    )(live, own, far, *banks)


def frame_kernel(frames_here, token_ref, out_ref):
    scale = HEAD_DIM ** (-0.5)
    pieces, _, parts, rows, _ = token_ref.shape
    size = pieces * rows
    query_spot = lax.broadcasted_iota(jnp.int32, (size, size), 0) % rows // frames_here
    key_spot = lax.broadcasted_iota(jnp.int32, (size, size), 1) % rows // frames_here
    same_spot = query_spot == key_spot
    for part in range(parts):
        queries, keys, values = (
            jnp.concatenate([token_ref[piece, which, part] for piece in range(pieces)], axis=0)
            for which in range(3)
        )
        scores = lax.dot_general(
            queries, keys, (((1,), (1,)), ((), ())), preferred_element_type=jnp.float32
        )
        scores = jnp.where(same_spot, scores, -jnp.inf)
        weights = jnp.exp((scores - jnp.max(scores, axis=1, keepdims=True)) * scale)
        totals = jnp.sum(weights, axis=1, keepdims=True)
        gathered = jnp.dot(weights.astype(jnp.bfloat16), values, preferred_element_type=jnp.float32)
        gathered = (gathered / totals).astype(out_ref.dtype)
        for piece in range(pieces):
            out_ref[piece, part] = gathered[piece * rows : (piece + 1) * rows]


def attend_frames(frames_here, tokens):
    pieces, _, parts, rows, width = tokens.shape
    return pl.pallas_call(
        functools.partial(frame_kernel, frames_here),
        grid=(width // HEAD_DIM,),
        in_specs=[pl.BlockSpec((pieces, 3, parts, rows, HEAD_DIM), lambda h: (0, 0, 0, 0, h))],
        out_specs=pl.BlockSpec((pieces, parts, rows, HEAD_DIM), lambda h: (0, 0, 0, h)),
        out_shape=jax.ShapeDtypeStruct((pieces, parts, rows, width), jnp.bfloat16),
        compiler_params=pltpu.CompilerParams(vmem_limit_bytes=VMEM_BYTES),
        cost_estimate=pl.CostEstimate(
            flops=16 * parts * (pieces * rows) ** 2 * width,
            bytes_accessed=8 * pieces * parts * rows * width,
            transcendentals=parts * (pieces * rows) ** 2 * width // HEAD_DIM,
        ),
    )(tokens)


def listed_kernel(place_ref, slots_ref, *refs):
    count = len(refs) // 2
    for source, target in zip(refs[:count], refs[count:]):
        target[...] = source[...]


def listed_banks(place, char_slots, char_bank, half, group, group_width):
    _, _, tokens, _ = char_bank.shape
    block = (2, 1, tokens, group_width)

    def source(step):
        def index(entry, place_ref, slots_ref):
            shard = place_ref[0] ^ step ^ (entry // 2 * half)
            return 0, slots_ref[shard * 2 + entry % 2], 0, group

        return pl.BlockSpec(block, index)

    return pl.pallas_call(
        listed_kernel,
        grid_spec=pltpu.PrefetchScalarGridSpec(
            num_scalar_prefetch=2,
            grid=(4,),
            in_specs=[source(step) for step in range(half)],
            out_specs=[pl.BlockSpec(block, lambda entry, *_: (0, entry, 0, 0)) for _ in range(half)],
        ),
        out_shape=[jax.ShapeDtypeStruct((2, 4, tokens, group_width), char_bank.dtype) for _ in range(half)],
        compiler_params=pltpu.CompilerParams(vmem_limit_bytes=VMEM_BYTES),
        cost_estimate=pl.CostEstimate(
            flops=0, bytes_accessed=32 * half * tokens * group_width, transcendentals=0
        ),
    )(place.reshape(1), char_slots.reshape(-1), *[char_bank] * half)


def local(bank_query, char_bank, char_slots, slot_live, frame_tokens, out_weight):
    spatial, frames_here, width = bank_query.shape
    heads_here = width // HEAD_DIM
    head_groups = lax.axis_size("heads")
    shards = lax.axis_size("frames")
    half = shards // 2
    place = lax.axis_index("frames")
    parts = max(1, spatial * frames_here // (PART_TILE * shards))
    across = shards // head_groups
    spots = spatial // (shards * parts)
    tile = spots * frames_here
    rows = shards * tile

    def swap(block, step):
        return lax.ppermute(block, "frames", [(a, a ^ step) for a in range(shards)])

    def by_part(block):
        cut = block.reshape(head_groups, parts, across, spots, frames_here, width)
        return jnp.moveaxis(cut, 1, 0).reshape(parts * rows, width)

    own = by_part(bank_query)
    far = swap(own, half)

    groups = HEAD_GROUPS if heads_here % HEAD_GROUPS == 0 else 1

    def banks_of(group, *before):
        blocks = listed_banks(
            place, after(char_slots, *before), char_bank, half, group, width // groups
        )
        blocks = [blocks[0]] + [swap(blocks[step], step) for step in range(1, half)]
        return blocks if char_bank.shape[2] % TILE_ROWS == 0 else [jnp.concatenate(blocks, axis=2)]

    banks = [banks_of(0)]
    tokens = frame_tokens.reshape(3, head_groups, parts, across, spots, frames_here, width)
    tokens = tokens.transpose(1, 3, 0, 2, 4, 5, 6).reshape(shards, 3, parts, tile, width)
    tokens = lax.all_to_all(after(tokens, far, *banks[0]), "frames", 0, 0, tiled=True)
    live = jnp.stack([slot_live[place], slot_live[place ^ half]])

    place_heads = lax.axis_index("heads")
    chips, core, chip = head_groups // 2, place_heads % 2, place_heads // 2

    def scatter_cores(block):
        block = block.reshape(chips, 2, -1, block.shape[-1])
        give = lax.dynamic_index_in_dim(block, 1 - core, 1, keepdims=False)
        keep = lax.dynamic_index_in_dim(block, core, 1, keepdims=False)
        return added(keep, lax.ppermute(give, "heads", [(h, h ^ 1) for h in range(head_groups)]))

    def scatter_chips(summed):
        parcels = [lax.dynamic_index_in_dim(summed, chip, 0, keepdims=False)]
        for step in range(1, chips):
            give = lax.dynamic_index_in_dim(summed, (chip + step) % chips, 0, keepdims=False)
            parcels.append(
                lax.ppermute(give, "heads", [(h, (h + 2 * step) % head_groups) for h in range(head_groups)])
            )
        return added(*parcels)

    split = (heads_here // groups, HEAD_DIM, rows)
    results = []
    for group in range(groups):
        near_out, near_level, far_out, far_level = attend_bank(group, parts, rows, live, own, far, banks[group])
        if group < groups - 1:
            banks.append(banks_of(group + 1, far_level))
        if group == 0:
            frame_parts = attend_frames(frames_here, after(tokens, far_level))
            back = lax.all_to_all(frame_parts, "frames", 0, 0, tiled=True)
            live = after(live, frame_parts)
        message = jnp.concatenate([far_out, *in_three(far_level)], axis=1)
        message = jnp.pad(message, ((0, 0), (0, -message.shape[1] % TILE_ROWS), (0, 0)))
        if group < groups - 1:
            got = swap(message, half)
            live = after(live, got)
        else:
            got = [swap(message[part], half) for part in range(parts)]
        results.append((near_out, near_level, got))
    results = [
        (near_out, near_level, after(got, results[-1][1]) if group < groups - 1 else got)
        for group, (near_out, near_level, got) in enumerate(results)
    ]

    def share_of(group, part, *before):
        near_out, near_level, got = results[group]
        got = after(got[part], *(before if group == groups - 1 else ()))
        size = heads_here // groups
        got_level = sum(wide(got[low : low + size]) for low in range(width // groups, width // groups + 3 * size, size))
        peak = jnp.maximum(near_level[part], got_level)
        near_share, got_share = jnp.exp(near_level[part] - peak), jnp.exp(got_level - peak)
        total = near_share + got_share
        return (
            wide(near_out[part].reshape(split)) * (near_share / total)[:, None, :]
            + wide(got[: width // groups].reshape(split)) * (got_share / total)[:, None, :]
        )

    def project(group, part, before, before_dot):
        low, high = group * width // groups, (group + 1) * width // groups
        frame_out = back[:, part].reshape(rows, width)[:, low:high]
        combined = share_of(group, part, *before).reshape(width // groups, rows) + wide(frame_out.T)
        return lax.dot_general(
            after(combined.astype(jnp.bfloat16), *before_dot), out_weight[low:high],
            (((0,), (0,)), ((), ())), preferred_element_type=jnp.float32,
        )

    early = [[project(group, part, (), ()) for group in range(groups - 1)] for part in range(parts)]
    projected, summed, pieces = [], [], []
    for part in range(parts):
        before = [term for terms in early for term in terms] if part == 0 else projected[-1:]
        total = project(groups - 1, part, before, summed[-1:])
        projected.append(functools.reduce(jnp.add, [*early[part], total]).astype(jnp.bfloat16))
        summed.append(scatter_cores(projected[-1]))
    for block in summed:
        pieces.append(scatter_chips(after(block, *pieces[-1:])))
    return jnp.concatenate(pieces, axis=0).reshape(spatial // head_groups, frames_here, -1)


def solution(mesh):
    in_specs = (
        P(None, "frames", "heads"),
        P(None, None, "frames", "heads"),
        P(),
        P(),
        P(None, None, "frames", "heads"),
        P("heads", None),
    )
    out_specs = P("heads", "frames", None)
    return jax.shard_map(local, mesh=mesh, in_specs=in_specs, out_specs=out_specs, check_vma=False)
```

```python
import functools

import jax
import jax.numpy as jnp
from jax import lax
from jax.experimental import pallas as pl
from jax.experimental.pallas import tpu as pltpu
from jax.sharding import PartitionSpec as P

HEAD_DIM = 128
TILE_ROWS = 16
PART_TILE = 32
COLUMN_CUTS = 2
HEAD_GROUPS = 2
VMEM_BYTES = 60 * 1024 * 1024


def after(block, *before):
    return lax.optimization_barrier((block, *before))[0] if before else block


def wide(block):
    return block.astype(jnp.float32)


def added(*blocks):
    return functools.reduce(jnp.add, [wide(block) for block in blocks]).astype(jnp.bfloat16)


def in_three(block):
    terms = []
    for _ in range(3):
        term = lax.reduce_precision(block, 8, 7)
        terms.append(term.astype(jnp.bfloat16))
        block = block - term
    return terms


def attend_columns(keys, values, queries, allowed):
    scale = HEAD_DIM ** (-0.5)
    scores = lax.dot_general(
        keys, queries, (((1,), (1,)), ((), ())), preferred_element_type=jnp.float32
    )
    scores = jnp.where(allowed, scores, -jnp.inf)
    peak = jnp.max(scores, axis=0, keepdims=True)
    weights = jnp.exp((scores - peak) * scale)
    totals = jnp.sum(weights, axis=0, keepdims=True)
    gathered = lax.dot_general(
        values, weights.astype(jnp.bfloat16), (((0,), (0,)), ((), ())),
        preferred_element_type=jnp.float32,
    )
    return gathered * (1.0 / totals), peak * scale + jnp.log(totals)


def bank_kernel(banks, live_ref, own_ref, far_ref, *refs):
    bank_refs = refs[:banks]
    head = pl.program_id(0)
    tokens = sum(bank.shape[2] for bank in bank_refs)
    second = lax.broadcasted_iota(jnp.int32, (2 * tokens, own_ref.shape[0]), 0) >= tokens
    for side, query_ref in enumerate((own_ref, far_ref)):
        out_ref, level_ref = refs[banks + 2 * side : banks + 2 * side + 2]
        keys, values = (
            jnp.concatenate([bank[which, 2 * side + slot] for slot in range(2) for bank in bank_refs], axis=0)
            for which in range(2)
        )
        allowed = jnp.logical_or(jnp.logical_not(second), live_ref[side, 1] > 0)
        gathered, level = attend_columns(keys, values, query_ref[...], allowed)
        rows = out_ref.shape[2]
        for part in range(out_ref.shape[0]):
            here = slice(part * rows, (part + 1) * rows)
            out_ref[part] = gathered[:, here].astype(out_ref.dtype)
            level_ref[part, pl.ds(head, 1), :] = level[:, here]


def attend_bank(group, parts, rows, live, own, far, banks):
    width = banks[0].shape[3]
    heads = width // HEAD_DIM
    keys_each = 2 * sum(bank.shape[2] for bank in banks)
    query_spec = pl.BlockSpec((parts * rows, HEAD_DIM), lambda h: (0, group * heads + h))
    out = jax.ShapeDtypeStruct((parts, width, rows), jnp.bfloat16)
    level = jax.ShapeDtypeStruct((parts, heads, rows), jnp.float32)
    out_spec = pl.BlockSpec((parts, HEAD_DIM, rows), lambda h: (0, h, 0))
    level_spec = pl.BlockSpec((parts, heads, rows), lambda h: (0, 0, 0))
    return pl.pallas_call(
        functools.partial(bank_kernel, len(banks)),
        grid=(heads,),
        in_specs=[pl.BlockSpec(memory_space=pltpu.SMEM), query_spec, query_spec]
        + [pl.BlockSpec((*bank.shape[:3], HEAD_DIM), lambda h: (0, 0, 0, h)) for bank in banks],
        out_specs=[out_spec, level_spec] * 2,
        out_shape=[out, level] * 2,
        compiler_params=pltpu.CompilerParams(vmem_limit_bytes=VMEM_BYTES),
        cost_estimate=pl.CostEstimate(
            flops=32 * parts * rows * width * keys_each,
            bytes_accessed=2 * (4 * parts * rows * width + sum(bank.size for bank in banks)),
            transcendentals=2 * parts * rows * heads * keys_each,
        ),
    )(live, own, far, *banks)


def frame_kernel(frames_here, token_ref, out_ref):
    scale = HEAD_DIM ** (-0.5)
    pieces, _, parts, rows, _ = token_ref.shape
    size = pieces * rows
    query_spot = lax.broadcasted_iota(jnp.int32, (size, size), 0) % rows // frames_here
    key_spot = lax.broadcasted_iota(jnp.int32, (size, size), 1) % rows // frames_here
    same_spot = query_spot == key_spot
    for part in range(parts):
        queries, keys, values = (
            jnp.concatenate([token_ref[piece, which, part] for piece in range(pieces)], axis=0)
            for which in range(3)
        )
        scores = lax.dot_general(
            queries, keys, (((1,), (1,)), ((), ())), preferred_element_type=jnp.float32
        )
        scores = jnp.where(same_spot, scores, -jnp.inf)
        weights = jnp.exp((scores - jnp.max(scores, axis=1, keepdims=True)) * scale)
        totals = jnp.sum(weights, axis=1, keepdims=True)
        gathered = jnp.dot(weights.astype(jnp.bfloat16), values, preferred_element_type=jnp.float32)
        gathered = (gathered / totals).astype(out_ref.dtype)
        for piece in range(pieces):
            out_ref[piece, part] = gathered[piece * rows : (piece + 1) * rows]


def attend_frames(frames_here, tokens):
    pieces, _, parts, rows, width = tokens.shape
    return pl.pallas_call(
        functools.partial(frame_kernel, frames_here),
        grid=(width // HEAD_DIM,),
        in_specs=[pl.BlockSpec((pieces, 3, parts, rows, HEAD_DIM), lambda h: (0, 0, 0, 0, h))],
        out_specs=pl.BlockSpec((pieces, parts, rows, HEAD_DIM), lambda h: (0, 0, 0, h)),
        out_shape=jax.ShapeDtypeStruct((pieces, parts, rows, width), jnp.bfloat16),
        compiler_params=pltpu.CompilerParams(vmem_limit_bytes=VMEM_BYTES),
        cost_estimate=pl.CostEstimate(
            flops=16 * parts * (pieces * rows) ** 2 * width,
            bytes_accessed=8 * pieces * parts * rows * width,
            transcendentals=parts * (pieces * rows) ** 2 * width // HEAD_DIM,
        ),
    )(tokens)


def listed_kernel(place_ref, slots_ref, *refs):
    count = len(refs) // 2
    for source, target in zip(refs[:count], refs[count:]):
        target[...] = source[...]


def listed_banks(place, char_slots, char_bank, half, group, group_width):
    _, _, tokens, _ = char_bank.shape
    block = (2, 1, tokens, group_width)

    def source(step):
        def index(entry, place_ref, slots_ref):
            shard = place_ref[0] ^ step ^ (entry // 2 * half)
            return 0, slots_ref[shard * 2 + entry % 2], 0, group

        return pl.BlockSpec(block, index)

    return pl.pallas_call(
        listed_kernel,
        grid_spec=pltpu.PrefetchScalarGridSpec(
            num_scalar_prefetch=2,
            grid=(4,),
            in_specs=[source(step) for step in range(half)],
            out_specs=[pl.BlockSpec(block, lambda entry, *_: (0, entry, 0, 0)) for _ in range(half)],
        ),
        out_shape=[jax.ShapeDtypeStruct((2, 4, tokens, group_width), char_bank.dtype) for _ in range(half)],
        compiler_params=pltpu.CompilerParams(vmem_limit_bytes=VMEM_BYTES),
        cost_estimate=pl.CostEstimate(
            flops=0, bytes_accessed=32 * half * tokens * group_width, transcendentals=0
        ),
    )(place.reshape(1), char_slots.reshape(-1), *[char_bank] * half)


def local(bank_query, char_bank, char_slots, slot_live, frame_tokens, out_weight):
    spatial, frames_here, width = bank_query.shape
    heads_here = width // HEAD_DIM
    head_groups = lax.axis_size("heads")
    shards = lax.axis_size("frames")
    half = shards // 2
    place = lax.axis_index("frames")
    parts = max(1, spatial * frames_here // (PART_TILE * shards))
    across = shards // head_groups
    spots = spatial // (shards * parts)
    tile = spots * frames_here
    rows = shards * tile

    def swap(block, step):
        return lax.ppermute(block, "frames", [(a, a ^ step) for a in range(shards)])

    def by_part(block):
        cut = block.reshape(head_groups, parts, across, spots, frames_here, width)
        return jnp.moveaxis(cut, 1, 0).reshape(parts * rows, width)

    own = by_part(bank_query)
    far = swap(own, half)

    groups = HEAD_GROUPS if heads_here % HEAD_GROUPS == 0 else 1

    def banks_of(group, *before):
        blocks = listed_banks(
            place, after(char_slots, *before), char_bank, half, group, width // groups
        )
        blocks = [blocks[0]] + [swap(blocks[step], step) for step in range(1, half)]
        return blocks if char_bank.shape[2] % TILE_ROWS == 0 else [jnp.concatenate(blocks, axis=2)]

    banks = [banks_of(0)]
    tokens = frame_tokens.reshape(3, head_groups, parts, across, spots, frames_here, width)
    tokens = tokens.transpose(1, 3, 0, 2, 4, 5, 6).reshape(shards, 3, parts, tile, width)
    tokens = lax.all_to_all(after(tokens, far, *banks[0]), "frames", 0, 0, tiled=True)
    live = jnp.stack([slot_live[place], slot_live[place ^ half]])

    place_heads = lax.axis_index("heads")
    chips, core, chip = head_groups // 2, place_heads % 2, place_heads // 2

    def scatter_cores(block):
        block = block.reshape(chips, 2, -1, block.shape[-1])
        give = lax.dynamic_index_in_dim(block, 1 - core, 1, keepdims=False)
        keep = lax.dynamic_index_in_dim(block, core, 1, keepdims=False)
        return added(keep, lax.ppermute(give, "heads", [(h, h ^ 1) for h in range(head_groups)]))

    def scatter_chips(summed):
        parcels = [lax.dynamic_index_in_dim(summed, chip, 0, keepdims=False)]
        for step in range(1, chips):
            give = lax.dynamic_index_in_dim(summed, (chip + step) % chips, 0, keepdims=False)
            parcels.append(
                lax.ppermute(give, "heads", [(h, (h + 2 * step) % head_groups) for h in range(head_groups)])
            )
        return added(*parcels)

    split = (heads_here // groups, HEAD_DIM, rows)
    results = []
    for group in range(groups):
        near_out, near_level, far_out, far_level = attend_bank(group, parts, rows, live, own, far, banks[group])
        if group < groups - 1:
            banks.append(banks_of(group + 1, far_level))
        if group == 0:
            frame_parts = attend_frames(frames_here, after(tokens, far_level))
            back = lax.all_to_all(frame_parts, "frames", 0, 0, tiled=True)
            live = after(live, frame_parts)
        message = jnp.concatenate([far_out, *in_three(far_level)], axis=1)
        message = jnp.pad(message, ((0, 0), (0, -message.shape[1] % TILE_ROWS), (0, 0)))
        if group < groups - 1:
            got = swap(message, half)
        else:
            got = [swap(message[part], half) for part in range(parts)]
        results.append((near_out, near_level, got))
    results = [
        (near_out, near_level, after(got, results[-1][1]) if group < groups - 1 else got)
        for group, (near_out, near_level, got) in enumerate(results)
    ]

    def share_of(group, part, *before):
        near_out, near_level, got = results[group]
        got = after(got[part], *(before if group == groups - 1 else ()))
        size = heads_here // groups
        got_level = sum(wide(got[low : low + size]) for low in range(width // groups, width // groups + 3 * size, size))
        peak = jnp.maximum(near_level[part], got_level)
        near_share, got_share = jnp.exp(near_level[part] - peak), jnp.exp(got_level - peak)
        total = near_share + got_share
        return (
            wide(near_out[part].reshape(split)) * (near_share / total)[:, None, :]
            + wide(got[: width // groups].reshape(split)) * (got_share / total)[:, None, :]
        )

    projected, summed, pieces = [], [], []
    cut = out_weight.shape[1] // COLUMN_CUTS
    for part in range(parts):
        shares = [share_of(group, part, *projected[-1:], *summed[-2:-1]) for group in range(groups)]
        ref_out = jnp.concatenate(shares, axis=0).reshape(width, rows)
        frame_out = back[:, part].reshape(rows, width)
        combined = (ref_out + wide(frame_out.T)).astype(jnp.bfloat16)
        for low in range(0, cut * COLUMN_CUTS, cut):
            projected.append(
                lax.dot_general(
                    after(combined, *summed[-2:-1]), out_weight[:, low : low + cut], (((0,), (0,)), ((), ())),
                    preferred_element_type=jnp.float32,
                ).astype(jnp.bfloat16)
            )
            summed.append(scatter_cores(projected[-1]))
    for block in summed:
        pieces.append(scatter_chips(after(block, *pieces[-2:-1])))
    pieces = [
        jnp.concatenate(pieces[low : low + COLUMN_CUTS], axis=1) for low in range(0, len(pieces), COLUMN_CUTS)
    ]
    return jnp.concatenate(pieces, axis=0).reshape(spatial // head_groups, frames_here, -1)


def solution(mesh):
    in_specs = (
        P(None, "frames", "heads"),
        P(None, None, "frames", "heads"),
        P(),
        P(),
        P(None, None, "frames", "heads"),
        P("heads", None),
    )
    out_specs = P("heads", "frames", None)
    return jax.shard_map(local, mesh=mesh, in_specs=in_specs, out_specs=out_specs, check_vma=False)
```

```python
import functools

import jax
import jax.numpy as jnp
from jax import lax
from jax.experimental import pallas as pl
from jax.experimental.pallas import tpu as pltpu
from jax.sharding import PartitionSpec as P

HEAD_DIM = 128
TILE_ROWS = 16
PART_TILE = 32
COLUMN_CUTS = 2
HEAD_GROUPS = 2
VMEM_BYTES = 60 * 1024 * 1024


def after(block, *before):
    return lax.optimization_barrier((block, *before))[0] if before else block


def wide(block):
    return block.astype(jnp.float32)


def added(*blocks):
    return functools.reduce(jnp.add, [wide(block) for block in blocks]).astype(jnp.bfloat16)


def in_three(block):
    terms = []
    for _ in range(3):
        term = lax.reduce_precision(block, 8, 7)
        terms.append(term.astype(jnp.bfloat16))
        block = block - term
    return terms


def attend_columns(keys, values, queries, allowed):
    scale = HEAD_DIM ** (-0.5)
    scores = lax.dot_general(
        keys, queries, (((1,), (1,)), ((), ())), preferred_element_type=jnp.float32
    )
    scores = jnp.where(allowed, scores, -jnp.inf)
    peak = jnp.max(scores, axis=0, keepdims=True)
    weights = jnp.exp((scores - peak) * scale)
    totals = jnp.sum(weights, axis=0, keepdims=True)
    gathered = lax.dot_general(
        values, weights.astype(jnp.bfloat16), (((0,), (0,)), ((), ())),
        preferred_element_type=jnp.float32,
    )
    return gathered * (1.0 / totals), peak * scale + jnp.log(totals)


def bank_kernel(banks, live_ref, own_ref, far_ref, *refs):
    bank_refs = refs[:banks]
    head = pl.program_id(0)
    tokens = sum(bank.shape[2] for bank in bank_refs)
    second = lax.broadcasted_iota(jnp.int32, (2 * tokens, own_ref.shape[0]), 0) >= tokens
    for side, query_ref in enumerate((own_ref, far_ref)):
        out_ref, level_ref = refs[banks + 2 * side : banks + 2 * side + 2]
        keys, values = (
            jnp.concatenate([bank[which, 2 * side + slot] for slot in range(2) for bank in bank_refs], axis=0)
            for which in range(2)
        )
        allowed = jnp.logical_or(jnp.logical_not(second), live_ref[side, 1] > 0)
        gathered, level = attend_columns(keys, values, query_ref[...], allowed)
        rows = out_ref.shape[2]
        for part in range(out_ref.shape[0]):
            here = slice(part * rows, (part + 1) * rows)
            out_ref[part] = gathered[:, here].astype(out_ref.dtype)
            level_ref[part, pl.ds(head, 1), :] = level[:, here]


def attend_bank(group, parts, rows, live, own, far, banks):
    width = banks[0].shape[3]
    heads = width // HEAD_DIM
    keys_each = 2 * sum(bank.shape[2] for bank in banks)
    query_spec = pl.BlockSpec((parts * rows, HEAD_DIM), lambda h: (0, group * heads + h))
    out = jax.ShapeDtypeStruct((parts, width, rows), jnp.bfloat16)
    level = jax.ShapeDtypeStruct((parts, heads, rows), jnp.float32)
    out_spec = pl.BlockSpec((parts, HEAD_DIM, rows), lambda h: (0, h, 0))
    level_spec = pl.BlockSpec((parts, heads, rows), lambda h: (0, 0, 0))
    return pl.pallas_call(
        functools.partial(bank_kernel, len(banks)),
        grid=(heads,),
        in_specs=[pl.BlockSpec(memory_space=pltpu.SMEM), query_spec, query_spec]
        + [pl.BlockSpec((*bank.shape[:3], HEAD_DIM), lambda h: (0, 0, 0, h)) for bank in banks],
        out_specs=[out_spec, level_spec] * 2,
        out_shape=[out, level] * 2,
        compiler_params=pltpu.CompilerParams(vmem_limit_bytes=VMEM_BYTES),
        cost_estimate=pl.CostEstimate(
            flops=32 * parts * rows * width * keys_each,
            bytes_accessed=2 * (4 * parts * rows * width + sum(bank.size for bank in banks)),
            transcendentals=2 * parts * rows * heads * keys_each,
        ),
    )(live, own, far, *banks)


def frame_kernel(frames_here, token_ref, out_ref):
    scale = HEAD_DIM ** (-0.5)
    pieces, _, parts, rows, _ = token_ref.shape
    size = pieces * rows
    query_spot = lax.broadcasted_iota(jnp.int32, (size, size), 0) % rows // frames_here
    key_spot = lax.broadcasted_iota(jnp.int32, (size, size), 1) % rows // frames_here
    same_spot = query_spot == key_spot
    for part in range(parts):
        queries, keys, values = (
            jnp.concatenate([token_ref[piece, which, part] for piece in range(pieces)], axis=0)
            for which in range(3)
        )
        scores = lax.dot_general(
            queries, keys, (((1,), (1,)), ((), ())), preferred_element_type=jnp.float32
        )
        scores = jnp.where(same_spot, scores, -jnp.inf)
        weights = jnp.exp((scores - jnp.max(scores, axis=1, keepdims=True)) * scale)
        totals = jnp.sum(weights, axis=1, keepdims=True)
        gathered = jnp.dot(weights.astype(jnp.bfloat16), values, preferred_element_type=jnp.float32)
        gathered = (gathered / totals).astype(out_ref.dtype)
        for piece in range(pieces):
            out_ref[piece, part] = gathered[piece * rows : (piece + 1) * rows]


def attend_frames(frames_here, tokens):
    pieces, _, parts, rows, width = tokens.shape
    return pl.pallas_call(
        functools.partial(frame_kernel, frames_here),
        grid=(width // HEAD_DIM,),
        in_specs=[pl.BlockSpec((pieces, 3, parts, rows, HEAD_DIM), lambda h: (0, 0, 0, 0, h))],
        out_specs=pl.BlockSpec((pieces, parts, rows, HEAD_DIM), lambda h: (0, 0, 0, h)),
        out_shape=jax.ShapeDtypeStruct((pieces, parts, rows, width), jnp.bfloat16),
        compiler_params=pltpu.CompilerParams(vmem_limit_bytes=VMEM_BYTES),
        cost_estimate=pl.CostEstimate(
            flops=16 * parts * (pieces * rows) ** 2 * width,
            bytes_accessed=8 * pieces * parts * rows * width,
            transcendentals=parts * (pieces * rows) ** 2 * width // HEAD_DIM,
        ),
    )(tokens)


def listed_kernel(place_ref, slots_ref, *refs):
    count = len(refs) // 2
    for source, target in zip(refs[:count], refs[count:]):
        target[...] = source[...]


def listed_banks(place, char_slots, char_bank, half, group, group_width):
    _, _, tokens, _ = char_bank.shape
    block = (2, 1, tokens, group_width)

    def source(step):
        def index(entry, place_ref, slots_ref):
            shard = place_ref[0] ^ step ^ (entry // 2 * half)
            return 0, slots_ref[shard * 2 + entry % 2], 0, group

        return pl.BlockSpec(block, index)

    return pl.pallas_call(
        listed_kernel,
        grid_spec=pltpu.PrefetchScalarGridSpec(
            num_scalar_prefetch=2,
            grid=(4,),
            in_specs=[source(step) for step in range(half)],
            out_specs=[pl.BlockSpec(block, lambda entry, *_: (0, entry, 0, 0)) for _ in range(half)],
        ),
        out_shape=[jax.ShapeDtypeStruct((2, 4, tokens, group_width), char_bank.dtype) for _ in range(half)],
        compiler_params=pltpu.CompilerParams(vmem_limit_bytes=VMEM_BYTES),
        cost_estimate=pl.CostEstimate(
            flops=0, bytes_accessed=32 * half * tokens * group_width, transcendentals=0
        ),
    )(place.reshape(1), char_slots.reshape(-1), *[char_bank] * half)


def local(bank_query, char_bank, char_slots, slot_live, frame_tokens, out_weight):
    spatial, frames_here, width = bank_query.shape
    heads_here = width // HEAD_DIM
    head_groups = lax.axis_size("heads")
    shards = lax.axis_size("frames")
    half = shards // 2
    place = lax.axis_index("frames")
    parts = max(1, spatial * frames_here // (PART_TILE * shards))
    across = shards // head_groups
    spots = spatial // (shards * parts)
    tile = spots * frames_here
    rows = shards * tile

    def swap(block, step):
        return lax.ppermute(block, "frames", [(a, a ^ step) for a in range(shards)])

    def by_part(block):
        cut = block.reshape(head_groups, parts, across, spots, frames_here, width)
        return jnp.moveaxis(cut, 1, 0).reshape(parts * rows, width)

    own = by_part(bank_query)
    far = swap(own, half)

    groups = HEAD_GROUPS if heads_here % HEAD_GROUPS == 0 else 1

    def banks_of(group, *before):
        blocks = listed_banks(
            place, after(char_slots, *before), char_bank, half, group, width // groups
        )
        blocks = [blocks[0]] + [swap(blocks[step], step) for step in range(1, half)]
        return blocks if char_bank.shape[2] % TILE_ROWS == 0 else [jnp.concatenate(blocks, axis=2)]

    banks = [banks_of(0)]
    tokens = frame_tokens.reshape(3, head_groups, parts, across, spots, frames_here, width)
    tokens = tokens.transpose(1, 3, 0, 2, 4, 5, 6).reshape(shards, 3, parts, tile, width)
    tokens = lax.all_to_all(after(tokens, far, *banks[0]), "frames", 0, 0, tiled=True)
    live = jnp.stack([slot_live[place], slot_live[place ^ half]])

    place_heads = lax.axis_index("heads")
    chips, core, chip = head_groups // 2, place_heads % 2, place_heads // 2

    def scatter_cores(block):
        block = block.reshape(chips, 2, -1, block.shape[-1])
        give = lax.dynamic_index_in_dim(block, 1 - core, 1, keepdims=False)
        keep = lax.dynamic_index_in_dim(block, core, 1, keepdims=False)
        return added(keep, lax.ppermute(give, "heads", [(h, h ^ 1) for h in range(head_groups)]))

    def scatter_chips(summed):
        parcels = [lax.dynamic_index_in_dim(summed, chip, 0, keepdims=False)]
        for step in range(1, chips):
            give = lax.dynamic_index_in_dim(summed, (chip + step) % chips, 0, keepdims=False)
            parcels.append(
                lax.ppermute(give, "heads", [(h, (h + 2 * step) % head_groups) for h in range(head_groups)])
            )
        return added(*parcels)

    split = (heads_here // groups, HEAD_DIM, rows)
    results = []
    for group in range(groups):
        near_out, near_level, far_out, far_level = attend_bank(group, parts, rows, live, own, far, banks[group])
        if group < groups - 1:
            banks.append(banks_of(group + 1, far_level))
        if group == 0:
            frame_parts = attend_frames(frames_here, after(tokens, far_level))
            back = lax.all_to_all(frame_parts, "frames", 0, 0, tiled=True)
            live = after(live, frame_parts)
        message = jnp.concatenate([far_out, *in_three(far_level)], axis=1)
        message = jnp.pad(message, ((0, 0), (0, -message.shape[1] % TILE_ROWS), (0, 0)))
        if group < groups - 1:
            got = swap(message, half)
        else:
            got = [swap(message[part], half) for part in range(parts)]
        results.append((near_out, near_level, got))
    results = [
        (near_out, near_level, after(got, results[-1][1]) if group < groups - 1 else got)
        for group, (near_out, near_level, got) in enumerate(results)
    ]

    def share_of(group, part, *before):
        near_out, near_level, got = results[group]
        got = after(got[part], *(before if group == groups - 1 else ()))
        size = heads_here // groups
        got_level = sum(wide(got[low : low + size]) for low in range(width // groups, width // groups + 3 * size, size))
        peak = jnp.maximum(near_level[part], got_level)
        near_share, got_share = jnp.exp(near_level[part] - peak), jnp.exp(got_level - peak)
        total = near_share + got_share
        return (
            wide(near_out[part].reshape(split)) * (near_share / total)[:, None, :]
            + wide(got[: width // groups].reshape(split)) * (got_share / total)[:, None, :]
        )

    projected, summed, pieces = [], [], []
    cut = out_weight.shape[1] // COLUMN_CUTS
    for part in range(parts):
        shares = [share_of(group, part, *projected[-1:], *summed[-2:-1]) for group in range(groups)]
        ref_out = jnp.concatenate(shares, axis=0).reshape(width, rows)
        frame_out = back[:, part].reshape(rows, width)
        combined = (ref_out + wide(frame_out.T)).astype(jnp.bfloat16)
        for low in range(0, cut * COLUMN_CUTS, cut):
            projected.append(
                lax.dot_general(
                    after(combined, *summed[-2:-1]), out_weight[:, low : low + cut], (((0,), (0,)), ((), ())),
                    preferred_element_type=jnp.float32,
                ).astype(jnp.bfloat16)
            )
            summed.append(scatter_cores(projected[-1]))
    for block in summed:
        before = pieces if len(pieces) == 1 else pieces[-2:-1]
        pieces.append(scatter_chips(after(block, *before)))
    pieces = [
        jnp.concatenate(pieces[low : low + COLUMN_CUTS], axis=1) for low in range(0, len(pieces), COLUMN_CUTS)
    ]
    return jnp.concatenate(pieces, axis=0).reshape(spatial // head_groups, frames_here, -1)


def solution(mesh):
    in_specs = (
        P(None, "frames", "heads"),
        P(None, None, "frames", "heads"),
        P(),
        P(),
        P(None, None, "frames", "heads"),
        P("heads", None),
    )
    out_specs = P("heads", "frames", None)
    return jax.shard_map(local, mesh=mesh, in_specs=in_specs, out_specs=out_specs, check_vma=False)
```

```python
import functools

import jax
import jax.numpy as jnp
from jax import lax
from jax.experimental import pallas as pl
from jax.experimental.pallas import tpu as pltpu
from jax.sharding import PartitionSpec as P

HEAD_DIM = 128
TILE_ROWS = 16
PART_TILE = 32
COLUMN_CUTS = 2
HEAD_GROUPS = 2
VMEM_BYTES = 60 * 1024 * 1024


def after(block, *before):
    return lax.optimization_barrier((block, *before))[0] if before else block


def wide(block):
    return block.astype(jnp.float32)


def added(*blocks):
    return functools.reduce(jnp.add, [wide(block) for block in blocks]).astype(jnp.bfloat16)


def in_three(block):
    terms = []
    for _ in range(3):
        term = lax.reduce_precision(block, 8, 7)
        terms.append(term.astype(jnp.bfloat16))
        block = block - term
    return terms


def attend_columns(keys, values, queries, allowed):
    scale = HEAD_DIM ** (-0.5)
    scores = lax.dot_general(
        keys, queries, (((1,), (1,)), ((), ())), preferred_element_type=jnp.float32
    )
    scores = jnp.where(allowed, scores, -jnp.inf)
    peak = jnp.max(scores, axis=0, keepdims=True)
    weights = jnp.exp((scores - peak) * scale)
    totals = jnp.sum(weights, axis=0, keepdims=True)
    gathered = lax.dot_general(
        values, weights.astype(jnp.bfloat16), (((0,), (0,)), ((), ())),
        preferred_element_type=jnp.float32,
    )
    return gathered * (1.0 / totals), peak * scale + jnp.log(totals)


def bank_kernel(banks, live_ref, own_ref, far_ref, *refs):
    bank_refs = refs[:banks]
    head = pl.program_id(0)
    tokens = sum(bank.shape[2] for bank in bank_refs)
    second = lax.broadcasted_iota(jnp.int32, (2 * tokens, own_ref.shape[0]), 0) >= tokens
    for side, query_ref in enumerate((own_ref, far_ref)):
        out_ref, level_ref = refs[banks + 2 * side : banks + 2 * side + 2]
        keys, values = (
            jnp.concatenate([bank[which, 2 * side + slot] for slot in range(2) for bank in bank_refs], axis=0)
            for which in range(2)
        )
        allowed = jnp.logical_or(jnp.logical_not(second), live_ref[side, 1] > 0)
        gathered, level = attend_columns(keys, values, query_ref[...], allowed)
        rows = out_ref.shape[2]
        for part in range(out_ref.shape[0]):
            here = slice(part * rows, (part + 1) * rows)
            out_ref[part] = gathered[:, here].astype(out_ref.dtype)
            level_ref[part, pl.ds(head, 1), :] = level[:, here]


def attend_bank(group, parts, rows, live, own, far, banks):
    width = banks[0].shape[3]
    heads = width // HEAD_DIM
    keys_each = 2 * sum(bank.shape[2] for bank in banks)
    query_spec = pl.BlockSpec((parts * rows, HEAD_DIM), lambda h: (0, group * heads + h))
    out = jax.ShapeDtypeStruct((parts, width, rows), jnp.bfloat16)
    level = jax.ShapeDtypeStruct((parts, heads, rows), jnp.float32)
    out_spec = pl.BlockSpec((parts, HEAD_DIM, rows), lambda h: (0, h, 0))
    level_spec = pl.BlockSpec((parts, heads, rows), lambda h: (0, 0, 0))
    return pl.pallas_call(
        functools.partial(bank_kernel, len(banks)),
        grid=(heads,),
        in_specs=[pl.BlockSpec(memory_space=pltpu.SMEM), query_spec, query_spec]
        + [pl.BlockSpec((*bank.shape[:3], HEAD_DIM), lambda h: (0, 0, 0, h)) for bank in banks],
        out_specs=[out_spec, level_spec] * 2,
        out_shape=[out, level] * 2,
        compiler_params=pltpu.CompilerParams(vmem_limit_bytes=VMEM_BYTES),
        cost_estimate=pl.CostEstimate(
            flops=32 * parts * rows * width * keys_each,
            bytes_accessed=2 * (4 * parts * rows * width + sum(bank.size for bank in banks)),
            transcendentals=2 * parts * rows * heads * keys_each,
        ),
    )(live, own, far, *banks)


def frame_kernel(frames_here, token_ref, out_ref):
    scale = HEAD_DIM ** (-0.5)
    pieces, _, parts, rows, _ = token_ref.shape
    size = pieces * rows
    query_spot = lax.broadcasted_iota(jnp.int32, (size, size), 0) % rows // frames_here
    key_spot = lax.broadcasted_iota(jnp.int32, (size, size), 1) % rows // frames_here
    same_spot = query_spot == key_spot
    for part in range(parts):
        queries, keys, values = (
            jnp.concatenate([token_ref[piece, which, part] for piece in range(pieces)], axis=0)
            for which in range(3)
        )
        scores = lax.dot_general(
            queries, keys, (((1,), (1,)), ((), ())), preferred_element_type=jnp.float32
        )
        scores = jnp.where(same_spot, scores, -jnp.inf)
        weights = jnp.exp((scores - jnp.max(scores, axis=1, keepdims=True)) * scale)
        totals = jnp.sum(weights, axis=1, keepdims=True)
        gathered = jnp.dot(weights.astype(jnp.bfloat16), values, preferred_element_type=jnp.float32)
        gathered = (gathered / totals).astype(out_ref.dtype)
        for piece in range(pieces):
            out_ref[piece, part] = gathered[piece * rows : (piece + 1) * rows]


def attend_frames(frames_here, tokens):
    pieces, _, parts, rows, width = tokens.shape
    return pl.pallas_call(
        functools.partial(frame_kernel, frames_here),
        grid=(width // HEAD_DIM,),
        in_specs=[pl.BlockSpec((pieces, 3, parts, rows, HEAD_DIM), lambda h: (0, 0, 0, 0, h))],
        out_specs=pl.BlockSpec((pieces, parts, rows, HEAD_DIM), lambda h: (0, 0, 0, h)),
        out_shape=jax.ShapeDtypeStruct((pieces, parts, rows, width), jnp.bfloat16),
        compiler_params=pltpu.CompilerParams(vmem_limit_bytes=VMEM_BYTES),
        cost_estimate=pl.CostEstimate(
            flops=16 * parts * (pieces * rows) ** 2 * width,
            bytes_accessed=8 * pieces * parts * rows * width,
            transcendentals=parts * (pieces * rows) ** 2 * width // HEAD_DIM,
        ),
    )(tokens)


def listed_kernel(place_ref, slots_ref, *refs):
    count = len(refs) // 2
    for source, target in zip(refs[:count], refs[count:]):
        target[...] = source[...]


def listed_banks(place, char_slots, char_bank, half, group, group_width):
    _, _, tokens, _ = char_bank.shape
    block = (2, 1, tokens, group_width)

    def source(step):
        def index(entry, place_ref, slots_ref):
            shard = place_ref[0] ^ step ^ (entry // 2 * half)
            return 0, slots_ref[shard * 2 + entry % 2], 0, group

        return pl.BlockSpec(block, index)

    return pl.pallas_call(
        listed_kernel,
        grid_spec=pltpu.PrefetchScalarGridSpec(
            num_scalar_prefetch=2,
            grid=(4,),
            in_specs=[source(step) for step in range(half)],
            out_specs=[pl.BlockSpec(block, lambda entry, *_: (0, entry, 0, 0)) for _ in range(half)],
        ),
        out_shape=[jax.ShapeDtypeStruct((2, 4, tokens, group_width), char_bank.dtype) for _ in range(half)],
        compiler_params=pltpu.CompilerParams(vmem_limit_bytes=VMEM_BYTES),
        cost_estimate=pl.CostEstimate(
            flops=0, bytes_accessed=32 * half * tokens * group_width, transcendentals=0
        ),
    )(place.reshape(1), char_slots.reshape(-1), *[char_bank] * half)


def local(bank_query, char_bank, char_slots, slot_live, frame_tokens, out_weight):
    spatial, frames_here, width = bank_query.shape
    heads_here = width // HEAD_DIM
    head_groups = lax.axis_size("heads")
    shards = lax.axis_size("frames")
    half = shards // 2
    place = lax.axis_index("frames")
    parts = max(1, spatial * frames_here // (PART_TILE * shards))
    across = shards // head_groups
    spots = spatial // (shards * parts)
    tile = spots * frames_here
    rows = shards * tile

    def swap(block, step):
        return lax.ppermute(block, "frames", [(a, a ^ step) for a in range(shards)])

    def by_part(block):
        cut = block.reshape(head_groups, parts, across, spots, frames_here, width)
        return jnp.moveaxis(cut, 1, 0).reshape(parts * rows, width)

    own = by_part(bank_query)
    far = swap(own, half)

    groups = HEAD_GROUPS if heads_here % HEAD_GROUPS == 0 else 1

    def listed_of(group):
        return listed_banks(place, char_slots, char_bank, half, group, width // groups)

    def banks_of(blocks, *before):
        blocks = [blocks[0]] + [swap(after(blocks[step], *before), step) for step in range(1, half)]
        return blocks if char_bank.shape[2] % TILE_ROWS == 0 else [jnp.concatenate(blocks, axis=2)]

    listed = [listed_of(group) for group in range(groups)]
    banks = [banks_of(listed[0])]
    tokens = frame_tokens.reshape(3, head_groups, parts, across, spots, frames_here, width)
    tokens = tokens.transpose(1, 3, 0, 2, 4, 5, 6).reshape(shards, 3, parts, tile, width)
    tokens = lax.all_to_all(after(tokens, far, *banks[0], *[blocks[0] for blocks in listed[1:]]), "frames", 0, 0, tiled=True)
    live = jnp.stack([slot_live[place], slot_live[place ^ half]])

    place_heads = lax.axis_index("heads")
    chips, core, chip = head_groups // 2, place_heads % 2, place_heads // 2

    def scatter_cores(block):
        block = block.reshape(chips, 2, -1, block.shape[-1])
        give = lax.dynamic_index_in_dim(block, 1 - core, 1, keepdims=False)
        keep = lax.dynamic_index_in_dim(block, core, 1, keepdims=False)
        return added(keep, lax.ppermute(give, "heads", [(h, h ^ 1) for h in range(head_groups)]))

    def scatter_chips(summed):
        parcels = [lax.dynamic_index_in_dim(summed, chip, 0, keepdims=False)]
        for step in range(1, chips):
            give = lax.dynamic_index_in_dim(summed, (chip + step) % chips, 0, keepdims=False)
            parcels.append(
                lax.ppermute(give, "heads", [(h, (h + 2 * step) % head_groups) for h in range(head_groups)])
            )
        return added(*parcels)

    split = (heads_here // groups, HEAD_DIM, rows)
    results = []
    for group in range(groups):
        near_out, near_level, far_out, far_level = attend_bank(group, parts, rows, live, own, far, banks[group])
        if group < groups - 1:
            banks.append(banks_of(listed[group + 1], far_level))
        if group == 0:
            frame_parts = attend_frames(frames_here, after(tokens, far_level))
            back = lax.all_to_all(frame_parts, "frames", 0, 0, tiled=True)
            live = after(live, frame_parts)
        message = jnp.concatenate([far_out, *in_three(far_level)], axis=1)
        message = jnp.pad(message, ((0, 0), (0, -message.shape[1] % TILE_ROWS), (0, 0)))
        if group < groups - 1:
            got = swap(message, half)
        else:
            got = [swap(message[part], half) for part in range(parts)]
        results.append((near_out, near_level, got))
    results = [
        (near_out, near_level, after(got, results[-1][1]) if group < groups - 1 else got)
        for group, (near_out, near_level, got) in enumerate(results)
    ]

    def share_of(group, part, *before):
        near_out, near_level, got = results[group]
        got = after(got[part], *(before if group == groups - 1 else ()))
        size = heads_here // groups
        got_level = sum(wide(got[low : low + size]) for low in range(width // groups, width // groups + 3 * size, size))
        peak = jnp.maximum(near_level[part], got_level)
        near_share, got_share = jnp.exp(near_level[part] - peak), jnp.exp(got_level - peak)
        total = near_share + got_share
        return (
            wide(near_out[part].reshape(split)) * (near_share / total)[:, None, :]
            + wide(got[: width // groups].reshape(split)) * (got_share / total)[:, None, :]
        )

    projected, summed, pieces = [], [], []
    cut = out_weight.shape[1] // COLUMN_CUTS
    for part in range(parts):
        shares = [share_of(group, part, *projected[-1:], *summed[-2:-1]) for group in range(groups)]
        ref_out = jnp.concatenate(shares, axis=0).reshape(width, rows)
        frame_out = back[:, part].reshape(rows, width)
        combined = (ref_out + wide(frame_out.T)).astype(jnp.bfloat16)
        for low in range(0, cut * COLUMN_CUTS, cut):
            projected.append(
                lax.dot_general(
                    after(combined, *summed[-2:-1]), out_weight[:, low : low + cut], (((0,), (0,)), ((), ())),
                    preferred_element_type=jnp.float32,
                ).astype(jnp.bfloat16)
            )
            summed.append(scatter_cores(projected[-1]))
    for block in summed:
        pieces.append(scatter_chips(after(block, *pieces[-2:-1])))
    pieces = [
        jnp.concatenate(pieces[low : low + COLUMN_CUTS], axis=1) for low in range(0, len(pieces), COLUMN_CUTS)
    ]
    return jnp.concatenate(pieces, axis=0).reshape(spatial // head_groups, frames_here, -1)


def solution(mesh):
    in_specs = (
        P(None, "frames", "heads"),
        P(None, None, "frames", "heads"),
        P(),
        P(),
        P(None, None, "frames", "heads"),
        P("heads", None),
    )
    out_specs = P("heads", "frames", None)
    return jax.shard_map(local, mesh=mesh, in_specs=in_specs, out_specs=out_specs, check_vma=False)
```
